128 devices in a mesh: gx: 8 (over y, core), gy: 16 (over z, x).
Axes of the slice: x: 4, y: 4, z: 4, core: 2. Of those that a mesh axis runs over, the one named last changes fastest.
Arguments:
- material: int32 [4, 2048, 4096], P(None, 'gx', 'gy'), may hold values from 0 to 15
- material_table: float32 [2, 16], replicated, may hold values from 0.5 to 4
- sink_cond: float32 [2048, 4096], P('gx', 'gy'), may hold values from 0.05 to 0.5
- drain_current: float32 [2048, 4096], P('gx', 'gy'), may hold values from 0.05 to 0.5
- instance_tile: int32 [262144], P(('gx', 'gy')), may hold values from 0 to 131071, as said below
- instance_power: float32 [262144], P(('gx', 'gy')), may hold values from 4 to 40
Outputs:
- thermal_rise: float32 [4, 2048, 4096], P(None, 'gx', 'gy')
- dynamic_wattage: float32 [2048, 4096], P('gx', 'gy')
The draws below stay inside these ranges and needn't reach their ends.
Inputs may be any that keep to these rules, and one draw needn't show every extreme that they name: Instance i adds its power to tile instance_tile[i]; in each aligned block of 2048 instances (the list of one device) at most 32 instances have tiles of one subdomain (instance_tile // 1024), and in every draw some subdomain gets exactly 32 from every block.
All inputs are finite; a program needn't handle non-finite values.
Results may differ from the reference program's by a relative error of at most 0.0003.
Values sent between devices are 32-bit elements; how exact they have to be, the bound alone decides.
A program may use at most 128 MiB of HBM per device.

```python
import math
import jax
import jax.numpy as jnp
from jax import lax

DIE_PLIES = 4
CX = 256
CY = 256
PB = 8
OV = 2
SWEEPS = 2
CJ = 8
OUTER = 2
INNER = 2
MATS = 16
INST_DEV = 2048
MESH_HEIGHT = 2048
MESH_WIDTH = 4096
TPX = 32
TPY = 32
TILES_DEV = 1024
NTILES = 131072
INSTANCES = 262144
MX = 64
MY = 128
AGGREGATE_HEIGHT = 32
AGGREGATE_WIDTH = 32
N_GX = 8
N_GY = 16
DEVICES = 128


def draw_instance_tile(key, part):
    key = jax.random.fold_in(key, 7)
    base_count = INST_DEV // DEVICES
    owner_key, block_key = jax.random.split(key)
    busiest = jax.random.randint(owner_key, (), 0, DEVICES, dtype=jnp.int32)
    block_keys = jax.random.split(block_key, DEVICES)

    def one_block(block_seed):
        order_key, shift_key, shuffle_key, local_key = jax.random.split(block_seed, 4)
        shuffled = jax.random.permutation(order_key, DEVICES).astype(jnp.int32)
        leading = shuffled[0]
        shuffled = jnp.where(shuffled == busiest, leading, shuffled)
        shuffled = shuffled.at[0].set(busiest)
        shifts = jax.random.randint(shift_key, (DEVICES // 2,), 0, base_count + 1, dtype=jnp.int32)
        shifts = shifts.at[0].set(base_count)
        counts = jnp.zeros((DEVICES,), jnp.int32)
        counts = counts.at[shuffled[0::2]].set(base_count + shifts)
        counts = counts.at[shuffled[1::2]].set(base_count - shifts)
        bounds = jnp.cumsum(counts).astype(jnp.int32)
        positions = jnp.arange(INST_DEV, dtype=jnp.int32)
        owners = jnp.searchsorted(bounds, positions, side='right').astype(jnp.int32)
        owners = jax.random.permutation(shuffle_key, owners)
        local_tiles = jax.random.randint(local_key, (INST_DEV,), 0, TILES_DEV, dtype=jnp.int32)
        return owners * TILES_DEV + local_tiles
    return jax.vmap(one_block)(block_keys).reshape(-1).astype(jnp.int32)


def plant(drawn, own_key, low, top_value):
    place = [jax.random.randint(jax.random.fold_in(own_key, axis), (), 0, length) for axis, length in enumerate(drawn.shape)]
    main_axis = drawn.shape.index(max(drawn.shape))
    next_to = place[:main_axis] + [(place[main_axis] + 1) % drawn.shape[main_axis]] + place[main_axis + 1:]
    return drawn.at[tuple(place)].set(low).at[tuple(next_to)].set(top_value)


def levels(stream_key, extent, cuts, least, high):
    loudness, own = 1.0, jax.random.fold_in(stream_key, 6)
    for axis_at, shards_of in cuts:
        heights = jnp.exp(jax.random.uniform(jax.random.fold_in(own, axis_at), (shards_of,), jnp.float32, least / len(cuts), high / len(cuts)))
        loudness = loudness * jnp.repeat(heights, extent[axis_at] // shards_of).reshape([-1 if axis == axis_at else 1 for axis in range(len(extent))])
    return loudness


def setup_inputs(seed: int = 0) -> dict:
    arg_keys = jax.random.split(jax.random.key(seed), 7)
    material = plant(jax.random.randint(arg_keys[0], (DIE_PLIES, MESH_HEIGHT, MESH_WIDTH), 0, MATS), jax.random.fold_in(arg_keys[0], 1), 0, MATS - 1).astype(jnp.int32)
    material_table = jnp.clip(jnp.exp(jax.random.uniform(arg_keys[1], (2, MATS), jnp.float32, math.log(0.5), math.log(4.0))), 0.5, 4.0)
    sink_cond = jnp.clip(jnp.exp(math.log(0.5) - 2.3025851 * jax.random.uniform(arg_keys[2], (MESH_HEIGHT, MESH_WIDTH), jnp.float32) ** levels(arg_keys[2], (MESH_HEIGHT, MESH_WIDTH), ((0, 8), (1, 16)), -0.2, 0.2)), 0.05, 0.5)
    drain_current = jnp.clip(jnp.exp(math.log(0.5) - 2.3025851 * jax.random.uniform(arg_keys[3], (MESH_HEIGHT, MESH_WIDTH), jnp.float32) ** levels(arg_keys[3], (MESH_HEIGHT, MESH_WIDTH), ((0, 8), (1, 16)), -0.2, 0.2)), 0.05, 0.5)
    instance_tile = draw_instance_tile(jax.random.fold_in(arg_keys[6], 71), 0)
    instance_power = jnp.clip(jnp.exp(math.log(40.0) - 2.3025851 * jax.random.uniform(arg_keys[5], (INSTANCES,), jnp.float32) ** levels(arg_keys[5], (INSTANCES,), ((0, 128),), -0.2, 0.2)), 4.0, 40.0)
    return {"material": material, "material_table": material_table, "sink_cond": sink_cond, "drain_current": drain_current, "instance_tile": instance_tile, "instance_power": instance_power}


DAMPING = 0.8
DRAIN_SLOPE = 0.5
FACE_FLOOR = 0.5
BALANCE_WEIGHT = 0.5


def lookup(material, table_row):
    summed = jnp.zeros(material.shape, jnp.float32)
    for number in range(table_row.shape[0]):
        summed = summed + jnp.where(material == number, table_row[number], jnp.float32(0.0))
    return summed


def harmonic(left_value, right_value):
    return 2.0 * left_value * right_value / jnp.maximum(left_value + right_value, FACE_FLOOR)


def diagonal(coeffs, sink_ext):
    upper_face, lower_face, left_face, right_face, vertical = coeffs
    zero_layer = jnp.zeros_like(vertical[:1])
    summed = upper_face + lower_face + left_face + right_face
    summed = summed + jnp.concatenate([zero_layer, vertical], 0) + jnp.concatenate([vertical, zero_layer], 0)
    summed = summed + jnp.concatenate([jnp.zeros_like(summed[:-1]), sink_ext[None]], 0)
    return jnp.maximum(summed, FACE_FLOOR)


def face_terms(lateral, vertical_cond, sink_padded, margin):
    face_row = harmonic(lateral[:, :-1, :], lateral[:, 1:, :])
    face_col = harmonic(lateral[:, :, :-1], lateral[:, :, 1:])
    face_ver = harmonic(vertical_cond[:-1], vertical_cond[1:])
    ext_rows = lateral.shape[1] - 2
    ext_cols = lateral.shape[2] - 2
    coeffs = (face_row[:, 0:ext_rows, 1:ext_cols + 1], face_row[:, 1:ext_rows + 1, 1:ext_cols + 1],
              face_col[:, 1:ext_rows + 1, 0:ext_cols], face_col[:, 1:ext_rows + 1, 1:ext_cols + 1],
              face_ver[:, 1:ext_rows + 1, 1:ext_cols + 1])
    sink_ext = sink_padded[1:ext_rows + 1, 1:ext_cols + 1]
    rim_width = margin + 1
    overall_height = ext_rows - 2 * margin
    width_cells = ext_cols - 2 * margin
    inner_faces = (face_row[:, rim_width:rim_width + overall_height, rim_width:rim_width + width_cells],
                   face_col[:, rim_width:rim_width + overall_height, rim_width:rim_width + width_cells],
                   face_ver[:, rim_width:rim_width + overall_height, rim_width:rim_width + width_cells],
                   sink_padded[rim_width:rim_width + overall_height, rim_width:rim_width + width_cells])
    return coeffs, diagonal(coeffs, sink_ext), inner_faces


def couple(margined_array, coeffs):
    upper_face, lower_face, left_face, right_face, vertical = coeffs
    centre = margined_array[:, 1:-1, 1:-1]
    lateral = (upper_face * margined_array[:, :-2, 1:-1] + lower_face * margined_array[:, 2:, 1:-1]
               + left_face * margined_array[:, 1:-1, :-2] + right_face * margined_array[:, 1:-1, 2:])
    zero_layer = jnp.zeros_like(vertical[:1])
    from_above = jnp.concatenate([zero_layer, vertical * centre[:-1]], 0)
    from_below = jnp.concatenate([vertical * centre[1:], zero_layer], 0)
    return lateral + from_above + from_below


def residual_of(thermal_forcing, margined_array, coeffs, diagonal_term):
    return thermal_forcing - (diagonal_term * margined_array[:, 1:-1, 1:-1] - couple(margined_array, coeffs))


def smooth(residual, coeffs, diagonal_term, sweeps):
    correction = jnp.zeros_like(residual)
    for number in range(sweeps):
        margined_array = jnp.pad(correction, ((0, 0), (1, 1), (1, 1)))
        correction = (1.0 - DAMPING) * correction + DAMPING * (residual + couple(margined_array, coeffs)) / diagonal_term
    return correction


def assemble_forcing(dynamic_wattage, drain_current, thermal_rise):
    topmost_ply = dynamic_wattage + drain_current * jnp.exp(DRAIN_SLOPE * thermal_rise[0])
    leftover = jnp.zeros((thermal_rise.shape[0] - 1,) + topmost_ply.shape, topmost_ply.dtype)
    return jnp.concatenate([topmost_ply[None], leftover], 0)


def coarse_terms(inner_faces, row_blocks, col_blocks):
    face_row, face_col, face_ver, sink_inner = inner_faces
    number_plies, overall_height, width_cells = face_row.shape
    block_row_count = overall_height // row_blocks
    block_column_count = width_cells // col_blocks
    east_face = face_row.reshape(number_plies, row_blocks, block_row_count, col_blocks, block_column_count)[:, :, block_row_count - 1].sum(axis=-1)
    north_face = face_col.reshape(number_plies, row_blocks, block_row_count, col_blocks, block_column_count)[:, :, :, :, block_column_count - 1].sum(axis=2)
    vertical_sum = face_ver.reshape(number_plies - 1, row_blocks, block_row_count, col_blocks, block_column_count).sum(axis=(2, 4))
    sink_sums = sink_inner.reshape(row_blocks, block_row_count, col_blocks, block_column_count).sum(axis=(1, 3))
    return jnp.concatenate([east_face, north_face, vertical_sum, sink_sums[None]], 0)


def unpack_coarse(coarse_stack, number_plies):
    east_face = coarse_stack[:number_plies]
    north_face = coarse_stack[number_plies:2 * number_plies]
    vertical = coarse_stack[2 * number_plies:3 * number_plies - 1]
    sink_sums = coarse_stack[3 * number_plies - 1]
    east_prev = jnp.pad(east_face, ((0, 0), (1, 0), (0, 0)))[:, :-1]
    north_prev = jnp.pad(north_face, ((0, 0), (0, 0), (1, 0)))[:, :, :-1]
    return east_face, east_prev, north_face, north_prev, vertical, sink_sums


def coarse_diagonal(coarse_stack, number_plies):
    east_face, east_prev, north_face, north_prev, vertical, sink_sums = unpack_coarse(coarse_stack, number_plies)
    zero_layer = jnp.zeros_like(vertical[:1])
    summed = east_face + east_prev + north_face + north_prev
    summed = summed + jnp.concatenate([zero_layer, vertical], 0) + jnp.concatenate([vertical, zero_layer], 0)
    return summed + jnp.concatenate([jnp.zeros_like(summed[:-1]), sink_sums[None]], 0)


def coarse_solve(coarse_resid, coarse_stack, coarse_diag, number_plies, sweeps):
    east_face, east_prev, north_face, north_prev, vertical, sink_sums = unpack_coarse(coarse_stack, number_plies)
    zero_layer = jnp.zeros_like(vertical[:1])
    solution = jnp.zeros_like(coarse_resid)
    for number in range(sweeps):
        margined_array = jnp.pad(solution, ((0, 0), (1, 1), (1, 1)))
        neighbours = (east_face * margined_array[:, 2:, 1:-1] + east_prev * margined_array[:, :-2, 1:-1]
                      + north_face * margined_array[:, 1:-1, 2:] + north_prev * margined_array[:, 1:-1, :-2])
        neighbours = neighbours + jnp.concatenate([zero_layer, vertical * solution[:-1]], 0)
        neighbours = neighbours + jnp.concatenate([vertical * solution[1:], zero_layer], 0)
        solution = (1.0 - DAMPING) * solution + DAMPING * (coarse_resid + neighbours) / coarse_diag
    balance = BALANCE_WEIGHT * jnp.sum(coarse_resid) / jnp.sum(coarse_diag)
    return solution + balance


def distribute(values, row_rep, col_rep):
    leading = values.shape[:-2]
    overall_height, width_cells = values.shape[-2], values.shape[-1]
    expanded = jnp.broadcast_to(values[..., :, None, :, None], leading + (overall_height, row_rep, width_cells, col_rep))
    return expanded.reshape(leading + (overall_height * row_rep, width_cells * col_rep))


def local_solves(residual, coeffs, diagonal_term):
    ext_rows = CX + 2 * OV
    ext_cols = CY + 2 * OV

    def solve_one(device_index):
        row_start = (device_index // N_GY) * CX
        col_start = (device_index % N_GY) * CY

        def window(array):
            return lax.dynamic_slice(array, (jnp.int32(0), row_start, col_start), (array.shape[0], ext_rows, ext_cols))

        correction = smooth(window(residual), tuple(window(coefficient) for coefficient in coeffs),
                            window(diagonal_term), SWEEPS)
        return correction[:, OV:OV + CX, OV:OV + CY]

    pieces = lax.map(solve_one, jnp.arange(N_GX * N_GY, dtype=jnp.int32))
    return pieces.reshape(N_GX, N_GY, DIE_PLIES, CX, CY).transpose(2, 0, 3, 1, 4).reshape(DIE_PLIES, MESH_HEIGHT, MESH_WIDTH)


def reference(material, material_table, sink_cond, drain_current, instance_tile, instance_power):
    rim_width = OV + 1
    enlarge = ((0, 0), (rim_width, rim_width), (rim_width, rim_width))
    lateral = jnp.pad(lookup(material, material_table[0]), enlarge)
    vertical_cond = jnp.pad(lookup(material, material_table[1]), enlarge)
    coeffs, diagonal_term, inner_faces = face_terms(lateral, vertical_cond, jnp.pad(sink_cond, rim_width), OV)
    coarse_stack = coarse_terms(inner_faces, MX, MY)
    coarse_diag = coarse_diagonal(coarse_stack, DIE_PLIES)
    tile_sums = jax.ops.segment_sum(instance_power, instance_tile, num_segments=NTILES)
    tile_sums = tile_sums.reshape(N_GX, N_GY, TPX, TPY).transpose(0, 2, 1, 3).reshape(N_GX * TPX, N_GY * TPY)
    dynamic_wattage = distribute(tile_sums / (PB * PB), PB, PB)
    wattage_wide = jnp.pad(dynamic_wattage, OV)
    drain_current_wide = jnp.pad(drain_current, OV)
    margin_fill = ((0, 0), (OV, OV), (OV, OV))
    thermal_rise = jnp.zeros((DIE_PLIES, MESH_HEIGHT, MESH_WIDTH), jnp.float32)
    for outer_step in range(OUTER):
        thermal_forcing = assemble_forcing(wattage_wide, drain_current_wide, jnp.pad(thermal_rise, margin_fill))
        for inner_step in range(INNER):
            margined_array = jnp.pad(thermal_rise, enlarge)
            residual = residual_of(thermal_forcing, margined_array, coeffs, diagonal_term)
            subdomain_piece = local_solves(residual, coeffs, diagonal_term)
            own_resid = residual[:, OV:OV + MESH_HEIGHT, OV:OV + MESH_WIDTH]
            coarse_resid = own_resid.reshape(DIE_PLIES, MX, AGGREGATE_HEIGHT, MY, AGGREGATE_WIDTH).sum(axis=(2, 4))
            aggregate_estimate = coarse_solve(coarse_resid, coarse_stack, coarse_diag, DIE_PLIES, CJ)
            thermal_rise = thermal_rise + subdomain_piece + distribute(aggregate_estimate, AGGREGATE_HEIGHT, AGGREGATE_WIDTH)
    return thermal_rise, dynamic_wattage
```

```python
import functools

import jax
import jax.numpy as jnp
from jax import lax
from jax.experimental import pallas as pl
from jax.experimental.pallas import tpu as pltpu
from jax.sharding import PartitionSpec as P

MESH = pl.DeviceIdType.MESH
F32 = jnp.float32
BF16 = jnp.bfloat16

NL = 4
N = 256
LN = 128
RO = 16
NR = N + 2 * RO
SW = 512
OUTER = 2
INNER = 2
CJ = 8
DAMPING = 0.8
DRAIN_SLOPE = 0.5
FACE_FLOOR = 0.5
BALANCE_WEIGHT = 0.5
DIRS = ((-1, -1), (-1, 0), (-1, 1), (0, -1), (0, 1), (1, -1), (1, 0), (1, 1))
DIAG = tuple(d for d in DIRS if d[0] and d[1])
OFF_LINE = tuple(d for d in DIRS if d[1])


def iota(shape, dim):
    return lax.broadcasted_iota(jnp.int32, shape, dim)


def harmonic(a, b):
    return 2.0 * a * b / jnp.maximum(a + b, FACE_FLOOR)


def shift(x, amount, axis):
    return pltpu.roll(x, amount % x.shape[axis], axis)


def lookup(ids, table):
    level = list(table)
    for bit in range(4):
        odd = ((ids >> bit) & 1) == 1
        level = [jnp.where(odd, level[2 * k + 1], level[2 * k]) for k in range(len(level) // 2)]
    return level[0]


def exact_dot(a, b):
    return lax.dot_general(
        a, b, (((1,), (0,)), ((), ())), precision=lax.Precision.HIGHEST, preferred_element_type=F32
    )


def pieces(x, count):
    out = []
    for _ in range(count - 1):
        part = x.astype(BF16)
        out.append(part)
        x = x - part.astype(F32)
    return out + [x.astype(BF16)]


def pick_dot(x, ones):
    return sum(jnp.dot(part, ones, preferred_element_type=F32) for part in pieces(x, 3))


class Layout:
    def __init__(self):
        self.count = 0

    def take(self):
        self.count += 1
        return self.count - 1


def kernel(nx, ny, *refs):
    (mat, tab, sink, drain, inst_tile, inst_power, out, dyn_out) = refs[:8]
    (
        lat, ver, fr, fc, fv, dg, wg, src, dyn, drn, snk, t_, r_, e1_,
        cf_t, cf_e, cf_f, acc, acc_n, pk, onehot_a, onehot_b, cb, cbn,
        tsum, tin1, tred, tin2,
        sq_row, rq_row, sq_e, rq_we, rq_o,
        cm, cmr, coef, ct, ln, nb, s2, ls2, cv, xt,
        st_row, rt_row, es, rt_we, rt_d,
        ssem, rsem,
    ) = refs[8:]
    mx, my = lax.axis_index("gx"), lax.axis_index("gy")

    def at(dx, dy):
        return {"gx": lax.rem(mx + (dx + nx), nx), "gy": lax.rem(my + (dy + ny), ny)}

    partners = [(d, 0) for d in range(1, nx)] + [(0, d) for d in range(1, ny)] + list(DIAG)
    barrier = pltpu.get_barrier_semaphore()
    for d in partners:
        pl.semaphore_signal(barrier, inc=1, device_id=at(*d), device_id_type=MESH)

    numbers = Layout()
    started = []

    def send(a, b, to):
        k = numbers.take()
        copy = pltpu.make_async_remote_copy(
            src_ref=a, dst_ref=b, send_sem=ssem.at[k], recv_sem=rsem.at[k],
            device_id=at(*to), device_id_type=MESH,
        )
        copy.start()
        started.append(copy)
        return copy

    lane8 = iota((8, LN), 1)
    first_lane = lane8 == 0
    last_lane = lane8 == LN - 1
    low_half = lane8 < LN // 2

    cols_all, rows_all = 32 * ny, 32 * nx
    n_inst = inst_tile.shape[0] * LN
    sub_c = iota((cols_all, LN), 0)
    sub_r = iota((rows_all, LN), 0)
    for k in range(n_inst // LN):
        t = inst_tile[k : k + 1, :]
        s = t >> 10
        row = (s // ny) * 32 + ((t >> 5) & 31)
        col = (s % ny) * 32 + (t & 31)
        span = slice(k * LN, (k + 1) * LN)
        onehot_a[:, span] = jnp.where(sub_c == col, 1.0, 0.0).astype(BF16)
        hit = sub_r == row
        for q, part in enumerate(pieces(inst_power[k : k + 1, :], 3)):
            onehot_b[q, :, span] = jnp.where(hit, part.astype(F32), 0.0).astype(BF16)
    total = None
    for q in range(3):
        term = lax.dot_general(
            onehot_a[...], onehot_b[q], (((1,), (1,)), ((), ())), preferred_element_type=F32
        )
        total = term if total is None else total + term
    tsum[0:8, :] = jnp.zeros((8, rows_all), F32)
    tsum[8 : 8 + cols_all, :] = total
    tsum[8 + cols_all :, :] = jnp.zeros((8, rows_all), F32)

    def window(j):
        return tsum.at[pl.ds(pl.multiple_of(j * 32, 32), 48), :]

    def pack(values):
        packed = jnp.zeros((8, LN), F32)
        for q, (a, b) in enumerate(values):
            both = shift(jnp.where(low_half, a, b), -(4 * q + 2), 1)
            mine = (lane8 >= 124 - 4 * q) & (lane8 < 128 - 4 * q)
            packed = jnp.where(mine, both, packed)
        return packed

    halves = (slice(0, LN), slice(LN, N))

    def raw(rows):
        mats = [tuple(mat[l, rows, h].astype(F32) for h in halves) for l in range(NL)]
        return mats + [tuple(a[rows, h] for h in halves) for a in (sink, drain)]

    @pl.loop(0, N // 8)
    def _(k):
        rows = pl.ds(pl.multiple_of(k * 8, 8), 8)
        pk[rows, :] = pack(raw(rows))

    for k in range(2):
        sq_e[:, k * LN : (k + 1) * LN] = pk[k * LN : (k + 1) * LN, :].T[104:128, :]
    for side, rows in enumerate((slice(0, 8), slice(N - 8, N))):
        for q, (a, b) in enumerate(raw(rows)):
            sq_row[side, q, 0] = a
            sq_row[side, q, 1] = b

    pl.semaphore_wait(barrier, len(partners))

    tile_in = []
    for d in range(1, ny):
        j = lax.rem(my + d, ny)
        tile_in.append(send(window(j), tin1.at[d - 1], (0, d)))
    margin_row = [send(sq_row.at[s], rq_row.at[s], (2 * s - 1, 0)) for s in range(2)]
    margin_we = [send(sq_e, rq_we.at[s], (0, 2 * s - 1)) for s in range(2)]
    margin_o = {}
    for k, d in enumerate([(-1, 0), (1, 0)] + list(DIAG)):
        half = 0 if d[0] < 0 else 1
        margin_o[d] = (k, send(sq_e.at[:, pl.ds(half * LN, LN)], rq_o.at[k], d))

    col_n = iota((LN, LN), 1)
    row_n = iota((LN, LN), 0)
    for l in range(NL):
        for h in range(2):
            span = pl.ds((2 * l + h) * LN, LN)
            goal = l * 32 + 8 + h * 4 + (row_n >> 5)
            cb[span, :] = jnp.where(col_n == goal, 1.0, 0.0).astype(BF16)
            hit = ((row_n & 31) == 31) & (col_n == goal)
            if h == 0:
                hit = hit | ((row_n == 0) & (col_n == l * 32 + 7))
            cbn[span, :] = jnp.where(hit, 1.0, 0.0).astype(BF16)
    table = [[tab[q, k] for k in range(16)] for q in range(2)]

    zero8 = jnp.zeros((8, LN), F32)
    for ref, places in ((t_, (0, NR - 8)), (fr, (0,)), (lat, (NR - 8,))):
        for l in range(NL):
            for h in range(2):
                for place in places:
                    ref[l, h, place : place + 8, :] = zero8

    @pl.loop(0, N // 8)
    def _(k):
        rows = pl.ds(pl.multiple_of(k * 8, 8), 8)
        into = pl.ds(pl.multiple_of(k * 8 + RO, 8), 8)
        for h in range(2):
            for l in range(NL):
                ids = mat[l, rows, halves[h]]
                lat[l, h, into, :] = lookup(ids, table[0])
                ver[l, h, into, :] = lookup(ids, table[1])
            snk[h, into, :] = sink[rows, halves[h]]
            drn[h, into, :] = drain[rows, halves[h]]

    total = window(my)[...]
    for d in range(1, ny):
        tile_in[d - 1].wait_recv()
        total = total + tin1[d - 1]
    for x in range(nx):
        tred[x] = shift(total, -(32 * x - 1), 1)[:, :LN]
    tile_in2 = []
    for d in range(1, nx):
        x = lax.rem(mx + d, nx)
        tile_in2.append(send(tred.at[x], tin2.at[d - 1], (d, 0)))

    edge_n = jnp.where(mx == 0, 0.0, 1.0)
    edge_s = jnp.where(mx == nx - 1, 0.0, 1.0)
    edge_w = jnp.where(my == 0, 0.0, 1.0)
    edge_e = jnp.where(my == ny - 1, 0.0, 1.0)
    for c in margin_row:
        c.wait_recv()
    for slot, base, keep in ((1, RO - 8, edge_n), (0, RO + N, edge_s)):
        rows = slice(base, base + 8)
        for h in range(2):
            for l in range(NL):
                ids = rq_row[slot, l, h].astype(jnp.int32)
                lat[l, h, rows, :] = lookup(ids, table[0]) * keep
                ver[l, h, rows, :] = lookup(ids, table[1]) * keep
            snk[h, rows, :] = rq_row[slot, 4, h] * keep
            drn[h, rows, :] = rq_row[slot, 5, h] * keep
    for c in margin_we:
        c.wait_recv()
    for _, c in margin_o.values():
        c.wait_recv()

    def from_dir(d):
        return rq_o[margin_o[(-d[0], -d[1])][0]]

    west = jnp.concatenate([from_dir((-1, -1)), rq_we[1], from_dir((1, -1))], axis=1)
    east = jnp.concatenate([from_dir((-1, 1)), rq_we[0], from_dir((1, 1))], axis=1)
    inner = jnp.concatenate([from_dir((-1, 0)), sq_e[...], from_dir((1, 0))], axis=1)
    c24 = iota((24, SW), 0) & 3
    outer = jnp.where(c24 < 2, west, east)
    strip_lane = iota((16, SW), 1)
    c16 = iota((16, SW), 0) & 3
    one = jnp.ones((16, SW), F32)
    keep_rows = jnp.where(strip_lane < LN, one * edge_n, jnp.where(strip_lane >= LN + N, one * edge_s, one))
    keep_outer = keep_rows * jnp.where(c16 < 2, one * edge_w, one * edge_e)
    sm_ids = outer[8:24, :].astype(jnp.int32)
    se_ids = inner[8:24, :].astype(jnp.int32)
    lat_m = lookup(sm_ids, table[0]) * keep_outer
    ver_m = lookup(sm_ids, table[1]) * keep_outer
    lat_e = lookup(se_ids, table[0]) * keep_rows
    row8 = iota((8, SW), 0)
    zero_s = jnp.zeros((8, SW), F32)
    mixed = shift(outer[0:8, :], 4, 0)
    sink_s = jnp.concatenate([jnp.where(row8 < 4, mixed, 0.0), zero_s], axis=0)
    drain_s = jnp.concatenate([zero_s, jnp.where(row8 >= 4, mixed, 0.0)], axis=0)

    def from_outside(x):
        return jnp.where(c16 == 1, shift(x, 1, 0), shift(x, -1, 0))

    def from_inside(x):
        return jnp.where(c16 == 1, shift(x, -1, 0), shift(x, 1, 0))

    fs_out = harmonic(lat_m, from_outside(lat_m))
    fs_in = harmonic(lat_m, from_inside(lat_e))
    fs_row = harmonic(lat_m, shift(lat_m, -1, 1))
    fs_row_prev = shift(fs_row, 1, 1)
    layer_rows = iota((16, SW), 0)
    fs_ver = jnp.where(layer_rows >= 4, harmonic(ver_m, shift(ver_m, 4, 0)), 0.0)
    fs_ver_prev = shift(fs_ver, -4, 0)
    d_s = jnp.maximum(fs_out + fs_in + fs_row + fs_row_prev + fs_ver + fs_ver_prev + sink_s, FACE_FLOOR)
    w_s = DAMPING / d_s

    def column_form(x, ref):
        x = jnp.where(c16 == 1, shift(x, -1, 0), jnp.where(c16 == 2, shift(x, 1, 0), 0.0))
        for k in range(SW // LN):
            block = jnp.concatenate(
                [x[:, k * LN : (k + 1) * LN], jnp.zeros((LN - 16, LN), F32)], axis=0
            )
            ref[k * LN : (k + 1) * LN, :] = block.T

    def columns(ref, base):
        tile = ref[pl.ds(base + (LN - RO), 8), :]
        return [shift(tile, 114 + 4 * l, 1) for l in range(NL)]

    column_form(fs_in, cf_f)

    def faces(base, sums):
        bf = columns(cf_f, base)
        here, below = pl.ds(base, 8), pl.ds(base + 1, 8)
        vs = [[ver[l, h, here, :] for h in range(2)] for l in range(NL)]
        for l in range(NL):
            a0, a1 = lat[l, 0, here, :], lat[l, 1, here, :]
            ra0, ra1 = shift(a0, -1, 1), shift(a1, -1, 1)
            c0 = harmonic(a0, jnp.where(last_lane, ra1, ra0))
            c1 = jnp.where(last_lane, bf[l], harmonic(a1, ra1))
            fc[l, 0, here, :] = c0
            fc[l, 1, here, :] = c1
            for h, a in ((0, a0), (1, a1)):
                fr[l, h, here, :] = harmonic(a, lat[l, h, below, :])
            if sums is not None:
                sums[0][2 * l] += jnp.where(first_lane, bf[l], c0)
                sums[0][2 * l + 1] += c1
            for h in range(2):
                if l < NL - 1:
                    v = harmonic(vs[l][h], vs[l + 1][h])
                    fv[l, h, here, :] = v
                else:
                    v = snk[h, here, :]
                if sums is not None:
                    sums[1][2 * l + h] += v

    faces(RO - 8, None)
    faces(RO + N, None)

    @pl.loop(0, N // 32)
    def _(a):
        sums = [[zero8] * 8, [zero8] * 8]
        for k in range(4):
            faces(pl.multiple_of(RO + 32 * a + 8 * k, 8), sums)
        rows = pl.ds(pl.multiple_of(a * 8, 8), 8)
        for q in range(8):
            acc_n[rows, q * LN : (q + 1) * LN] = sums[0][q]
            acc[rows, q * LN : (q + 1) * LN] = sums[1][q]

    @pl.loop(0, N // 8 + 2)
    def _(k):
        base = pl.multiple_of(RO - 8 + 8 * k, 8)
        here, above = pl.ds(base, 8), pl.ds(base - 1, 8)
        bf = columns(cf_f, base)
        for l in range(NL):
            c0, c1 = fc[l, 0, here, :], fc[l, 1, here, :]
            rc0, rc1 = shift(c0, 1, 1), shift(c1, 1, 1)
            west_face = (jnp.where(first_lane, bf[l], rc0), jnp.where(first_lane, rc0, rc1))
            for h, c in ((0, c0), (1, c1)):
                d = fr[l, h, above, :] + fr[l, h, here, :] + west_face[h] + c
                if l > 0:
                    d = d + fv[l - 1, h, here, :]
                if l < NL - 1:
                    d = d + fv[l, h, here, :]
                else:
                    d = d + snk[h, here, :]
                d = jnp.maximum(d, FACE_FLOOR)
                dg[l, h, here, :] = d
                wg[l, h, here, :] = DAMPING / d

    block_lane = lane8 & 31
    own_block = (block_lane >= 8) & (block_lane < 16)

    def block_rows(x):
        return x.reshape(8, 8, LN).sum(axis=1)

    def edge_sums(start):
        rows = [fr[l, h, pl.ds(start, 8, stride=32), :] for l in range(NL) for h in range(2)]
        return pick_dot(jnp.concatenate(rows, axis=1), cb[...])

    c_east = edge_sums(RO + 31)
    c_east_prev = edge_sums(RO - 1)
    c_north_wide = block_rows(pick_dot(acc_n[...], cbn[...]))
    c_north = jnp.where(own_block, c_north_wide, 0.0)
    c_north_prev = jnp.where(own_block, shift(c_north_wide, 1, 1), 0.0)
    up_sink = block_rows(pick_dot(acc[...], cb[...]))
    c_up = jnp.where(lane8 < 96, up_sink, 0.0)
    c_sink = jnp.where(lane8 >= 96, up_sink, 0.0)
    c_diag = c_east + c_east_prev + c_north + c_north_prev + c_up + shift(c_up, 32, 1) + c_sink
    for q, x in enumerate((c_east, c_north, c_up, c_diag)):
        cm[q] = x
    ct[0, 1] = c_diag
    cm_in = {d: (k, send(cm, cmr.at[k], d)) for k, d in enumerate(DIRS)}

    total = tred[mx]
    for d in range(1, nx):
        tile_in2[d - 1].wait_recv()
        total = total + tin2[d - 1]
    total = total * (1.0 / 64.0)
    wide = jnp.concatenate([total, jnp.zeros((LN - 48, LN), F32)], axis=0)
    to_rows = jnp.where(iota((LN, SW), 0) == ((iota((LN, SW), 1) - 120) >> 3), 1.0, 0.0)
    dyn_t = exact_dot(wide[:48, :], to_rows)
    dyn_s = jnp.where(layer_rows == 13, dyn_t[7:8, :], jnp.where(layer_rows == 14, dyn_t[40:41, :], 0.0))
    spread_rows = jnp.where(iota((NR, LN), 1) == ((iota((NR, LN), 0) - 8) >> 3), 1.0, 0.0)
    spread_cols = jnp.where(iota((LN, N), 0) == (iota((LN, N), 1) >> 3) + 8, 1.0, 0.0)
    dyn_all = exact_dot(exact_dot(spread_rows, wide.T), spread_cols)
    for h in range(2):
        dyn[h] = dyn_all[:, halves[h]]
    dyn_out[...] = dyn_all[RO : RO + N, :]

    for _, c in cm_in.values():
        c.wait_recv()

    def assemble(own, other):
        rows = []
        for dx in (-1, 0, 1):
            centre = own if dx == 0 else other((dx, 0))
            rows.append(centre + shift(other((dx, -1)), -8, 1) + shift(other((dx, 1)), 8, 1))
        return jnp.concatenate(rows, axis=0)

    w_east, w_north, w_up, w_diag = (
        assemble(cm[q], lambda d, q=q: cmr[cm_in[(-d[0], -d[1])][0], q]) for q in range(4)
    )
    gain = jnp.where((iota((24, LN), 1) & 31) < 24, DAMPING / jnp.maximum(w_diag, 1e-30), 0.0)
    coef[0] = gain
    coef[1] = gain * w_east
    coef[2] = gain * shift(w_east, 1, 0)
    coef[3] = gain * w_north
    coef[4] = gain * shift(w_north, 1, 1)
    coef[5] = gain * w_up
    coef[6] = gain * shift(w_up, 32, 1)

    def couple(ref, base, edge, live):
        here, above, below = pl.ds(base, 8), pl.ds(base - 1, 8), pl.ds(base + 1, 8)
        res = [[None, None] for _ in range(NL)]
        mid = [[ref[l, h, here, :] for h in range(2)] for l in range(live)]
        for l in range(live):
            a0, a1 = mid[l]
            f0, f1 = fc[l, 0, here, :], fc[l, 1, here, :]
            ra0, ra1 = shift(a0, -1, 1), shift(a1, -1, 1)
            p0, p1 = shift(f0 * a0, 1, 1), shift(f1 * a1, 1, 1)
            lateral = (
                f0 * jnp.where(last_lane, ra1, ra0) + jnp.where(first_lane, edge[l], p0),
                jnp.where(last_lane, edge[l], f1 * ra1) + jnp.where(first_lane, p0, p1),
            )
            for h in range(2):
                res[l][h] = (
                    lateral[h]
                    + fr[l, h, above, :] * ref[l, h, above, :]
                    + fr[l, h, here, :] * ref[l, h, below, :]
                )
        for l in range(live):
            for h in range(2):
                for face, to in ((l - 1, l - 1), (l, l + 1)):
                    if 0 <= to < NL:
                        term = fv[face, h, here, :] * mid[l][h]
                        res[to][h] = term if res[to][h] is None else res[to][h] + term
        return mid, res

    strip_top = layer_rows >= 12

    def source_strip(tm):
        return jnp.where(strip_top, dyn_s + drain_s * jnp.exp(DRAIN_SLOPE * jnp.where(strip_top, tm, 0.0)), 0.0)

    tm = te = source_s = None
    sweeps = OUTER * INNER
    for it in range(sweeps):
        first, last = it == 0, it == sweeps - 1
        fresh = it % INNER == 0
        if fresh:
            source_s = dyn_s + drain_s if first else source_strip(tm)
        if first:
            r_s = source_s
        else:
            r_s = source_s - (
                d_s * tm
                - fs_out * from_outside(tm)
                - fs_in * from_inside(te)
                - fs_row * shift(tm, -1, 1)
                - fs_row_prev * shift(tm, 1, 1)
                - fs_ver * shift(tm, 4, 0)
                - fs_ver_prev * shift(tm, -4, 0)
            )
            column_form(fs_in * tm, cf_t)
        column_form(fs_in * (w_s * r_s), cf_e)

        def residual(base, sums):
            here = pl.ds(base, 8)
            if first:
                for h in range(2):
                    r = dyn[h, here, :] + drn[h, here, :]
                    src[h, here, :] = r
                    r_[0, h, here, :] = r
                    e1_[0, h, here, :] = wg[0, h, here, :] * r
                    if sums is not None:
                        sums[h] += r
                return
            mid, res = couple(t_, base, columns(cf_t, base), NL)
            for l in range(NL):
                for h in range(2):
                    r = res[l][h] - dg[l, h, here, :] * mid[l][h]
                    if l == 0:
                        if fresh:
                            s = dyn[h, here, :] + drn[h, here, :] * jnp.exp(DRAIN_SLOPE * mid[0][h])
                            src[h, here, :] = s
                        else:
                            s = src[h, here, :]
                        r = r + s
                    r_[l, h, here, :] = r
                    e1_[l, h, here, :] = wg[l, h, here, :] * r
                    if sums is not None:
                        sums[2 * l + h] += r

        residual(RO - 8, None)
        residual(RO + N, None)

        @pl.loop(0, N // 32)
        def _(a):
            sums = [zero8] * 8
            for k in range(4):
                residual(pl.multiple_of(RO + 32 * a + 8 * k, 8), sums)
            rows = pl.ds(pl.multiple_of(a * 8, 8), 8)
            for q in range(8):
                acc[rows, q * LN : (q + 1) * LN] = sums[q]

        own_c = block_rows(pick_dot(acc[...], cb[...]))
        ct[it, 0] = own_c
        parts = 2 if first else 1
        line = [
            send(ct.at[it, pl.ds(0, parts)], ln.at[it, d - 1, pl.ds(0, parts)], (d, 0)) for d in range(1, nx)
        ]
        side = {
            d: (k, send(ct.at[it, 0], nb.at[it, k], d)) for k, d in enumerate(OFF_LINE)
        }

        live = 1 if first else NL

        @pl.loop(0, N // 8)
        def _(k):
            base = pl.multiple_of(RO + 8 * k, 8)
            here = pl.ds(base, 8)
            mid, res = couple(e1_, base, columns(cf_e, base), live)
            tops = []
            for l in range(NL):
                pair = []
                for h in range(2):
                    u = None
                    if l < live:
                        u = (1.0 - DAMPING) * mid[l][h] + wg[l, h, here, :] * (r_[l, h, here, :] + res[l][h])
                    elif res[l][h] is not None:
                        u = wg[l, h, here, :] * res[l][h]
                    else:
                        u = zero8
                    if not first:
                        u = u + t_[l, h, here, :]
                    t_[l, h, here, :] = u
                    pair.append(u)
                tops.append(tuple(pair))
            if not last:
                pk[pl.ds(pl.multiple_of(8 * k, 8), 8), :] = pack(tops)

        if not last:
            for k in range(2):
                es[it, :, k * LN : (k + 1) * LN] = pk[k * LN : (k + 1) * LN, :].T[112:128, :]
            for s, base in enumerate((RO, RO + N - 8)):
                for l in range(NL):
                    for h in range(2):
                        st_row[it, s, l, h] = t_[l, h, base : base + 8, :]
            row_in = [send(st_row.at[it, s], rt_row.at[it, s], (2 * s - 1, 0)) for s in range(2)]
            we_in = [send(es.at[it], rt_we.at[it, s], (0, 2 * s - 1)) for s in range(2)]
            diag_in = {}
            for k, d in enumerate(DIAG):
                half = 0 if d[0] < 0 else 1
                diag_in[d] = (k, send(es.at[it, :, pl.ds(half * LN, LN)], rt_d.at[it, k], d))

        total = [ct[it, q] for q in range(parts)]
        for d in range(1, nx):
            line[d - 1].wait_recv()
            for q in range(parts):
                total[q] = total[q] + ln[it, d - 1, q]
        sub8 = iota((8, LN), 0)
        packed = jnp.where(sub8 == 0, total[0].sum(axis=0, keepdims=True), 0.0)
        if first:
            packed = jnp.where(sub8 == 1, total[1].sum(axis=0, keepdims=True), packed)
        s2[it] = packed
        gather = [send(s2.at[it], ls2.at[it, d - 1], (0, d)) for d in range(1, ny)]
        for _, c in side.values():
            c.wait_recv()

        def other(d):
            if d[1] == 0:
                return ln[it, 0 if d[0] < 0 else nx - 2, 0]
            return nb[it, side[(-d[0], -d[1])][0]]

        rw = coef[0] * assemble(own_c, other)
        x = rw
        for _ in range(CJ - 1):
            x = (
                (1.0 - DAMPING) * x + rw
                + coef[1] * shift(x, -1, 0) + coef[2] * shift(x, 1, 0)
                + coef[3] * shift(x, -1, 1) + coef[4] * shift(x, 1, 1)
                + coef[5] * shift(x, -32, 1) + coef[6] * shift(x, 32, 1)
            )
        total = packed
        for d in range(1, ny):
            gather[d - 1].wait_recv()
            total = total + ls2[it, d - 1]
        sums = total.sum(axis=1, keepdims=True)
        if first:
            diag_total = sums[1:2, :]
        x = x + BALANCE_WEIGHT * sums[0:1, :] / diag_total

        lane24 = iota((24, LN), 1)
        for l in range(NL):
            for h in range(2):
                cv[l, h] = jnp.take_along_axis(x, l * 32 + 8 + h * 4 + (lane24 >> 5), axis=1)

        if last:
            @pl.loop(0, N // 32)
            def _(a):
                for l in range(NL):
                    for h in range(2):
                        add = cv[l, h, pl.ds(8 + a, 1), :]
                        for k in range(4):
                            rows = pl.ds(pl.multiple_of(32 * a + 8 * k, 8), 8)
                            here = pl.ds(pl.multiple_of(RO + 32 * a + 8 * k, 8), 8)
                            out[l, rows, halves[h]] = t_[l, h, here, :] + add
            break

        @pl.loop(0, N // 32)
        def _(a):
            for l in range(NL):
                for h in range(2):
                    add = cv[l, h, pl.ds(8 + a, 1), :]
                    for k in range(4):
                        here = pl.ds(pl.multiple_of(RO + 32 * a + 8 * k, 8), 8)
                        t_[l, h, here, :] = t_[l, h, here, :] + add

        xt[...] = jnp.concatenate([x, jnp.zeros((LN - 24, LN), F32)], axis=0).T
        row16 = iota((16, LN), 0)
        ring = jnp.zeros((16, LN), F32)
        own_v = ring
        for l in range(NL):
            for pair in range(2):
                mine = (row16 >> 1) == 2 * (NL - 1 - l) + pair
                ring = jnp.where(mine, xt[l * 32 + (7, 16)[pair] : l * 32 + (7, 16)[pair] + 1, :], ring)
                own_v = jnp.where(mine, xt[l * 32 + (15, 8)[pair] : l * 32 + (15, 8)[pair] + 1, :], own_v)
        lane16 = iota((16, LN), 1)

        def along(v):
            return jnp.concatenate(
                [jnp.take_along_axis(v, 4 + 4 * k + (lane16 >> 5), axis=1) for k in range(SW // LN)], axis=1
            )

        for c in row_in:
            c.wait_recv()
        for slot, base, at_row in ((1, RO - 8, 7), (0, RO + N, 16)):
            for l in range(NL):
                for h in range(2):
                    t_[l, h, base : base + 8, :] = rt_row[it, slot, l, h] + cv[l, h, at_row : at_row + 1, :]
        for c in we_in:
            c.wait_recv()
        for _, c in diag_in.values():
            c.wait_recv()

        def corner(d):
            return rt_d[it, diag_in[(-d[0], -d[1])][0]]

        west = jnp.concatenate([corner((-1, -1)), rt_we[it, 1], corner((1, -1))], axis=1)
        east = jnp.concatenate([corner((-1, 1)), rt_we[it, 0], corner((1, 1))], axis=1)
        tm = jnp.where(c16 < 2, west, east) + along(ring)
        blank = jnp.zeros((16, LN), F32)
        te = jnp.concatenate([blank, es[it], blank], axis=1) + along(own_v)

    for c in started:
        c.wait_send()


def n_copies(nx, ny):
    setup = (ny - 1) + 2 + 2 + 6 + (nx - 1) + 8
    each = (nx - 1) + 6 + (ny - 1)
    return setup + OUTER * INNER * each + (OUTER * INNER - 1) * 8


def solution(mesh):
    nx, ny = mesh.shape["gx"], mesh.shape["gy"]
    its = OUTER * INNER

    def step(material, material_table, sink_cond, drain_current, instance_tile, instance_power):
        n_inst = instance_tile.shape[0]
        field = pltpu.VMEM((NL, 2, NR, LN), F32)
        single = pltpu.VMEM((2, NR, LN), F32)
        vm = lambda *shape: pltpu.VMEM(shape, F32)
        copies = n_copies(nx, ny)
        scratch = [
            field, field, field, field, pltpu.VMEM((NL - 1, 2, NR, LN), F32), field, field,
            single, single, single, single, field, field, field,
            vm(SW, LN), vm(SW, LN), vm(SW, LN), vm(64, 8 * LN), vm(64, 8 * LN), vm(N, LN),
            pltpu.VMEM((32 * ny, n_inst), BF16), pltpu.VMEM((3, 32 * nx, n_inst), BF16),
            pltpu.VMEM((8 * LN, LN), BF16), pltpu.VMEM((8 * LN, LN), BF16),
            vm(32 * ny + 16, 32 * nx), vm(ny - 1, 48, 32 * nx), vm(nx, 48, LN), vm(nx - 1, 48, LN),
            vm(2, 6, 2, 8, LN), vm(2, 6, 2, 8, LN), vm(24, N), vm(2, 24, N), vm(6, 24, LN),
            vm(4, 8, LN), vm(8, 4, 8, LN), vm(7, 24, LN), vm(its, 2, 8, LN), vm(its, nx - 1, 2, 8, LN),
            vm(its, 6, 8, LN), vm(its, 8, LN), vm(its, ny - 1, 8, LN), vm(NL, 2, 24, LN), vm(LN, LN),
            vm(its - 1, 2, NL, 2, 8, LN), vm(its - 1, 2, NL, 2, 8, LN),
            vm(its - 1, 16, N), vm(its - 1, 2, 16, N), vm(its - 1, 4, 16, LN),
            pltpu.SemaphoreType.DMA((copies,)), pltpu.SemaphoreType.DMA((copies,)),
        ]
        vmem = pl.BlockSpec(memory_space=pltpu.VMEM)
        smem = pl.BlockSpec(memory_space=pltpu.SMEM)
        return pl.pallas_call(
            functools.partial(kernel, nx, ny),
            out_shape=(
                jax.ShapeDtypeStruct((NL, N, N), F32),
                jax.ShapeDtypeStruct((N, N), F32),
            ),
            in_specs=[vmem, smem, vmem, vmem, vmem, vmem],
            out_specs=(vmem, vmem),
            scratch_shapes=scratch,
            compiler_params=pltpu.CompilerParams(
                collective_id=0, has_side_effects=True, vmem_limit_bytes=56 * 1024 * 1024
            ),
        )(
            material,
            material_table,
            sink_cond,
            drain_current,
            instance_tile.reshape(n_inst // LN, LN),
            instance_power.reshape(n_inst // LN, LN),
        )

    return jax.shard_map(
        step,
        mesh=mesh,
        in_specs=(
            P(None, "gx", "gy"),
            P(),
            P("gx", "gy"),
            P("gx", "gy"),
            P(("gx", "gy")),
            P(("gx", "gy")),
        ),
        out_specs=(P(None, "gx", "gy"), P("gx", "gy")),
        check_vma=False,
    )
```

```python
import functools

import jax
import jax.numpy as jnp
from jax import lax
from jax.experimental import pallas as pl
from jax.experimental.pallas import tpu as pltpu
from jax.sharding import PartitionSpec as P

MESH = pl.DeviceIdType.MESH
F32 = jnp.float32
BF16 = jnp.bfloat16

NL = 4
N = 256
LN = 128
RO = 16
NR = N + 2 * RO
SW = 512
OUTER = 2
INNER = 2
CJ = 8
DAMPING = 0.8
DRAIN_SLOPE = 0.5
FACE_FLOOR = 0.5
BALANCE_WEIGHT = 0.5
DIRS = ((-1, -1), (-1, 0), (-1, 1), (0, -1), (0, 1), (1, -1), (1, 0), (1, 1))
DIAG = tuple(d for d in DIRS if d[0] and d[1])
OFF_LINE = tuple(d for d in DIRS if d[1])


def iota(shape, dim):
    return lax.broadcasted_iota(jnp.int32, shape, dim)


def harmonic(a, b):
    return 2.0 * a * b / jnp.maximum(a + b, FACE_FLOOR)


def shift(x, amount, axis):
    return pltpu.roll(x, amount % x.shape[axis], axis)


def lookup(ids, table):
    level = list(table)
    for bit in range(4):
        odd = ((ids >> bit) & 1) == 1
        level = [jnp.where(odd, level[2 * k + 1], level[2 * k]) for k in range(len(level) // 2)]
    return level[0]


def exact_dot(a, b):
    return lax.dot_general(
        a, b, (((1,), (0,)), ((), ())), precision=lax.Precision.HIGHEST, preferred_element_type=F32
    )


def pieces(x, count):
    out = []
    for _ in range(count - 1):
        part = x.astype(BF16)
        out.append(part)
        x = x - part.astype(F32)
    return out + [x.astype(BF16)]


def pick_dot(x, ones):
    return sum(jnp.dot(part, ones, preferred_element_type=F32) for part in pieces(x, 3))


class Layout:
    def __init__(self):
        self.count = 0

    def take(self):
        self.count += 1
        return self.count - 1


def kernel(nx, ny, *refs):
    (mat_hbm, tab, sink_hbm, drain_hbm, inst_tile, inst_power, out_hbm, dyn_hbm) = refs[:8]
    (
        mat, sink, drain, out, dyn_out,
        lat, ver, fr, fc, fv, dg, wg, src, drn, snk, t_, r_, e1_,
        cf_t, cf_e, cf_f, acc, acc_n, pk, cb, cbn,
        dest, slots, sout, tin1, tred, tin2, dense_a, dense_b, ts, tst, th, dynr,
        sq_row, rq_row, sq_e, rq_we, rq_o,
        cm, cmr, coef, ct, nb, s1, ls1, s2, ls2, cv, xt,
        st_row, rt_row, es, rt_we, rt_d,
        ssem, rsem, lsem,
    ) = refs[8:]
    mx, my = lax.axis_index("gx"), lax.axis_index("gy")

    def at(dx, dy):
        return {"gx": lax.rem(mx + (dx + nx), nx), "gy": lax.rem(my + (dy + ny), ny)}

    partners = [(d, 0) for d in range(1, nx)] + [(0, d) for d in range(1, ny)] + list(DIAG)
    barrier = pltpu.get_barrier_semaphore()
    for d in partners:
        pl.semaphore_signal(barrier, inc=1, device_id=at(*d), device_id_type=MESH)

    fetch = [
        pltpu.make_async_copy(a, b, lsem.at[k])
        for k, (a, b) in enumerate(((mat_hbm, mat), (sink_hbm, sink), (drain_hbm, drain)))
    ]
    for c in fetch:
        c.start()

    numbers = Layout()
    started = []

    def send(a, b, to):
        k = numbers.take()
        copy = pltpu.make_async_remote_copy(
            src_ref=a, dst_ref=b, send_sem=ssem.at[k], recv_sem=rsem.at[k],
            device_id=at(*to), device_id_type=MESH,
        )
        copy.start()
        started.append(copy)
        return copy

    lane8 = iota((8, LN), 1)
    first_lane = lane8 == 0
    last_lane = lane8 == LN - 1
    low_half = lane8 < LN // 2

    devices = nx * ny
    chunks = inst_tile.shape[0]
    sub_d = iota((devices, LN), 0)
    lane_d = iota((devices, LN), 1)
    up_to = jnp.where(iota((LN, LN), 0) <= iota((LN, LN), 1), 1.0, 0.0).astype(BF16)
    for k in range(chunks):
        s = inst_tile[k : k + 1, :] >> 10
        owner = (s % ny) * nx + s // ny
        dest[:, k * LN : (k + 1) * LN] = jnp.where(sub_d == owner, 1.0, 0.0).astype(BF16)
    before = jnp.zeros((devices, 1), F32)
    slot_row = iota((64, LN), 0)
    for k in range(chunks):
        span = slice(k * LN, (k + 1) * LN)
        d = dest[:, span]
        within = jnp.dot(d, up_to, preferred_element_type=F32)
        rank = jnp.sum(d.astype(F32) * (within + before), axis=0, keepdims=True)
        before = before + within[:, LN - 1 : LN]
        at_slot = (slot_row & 31) == rank.astype(jnp.int32) - 1
        t = inst_tile[k : k + 1, :]
        ids = ((t & 992).astype(F32), (t & 31).astype(F32), jnp.zeros((1, LN), F32))
        for q, part in enumerate(pieces(inst_power[k : k + 1, :], 3)):
            value = jnp.where(slot_row < 32, part.astype(F32), ids[q])
            slots[q, :, span] = jnp.where(at_slot, value, 0.0).astype(BF16)
    total = None
    for q in range(3):
        term = lax.dot_general(
            dest[...], slots[q], (((1,), (1,)), ((), ())), preferred_element_type=F32
        )
        total = term if total is None else total + term
    sout[...] = jnp.concatenate([total, jnp.zeros((devices, LN - 64), F32)], axis=1)
    power_sum = jnp.zeros((8, LN), F32)
    for k in range(chunks // 8):
        power_sum = power_sum + inst_power[8 * k : 8 * k + 8, :]

    def bundle(j):
        return sout.at[pl.ds(pl.multiple_of(j * nx, nx), nx), :]

    pl.semaphore_wait(barrier, len(partners))
    tile_in = []
    for d in range(1, ny):
        tile_in.append(send(bundle(lax.rem(my + d, ny)), tin1.at[pl.ds(d * nx, nx)], (0, d)))
    tin1[0:nx, :] = bundle(my)[...]

    def pack(values):
        packed = jnp.zeros((8, LN), F32)
        for q, (a, b) in enumerate(values):
            both = shift(jnp.where(low_half, a, b), -(4 * q + 2), 1)
            mine = (lane8 >= 124 - 4 * q) & (lane8 < 128 - 4 * q)
            packed = jnp.where(mine, both, packed)
        return packed

    halves = (slice(0, LN), slice(LN, N))

    def raw(rows):
        mats = [tuple(mat[l, rows, h].astype(F32) for h in halves) for l in range(NL)]
        return mats + [tuple(a[rows, h] for h in halves) for a in (sink, drain)]

    for c in fetch:
        c.wait()

    @pl.loop(0, N // 32)
    def _(a):
        for k in range(4):
            rows = pl.ds(pl.multiple_of(a * 32 + k * 8, 8), 8)
            pk[rows, :] = pack(raw(rows))

    for k in range(2):
        sq_e[:, k * LN : (k + 1) * LN] = pk[k * LN : (k + 1) * LN, :].T[104:128, :]
    for side, rows in enumerate((slice(0, 8), slice(N - 8, N))):
        for q, (a, b) in enumerate(raw(rows)):
            sq_row[side, q, 0] = a
            sq_row[side, q, 1] = b

    margin_row = [send(sq_row.at[s], rq_row.at[s], (2 * s - 1, 0)) for s in range(2)]
    margin_we = [send(sq_e, rq_we.at[s], (0, 2 * s - 1)) for s in range(2)]
    margin_o = {}
    for k, d in enumerate([(-1, 0), (1, 0)] + list(DIAG)):
        half = 0 if d[0] < 0 else 1
        margin_o[d] = (k, send(sq_e.at[:, pl.ds(half * LN, LN)], rq_o.at[k], d))

    col_n = iota((LN, LN), 1)
    row_n = iota((LN, LN), 0)
    for l in range(NL):
        for h in range(2):
            span = pl.ds((2 * l + h) * LN, LN)
            goal = l * 32 + 8 + h * 4 + (row_n >> 5)
            cb[span, :] = jnp.where(col_n == goal, 1.0, 0.0).astype(BF16)
            hit = ((row_n & 31) == 31) & (col_n == goal)
            if h == 0:
                hit = hit | ((row_n == 0) & (col_n == l * 32 + 7))
            cbn[span, :] = jnp.where(hit, 1.0, 0.0).astype(BF16)
    table = [[tab[q, k] for k in range(16)] for q in range(2)]

    zero8 = jnp.zeros((8, LN), F32)
    for ref, places in ((t_, (0, NR - 8)), (fr, (0,)), (lat, (NR - 8,))):
        for l in range(NL):
            for h in range(2):
                for place in places:
                    ref[l, h, place : place + 8, :] = zero8

    @pl.loop(0, N // 8, init_carry=power_sum)
    def source_sum(k, source_sum):
        rows = pl.ds(pl.multiple_of(k * 8, 8), 8)
        into = pl.ds(pl.multiple_of(k * 8 + RO, 8), 8)
        for h in range(2):
            for l in range(NL):
                ids = mat[l, rows, halves[h]]
                lat[l, h, into, :] = lookup(ids, table[0])
                ver[l, h, into, :] = lookup(ids, table[1])
            snk[h, into, :] = sink[rows, halves[h]]
            d = drain[rows, halves[h]]
            drn[h, into, :] = d
            source_sum = source_sum + d
        return source_sum

    for c in tile_in:
        c.wait_recv()
    for x in range(nx):
        tred[x] = tin1[pl.ds(x, ny, stride=nx), :]
    tile_in2 = []
    for d in range(1, nx):
        x = lax.rem(mx + d, nx)
        tile_in2.append(send(tred.at[x], tin2.at[pl.ds(d * ny, ny)], (d, 0)))
    tin2[0:ny, :] = tred[mx]

    edge_n = jnp.where(mx == 0, 0.0, 1.0)
    edge_s = jnp.where(mx == nx - 1, 0.0, 1.0)
    edge_w = jnp.where(my == 0, 0.0, 1.0)
    edge_e = jnp.where(my == ny - 1, 0.0, 1.0)
    for c in margin_row:
        c.wait_recv()
    for slot, base, keep in ((1, RO - 8, edge_n), (0, RO + N, edge_s)):
        rows = slice(base, base + 8)
        for h in range(2):
            for l in range(NL):
                ids = rq_row[slot, l, h].astype(jnp.int32)
                lat[l, h, rows, :] = lookup(ids, table[0]) * keep
                ver[l, h, rows, :] = lookup(ids, table[1]) * keep
            snk[h, rows, :] = rq_row[slot, 4, h] * keep
            drn[h, rows, :] = rq_row[slot, 5, h] * keep
    for c in margin_we:
        c.wait_recv()
    for _, c in margin_o.values():
        c.wait_recv()

    def from_dir(d):
        return rq_o[margin_o[(-d[0], -d[1])][0]]

    west = jnp.concatenate([from_dir((-1, -1)), rq_we[1], from_dir((1, -1))], axis=1)
    east = jnp.concatenate([from_dir((-1, 1)), rq_we[0], from_dir((1, 1))], axis=1)
    inner = jnp.concatenate([from_dir((-1, 0)), sq_e[...], from_dir((1, 0))], axis=1)
    c24 = iota((24, SW), 0) & 3
    outer = jnp.where(c24 < 2, west, east)
    strip_lane = iota((16, SW), 1)
    c16 = iota((16, SW), 0) & 3
    one = jnp.ones((16, SW), F32)
    keep_rows = jnp.where(strip_lane < LN, one * edge_n, jnp.where(strip_lane >= LN + N, one * edge_s, one))
    keep_outer = keep_rows * jnp.where(c16 < 2, one * edge_w, one * edge_e)
    sm_ids = outer[8:24, :].astype(jnp.int32)
    se_ids = inner[8:24, :].astype(jnp.int32)
    lat_m = lookup(sm_ids, table[0]) * keep_outer
    ver_m = lookup(sm_ids, table[1]) * keep_outer
    lat_e = lookup(se_ids, table[0]) * keep_rows
    row8 = iota((8, SW), 0)
    zero_s = jnp.zeros((8, SW), F32)
    mixed = shift(outer[0:8, :], 4, 0)
    sink_s = jnp.concatenate([jnp.where(row8 < 4, mixed, 0.0), zero_s], axis=0)
    drain_s = jnp.concatenate([zero_s, jnp.where(row8 >= 4, mixed, 0.0)], axis=0)

    def from_outside(x):
        return jnp.where(c16 == 1, shift(x, 1, 0), shift(x, -1, 0))

    def from_inside(x):
        return jnp.where(c16 == 1, shift(x, -1, 0), shift(x, 1, 0))

    fs_out = harmonic(lat_m, from_outside(lat_m))
    fs_in = harmonic(lat_m, from_inside(lat_e))
    fs_row = harmonic(lat_m, shift(lat_m, -1, 1))
    fs_row_prev = shift(fs_row, 1, 1)
    layer_rows = iota((16, SW), 0)
    fs_ver = jnp.where(layer_rows >= 4, harmonic(ver_m, shift(ver_m, 4, 0)), 0.0)
    fs_ver_prev = shift(fs_ver, -4, 0)
    d_s = jnp.maximum(fs_out + fs_in + fs_row + fs_row_prev + fs_ver + fs_ver_prev + sink_s, FACE_FLOOR)
    w_s = DAMPING / d_s

    def column_form(x, ref):
        x = jnp.where(c16 == 1, shift(x, -1, 0), jnp.where(c16 == 2, shift(x, 1, 0), 0.0))
        for k in range(SW // LN):
            block = jnp.concatenate(
                [x[:, k * LN : (k + 1) * LN], jnp.zeros((LN - 16, LN), F32)], axis=0
            )
            ref[k * LN : (k + 1) * LN, :] = block.T

    def columns(ref, base):
        tile = ref[pl.ds(base + (LN - RO), 8), :]
        return [shift(tile, 114 + 4 * l, 1) for l in range(NL)]

    column_form(fs_in, cf_f)

    def faces(base, sums):
        bf = columns(cf_f, base)
        here, below = pl.ds(base, 8), pl.ds(base + 1, 8)
        vs = [[ver[l, h, here, :] for h in range(2)] for l in range(NL)]
        for l in range(NL):
            a0, a1 = lat[l, 0, here, :], lat[l, 1, here, :]
            ra0, ra1 = shift(a0, -1, 1), shift(a1, -1, 1)
            c0 = harmonic(a0, jnp.where(last_lane, ra1, ra0))
            c1 = jnp.where(last_lane, bf[l], harmonic(a1, ra1))
            fc[l, 0, here, :] = c0
            fc[l, 1, here, :] = c1
            for h, a in ((0, a0), (1, a1)):
                fr[l, h, here, :] = harmonic(a, lat[l, h, below, :])
            if sums is not None:
                sums[0][2 * l] += jnp.where(first_lane, bf[l], c0)
                sums[0][2 * l + 1] += c1
            for h in range(2):
                if l < NL - 1:
                    v = harmonic(vs[l][h], vs[l + 1][h])
                    fv[l, h, here, :] = v
                else:
                    v = snk[h, here, :]
                if sums is not None:
                    sums[1][2 * l + h] += v

    faces(RO - 8, None)
    faces(RO + N, None)

    @pl.loop(0, N // 32)
    def _(a):
        sums = [[zero8] * 8, [zero8] * 8]
        for k in range(4):
            faces(pl.multiple_of(RO + 32 * a + 8 * k, 8), sums)
        rows = pl.ds(pl.multiple_of(a * 8, 8), 8)
        for q in range(8):
            acc_n[rows, q * LN : (q + 1) * LN] = sums[0][q]
            acc[rows, q * LN : (q + 1) * LN] = sums[1][q]

    for c in tile_in2:
        c.wait_recv()
    quarter = devices // 4
    lane_q = iota((quarter, LN), 1)
    power = jnp.zeros((quarter, LN), F32)
    ids = power
    for k in range(4):
        part = tin2[k * quarter : (k + 1) * quarter, :]
        mine = (lane_q >> 5) == k
        power = jnp.where(mine, shift(part, 32 * k, 1), power)
        ids = jnp.where(mine, shift(part, 32 * k - 32, 1), ids)
    ids = ids.astype(jnp.int32)
    powers = [part.astype(F32) for part in pieces(power, 3)]
    sub32 = iota((32, LN), 0)
    for k in range(quarter):
        span = slice(k * LN, (k + 1) * LN)
        one_id = ids[k : k + 1, :]
        dense_a[:, span] = jnp.where(sub32 == (one_id >> 5), 1.0, 0.0).astype(BF16)
        hit = sub32 == (one_id & 31)
        for q in range(3):
            dense_b[q, :, span] = jnp.where(hit, powers[q][k : k + 1, :], 0.0).astype(BF16)
    total = None
    for q in range(3):
        term = lax.dot_general(
            dense_a[...], dense_b[q], (((1,), (1,)), ((), ())), preferred_element_type=F32
        )
        total = term if total is None else total + term
    total = jnp.concatenate([total * (1.0 / 64.0), jnp.zeros((32, LN - 32), F32)], axis=1)
    ts[...] = total
    tst[...] = jnp.concatenate([total, jnp.zeros((LN - 32, LN), F32)], axis=0).T[0:32, :]
    th_in = [
        send(a.at[pl.ds(24 * s, 8)], th.at[2 * q + s], d)
        for q, a in enumerate((ts, tst))
        for s, d in enumerate(((-1, 0), (1, 0)) if q == 0 else ((0, -1), (0, 1)))
    ]
    spread_cols = jnp.where(iota((LN, N), 0) == (iota((LN, N), 1) >> 3), 1.0, 0.0).astype(BF16)
    wide = pick_dot(total, spread_cols)
    for h in range(2):
        dynr[h, 8:40, :] = wide[:, halves[h]]

    @pl.loop(0, N // 32)
    def _(a):
        for k in range(4):
            for h in range(2):
                dyn_out[pl.ds(pl.multiple_of(a * 32 + k * 8, 8), 8), halves[h]] = jnp.broadcast_to(
                    dynr[h, pl.ds(8 + 4 * a + k, 1), :], (8, LN)
                )

    dyn_copy = pltpu.make_async_copy(dyn_out, dyn_hbm, lsem.at[0])
    dyn_copy.start()

    def diagonal(base):
        here, above = pl.ds(base, 8), pl.ds(base - 1, 8)
        bf = columns(cf_f, base)
        for l in range(NL):
            c0, c1 = fc[l, 0, here, :], fc[l, 1, here, :]
            rc0, rc1 = shift(c0, 1, 1), shift(c1, 1, 1)
            west_face = (jnp.where(first_lane, bf[l], rc0), jnp.where(first_lane, rc0, rc1))
            for h, c in ((0, c0), (1, c1)):
                d = fr[l, h, above, :] + fr[l, h, here, :] + west_face[h] + c
                if l > 0:
                    d = d + fv[l - 1, h, here, :]
                if l < NL - 1:
                    d = d + fv[l, h, here, :]
                else:
                    d = d + snk[h, here, :]
                d = jnp.maximum(d, FACE_FLOOR)
                dg[l, h, here, :] = d
                wg[l, h, here, :] = DAMPING / d

    diagonal(RO - 8)
    diagonal(RO + N)

    @pl.loop(0, N // 32)
    def _(a):
        for k in range(4):
            diagonal(pl.multiple_of(RO + 32 * a + 8 * k, 8))

    block_lane = lane8 & 31
    own_block = (block_lane >= 8) & (block_lane < 16)

    def block_rows(x):
        return x.reshape(8, 8, LN).sum(axis=1)

    def edge_sums(start):
        rows = [fr[l, h, pl.ds(start, 8, stride=32), :] for l in range(NL) for h in range(2)]
        return pick_dot(jnp.concatenate(rows, axis=1), cb[...])

    c_east = edge_sums(RO + 31)
    c_east_prev = edge_sums(RO - 1)
    c_north_wide = block_rows(pick_dot(acc_n[...], cbn[...]))
    c_north = jnp.where(own_block, c_north_wide, 0.0)
    c_north_prev = jnp.where(own_block, shift(c_north_wide, 1, 1), 0.0)
    up_sink = block_rows(pick_dot(acc[...], cb[...]))
    c_up = jnp.where(lane8 < 96, up_sink, 0.0)
    c_sink = jnp.where(lane8 >= 96, up_sink, 0.0)
    c_diag = c_east + c_east_prev + c_north + c_north_prev + c_up + shift(c_up, 32, 1) + c_sink
    for q, x in enumerate((c_east, c_north, c_up, c_diag)):
        cm[q] = x
    cm_in = {d: (k, send(cm, cmr.at[k], d)) for k, d in enumerate(DIRS)}

    def sum_along_gx(it, *tiles):
        parts = len(tiles)
        for q, x in enumerate(tiles):
            s1[it, q] = x
        span = pl.ds(0, parts)
        return [send(s1.at[it, span], ls1.at[it, d - 1, span], (d, 0)) for d in range(1, nx)]

    def sum_along_gy(it, arriving, parts):
        span = pl.ds(0, parts)
        total = [s1[it, q] for q in range(parts)]
        for d in range(1, nx):
            arriving[d - 1].wait_recv()
            for q in range(parts):
                total[q] = total[q] + ls1[it, d - 1, q]
        for q in range(parts):
            s2[it, q] = total[q]
        return [send(s2.at[it, span], ls2.at[it, d - 1, span], (0, d)) for d in range(1, ny)]

    def sum_end(it, arriving, parts):
        total = [s2[it, q] for q in range(parts)]
        for d in range(1, ny):
            arriving[d - 1].wait_recv()
            for q in range(parts):
                total[q] = total[q] + ls2[it, d - 1, q]
        return [x.sum(axis=0, keepdims=True).sum(axis=1, keepdims=True) for x in total]

    sums_gx = sum_along_gx(0, source_sum, c_diag)

    def assemble(own, other):
        rows = []
        for dx in (-1, 0, 1):
            centre = own if dx == 0 else other((dx, 0))
            rows.append(centre + shift(other((dx, -1)), -8, 1) + shift(other((dx, 1)), 8, 1))
        return jnp.concatenate(rows, axis=0)

    def couplings():
        for _, c in cm_in.values():
            c.wait_recv()
        w_east, w_north, w_up, w_diag = (
            assemble(cm[q], lambda d, q=q: cmr[cm_in[(-d[0], -d[1])][0], q]) for q in range(4)
        )
        gain = jnp.where((iota((24, LN), 1) & 31) < 24, DAMPING / jnp.maximum(w_diag, 1e-30), 0.0)
        coef[0] = gain
        coef[1] = gain * w_east
        coef[2] = gain * shift(w_east, 1, 0)
        coef[3] = gain * w_north
        coef[4] = gain * shift(w_north, 1, 1)
        coef[5] = gain * w_up
        coef[6] = gain * shift(w_up, 32, 1)

    def couple(ref, base, edge, live):
        here, above, below = pl.ds(base, 8), pl.ds(base - 1, 8), pl.ds(base + 1, 8)
        res = [[None, None] for _ in range(NL)]
        mid = [[ref[l, h, here, :] for h in range(2)] for l in range(live)]
        for l in range(live):
            a0, a1 = mid[l]
            f0, f1 = fc[l, 0, here, :], fc[l, 1, here, :]
            ra0, ra1 = shift(a0, -1, 1), shift(a1, -1, 1)
            p0, p1 = shift(f0 * a0, 1, 1), shift(f1 * a1, 1, 1)
            lateral = (
                f0 * jnp.where(last_lane, ra1, ra0) + jnp.where(first_lane, edge[l], p0),
                jnp.where(last_lane, edge[l], f1 * ra1) + jnp.where(first_lane, p0, p1),
            )
            for h in range(2):
                res[l][h] = (
                    lateral[h]
                    + fr[l, h, above, :] * ref[l, h, above, :]
                    + fr[l, h, here, :] * ref[l, h, below, :]
                )
        for l in range(live):
            for h in range(2):
                for face, to in ((l - 1, l - 1), (l, l + 1)):
                    if 0 <= to < NL:
                        term = fv[face, h, here, :] * mid[l][h]
                        res[to][h] = term if res[to][h] is None else res[to][h] + term
        return mid, res

    def dyn_rows(base, h):
        return dynr[h, pl.ds(base // 8 + 6, 1), :]

    strip_top = layer_rows >= 12
    row16 = iota((16, LN), 0)
    lane16 = iota((16, LN), 1)
    lane24 = iota((24, LN), 1)
    tm = te = source_s = dyn_s = diag_total = None
    sweeps = OUTER * INNER
    for it in range(sweeps):
        first, last = it == 0, it == sweeps - 1
        parts = 2 if first else 1

        def residual(base, sums):
            here = pl.ds(base, 8)
            if first:
                for h in range(2):
                    r = dyn_rows(base, h) + drn[h, here, :]
                    src[h, here, :] = r
                    r_[0, h, here, :] = r
                    e1_[0, h, here, :] = wg[0, h, here, :] * r
                    if sums is not None:
                        sums[h] += r
                return
            mid, res = couple(t_, base, columns(cf_t, base), NL)
            for l in range(NL):
                for h in range(2):
                    r = res[l][h] - dg[l, h, here, :] * mid[l][h]
                    if l == 0:
                        r = r + src[h, here, :]
                    r_[l, h, here, :] = r
                    e1_[l, h, here, :] = wg[l, h, here, :] * r
                    if sums is not None:
                        sums[2 * l + h] += r

        if not first:
            r_s = source_s - (
                d_s * tm
                - fs_out * from_outside(tm)
                - fs_in * from_inside(te)
                - fs_row * shift(tm, -1, 1)
                - fs_row_prev * shift(tm, 1, 1)
                - fs_ver * shift(tm, 4, 0)
                - fs_ver_prev * shift(tm, -4, 0)
            )
            column_form(fs_in * tm, cf_t)
            column_form(fs_in * (w_s * r_s), cf_e)

        @pl.loop(0, N // 32)
        def _(a):
            sums = [zero8] * 8
            for k in range(4):
                residual(pl.multiple_of(RO + 32 * a + 8 * k, 8), sums)
            rows = pl.ds(pl.multiple_of(a * 8, 8), 8)
            for q in range(8):
                acc[rows, q * LN : (q + 1) * LN] = sums[q]

        own_c = block_rows(pick_dot(acc[...], cb[...]))
        ct[it] = own_c
        side = {d: (k, send(ct.at[it], nb.at[it, k], d)) for k, d in enumerate(DIRS)}

        if first:
            for c in th_in:
                c.wait_recv()
            sub8 = iota((8, LN), 0)
            rims = jnp.where(sub8 == 0, th[1, 7:8, :], jnp.where(sub8 == 1, th[0, 0:1, :], 0.0))
            wide_rims = pick_dot(rims, spread_cols)
            for h in range(2):
                dynr[h, 0:8, :] = jnp.broadcast_to(wide_rims[0:1, halves[h]], (8, LN))
                dynr[h, 40:48, :] = jnp.broadcast_to(wide_rims[1:2, halves[h]], (8, LN))
            rims = jnp.where(sub8 == 0, th[3, 7:8, :], jnp.where(sub8 == 1, th[2, 0:1, :], 0.0))
            spread_rows = iota((LN, SW), 0) == ((iota((LN, SW), 1) - LN) >> 3)
            tall_rims = pick_dot(rims, jnp.where(spread_rows, 1.0, 0.0).astype(BF16))
            dyn_s = jnp.where(
                layer_rows == 13, tall_rims[0:1, :], jnp.where(layer_rows == 14, tall_rims[1:2, :], 0.0)
            )
            source_s = dyn_s + drain_s
            column_form(fs_in * (w_s * source_s), cf_e)
        residual(RO - 8, None)
        residual(RO + N, None)

        sums_gy = sum_along_gy(it, sums_gx, parts)

        live = 1 if first else NL

        @pl.loop(0, N // 32)
        def _(a):
            for k in range(4):
                base = pl.multiple_of(RO + 32 * a + 8 * k, 8)
                here = pl.ds(base, 8)
                mid, res = couple(e1_, base, columns(cf_e, base), live)
                tops = []
                for l in range(NL):
                    pair = []
                    for h in range(2):
                        if l < live:
                            u = (1.0 - DAMPING) * mid[l][h] + wg[l, h, here, :] * (r_[l, h, here, :] + res[l][h])
                        elif res[l][h] is not None:
                            u = wg[l, h, here, :] * res[l][h]
                        else:
                            u = zero8
                        if not first:
                            u = u + t_[l, h, here, :]
                        t_[l, h, here, :] = u
                        pair.append(u)
                    tops.append(tuple(pair))
                if not last:
                    pk[pl.ds(pl.multiple_of(32 * a + 8 * k, 8), 8), :] = pack(tops)

        if not last:
            for s, base in enumerate((RO, RO + N - 8)):
                for l in range(NL):
                    for h in range(2):
                        st_row[it, s, l, h] = t_[l, h, base : base + 8, :]
            row_in = [send(st_row.at[it, s], rt_row.at[it, s], (2 * s - 1, 0)) for s in range(2)]
            for k in range(2):
                es[it, :, k * LN : (k + 1) * LN] = pk[k * LN : (k + 1) * LN, :].T[112:128, :]
            we_in = [send(es.at[it], rt_we.at[it, s], (0, 2 * s - 1)) for s in range(2)]
            diag_in = {}
            for k, d in enumerate(DIAG):
                half = 0 if d[0] < 0 else 1
                diag_in[d] = (k, send(es.at[it, :, pl.ds(half * LN, LN)], rt_d.at[it, k], d))

        if first:
            couplings()
        for _, c in side.values():
            c.wait_recv()
        rw = coef[0] * assemble(own_c, lambda d: nb[it, side[(-d[0], -d[1])][0]])
        x = rw
        for _ in range(CJ - 1):
            x = (
                (1.0 - DAMPING) * x + rw
                + coef[1] * shift(x, -1, 0) + coef[2] * shift(x, 1, 0)
                + coef[3] * shift(x, -1, 1) + coef[4] * shift(x, 1, 1)
                + coef[5] * shift(x, -32, 1) + coef[6] * shift(x, 32, 1)
            )
        sums = sum_end(it, sums_gy, parts)
        if first:
            diag_total = sums[1]
        x = x + BALANCE_WEIGHT * sums[0] / diag_total

        for l in range(NL):
            for h in range(2):
                cv[l, h] = jnp.take_along_axis(x, l * 32 + 8 + h * 4 + (lane24 >> 5), axis=1)

        if last:
            writes = []
            for part in range(4):

                @pl.loop(2 * part, 2 * part + 2)
                def _(a):
                    for l in range(NL):
                        for h in range(2):
                            add = cv[l, h, pl.ds(8 + a, 1), :]
                            for k in range(4):
                                rows = pl.ds(pl.multiple_of(32 * a + 8 * k, 8), 8)
                                here = pl.ds(pl.multiple_of(RO + 32 * a + 8 * k, 8), 8)
                                out[l, rows, halves[h]] = t_[l, h, here, :] + add

                span = pl.ds(64 * part, 64)
                writes.append(
                    pltpu.make_async_copy(out.at[:, span, :], out_hbm.at[:, span, :], lsem.at[3 + part])
                )
                writes[-1].start()
            break

        fresh = (it + 1) % INNER == 0

        @pl.loop(0, N // 32, init_carry=zero8)
        def source_sum(a, source_sum):
            for l in range(NL):
                for h in range(2):
                    add = cv[l, h, pl.ds(8 + a, 1), :]
                    for k in range(4):
                        base = pl.multiple_of(RO + 32 * a + 8 * k, 8)
                        here = pl.ds(base, 8)
                        u = t_[l, h, here, :] + add
                        t_[l, h, here, :] = u
                        if l == 0:
                            if fresh:
                                s = dyn_rows(base, h) + drn[h, here, :] * jnp.exp(DRAIN_SLOPE * u)
                                src[h, here, :] = s
                            else:
                                s = src[h, here, :]
                            source_sum = source_sum + s
                        if l == NL - 1:
                            source_sum = source_sum - snk[h, here, :] * u
            return source_sum

        sums_gx = sum_along_gx(it + 1, source_sum)

        xt[...] = jnp.concatenate([x, jnp.zeros((LN - 24, LN), F32)], axis=0).T
        ring = jnp.zeros((16, LN), F32)
        own_v = ring
        for l in range(NL):
            for pair in range(2):
                mine = (row16 >> 1) == 2 * (NL - 1 - l) + pair
                ring = jnp.where(mine, xt[l * 32 + (7, 16)[pair] : l * 32 + (7, 16)[pair] + 1, :], ring)
                own_v = jnp.where(mine, xt[l * 32 + (15, 8)[pair] : l * 32 + (15, 8)[pair] + 1, :], own_v)

        def along(v):
            return jnp.concatenate(
                [jnp.take_along_axis(v, 4 + 4 * k + (lane16 >> 5), axis=1) for k in range(SW // LN)], axis=1
            )

        for c in row_in:
            c.wait_recv()
        for slot, base, at_row in ((1, RO - 8, 7), (0, RO + N, 16)):
            for l in range(NL):
                for h in range(2):
                    u = rt_row[it, slot, l, h] + cv[l, h, at_row : at_row + 1, :]
                    t_[l, h, base : base + 8, :] = u
                    if l == 0 and fresh:
                        src[h, base : base + 8, :] = dyn_rows(base, h) + drn[
                            h, base : base + 8, :
                        ] * jnp.exp(DRAIN_SLOPE * u)
        for c in we_in:
            c.wait_recv()
        for _, c in diag_in.values():
            c.wait_recv()

        def corner(d):
            return rt_d[it, diag_in[(-d[0], -d[1])][0]]

        west = jnp.concatenate([corner((-1, -1)), rt_we[it, 1], corner((1, -1))], axis=1)
        east = jnp.concatenate([corner((-1, 1)), rt_we[it, 0], corner((1, 1))], axis=1)
        tm = jnp.where(c16 < 2, west, east) + along(ring)
        blank = jnp.zeros((16, LN), F32)
        te = jnp.concatenate([blank, es[it], blank], axis=1) + along(own_v)
        if fresh:
            source_s = jnp.where(
                strip_top, dyn_s + drain_s * jnp.exp(DRAIN_SLOPE * jnp.where(strip_top, tm, 0.0)), 0.0
            )

    for c in started:
        c.wait_send()
    dyn_copy.wait()
    for c in writes:
        c.wait()


def hand_over(a, b, to_a, to_b, sem):
    copies = [
        pltpu.make_async_copy(a.at[l], to_a.at[l], sem.at[l]) for l in range(NL)
    ] + [pltpu.make_async_copy(b, to_b, sem.at[NL])]
    for c in copies:
        c.start()
    for c in copies:
        c.wait()


def n_copies(nx, ny):
    setup = (ny - 1) + 2 + 2 + 6 + (nx - 1) + 4 + 8
    each = 8 + (nx - 1) + (ny - 1)
    return setup + OUTER * INNER * each + (OUTER * INNER - 1) * 8


def solution(mesh):
    nx, ny = mesh.shape["gx"], mesh.shape["gy"]
    its = OUTER * INNER
    devices = nx * ny

    def step(material, material_table, sink_cond, drain_current, instance_tile, instance_power):
        n_inst = instance_tile.shape[0]
        field = pltpu.VMEM((NL, 2, NR, LN), F32)
        single = pltpu.VMEM((2, NR, LN), F32)
        vm = lambda *shape: pltpu.VMEM(shape, F32)
        half = lambda *shape: pltpu.VMEM(shape, BF16)
        copies = n_copies(nx, ny)
        scratch = [
            pltpu.VMEM((NL, N, N), jnp.int32), vm(N, N), vm(N, N), vm(NL, N, N), vm(N, N),
            field, field, field, field, pltpu.VMEM((NL - 1, 2, NR, LN), F32), field, field,
            single, single, single, field, field, field,
            vm(SW, LN), vm(SW, LN), vm(SW, LN), vm(64, 8 * LN), vm(64, 8 * LN), vm(N, LN),
            half(8 * LN, LN), half(8 * LN, LN),
            half(devices, n_inst), half(3, 64, n_inst), vm(devices, LN), vm(devices, LN),
            vm(nx, ny, LN), vm(devices, LN), half(32, 32 * devices), half(3, 32, 32 * devices),
            vm(32, LN), vm(32, LN), vm(4, 8, LN), vm(2, 48, LN),
            vm(2, 6, 2, 8, LN), vm(2, 6, 2, 8, LN), vm(24, N), vm(2, 24, N), vm(6, 24, LN),
            vm(4, 8, LN), vm(8, 4, 8, LN), vm(7, 24, LN), vm(its, 8, LN), vm(its, 8, 8, LN),
            vm(its, 2, 8, LN), vm(its, nx - 1, 2, 8, LN), vm(its, 2, 8, LN), vm(its, ny - 1, 2, 8, LN),
            vm(NL, 2, 24, LN), vm(LN, LN),
            vm(its - 1, 2, NL, 2, 8, LN), vm(its - 1, 2, NL, 2, 8, LN),
            vm(its - 1, 16, N), vm(its - 1, 2, 16, N), vm(its - 1, 4, 16, LN),
            pltpu.SemaphoreType.DMA((copies,)), pltpu.SemaphoreType.DMA((copies,)), pltpu.SemaphoreType.DMA((7,)),
        ]
        vmem = pl.BlockSpec(memory_space=pltpu.VMEM)
        smem = pl.BlockSpec(memory_space=pltpu.SMEM)
        hbm = pl.BlockSpec(memory_space=pl.ANY)
        shapes = (jax.ShapeDtypeStruct((NL, N, N), F32), jax.ShapeDtypeStruct((N, N), F32))
        results = pl.pallas_call(
            functools.partial(kernel, nx, ny),
            out_shape=shapes,
            in_specs=[hbm, smem, hbm, hbm, vmem, vmem],
            out_specs=(hbm, hbm),
            scratch_shapes=scratch,
            compiler_params=pltpu.CompilerParams(
                collective_id=0, has_side_effects=True, vmem_limit_bytes=56 * 1024 * 1024
            ),
        )(
            material,
            material_table,
            sink_cond,
            drain_current,
            instance_tile.reshape(n_inst // LN, LN),
            instance_power.reshape(n_inst // LN, LN),
        )
        return pl.pallas_call(
            hand_over,
            out_shape=shapes,
            in_specs=[vmem, vmem],
            out_specs=(hbm, hbm),
            scratch_shapes=[pltpu.SemaphoreType.DMA((NL + 1,))],
        )(*results)

    return jax.shard_map(
        step,
        mesh=mesh,
        in_specs=(
            P(None, "gx", "gy"),
            P(),
            P("gx", "gy"),
            P("gx", "gy"),
            P(("gx", "gy")),
            P(("gx", "gy")),
        ),
        out_specs=(P(None, "gx", "gy"), P("gx", "gy")),
        check_vma=False,
    )
```

```python
import functools

import jax
import jax.numpy as jnp
from jax import lax
from jax.experimental import pallas as pl
from jax.experimental.pallas import tpu as pltpu
from jax.sharding import PartitionSpec as P

MESH = pl.DeviceIdType.MESH
F32 = jnp.float32
BF16 = jnp.bfloat16

NL = 4
N = 256
LN = 128
RO = 16
NR = N + 2 * RO
NQ = 6
SL = 384
SO = 64
OUTER = 2
INNER = 2
CJ = 8
DAMPING = 0.8
DRAIN_SLOPE = 0.5
FACE_FLOOR = 0.5
BALANCE_WEIGHT = 0.5
DIRS = ((-1, -1), (-1, 0), (-1, 1), (0, -1), (0, 1), (1, -1), (1, 0), (1, 1))
DIAG = tuple(d for d in DIRS if d[0] and d[1])
OFF_LINE = tuple(d for d in DIRS if d[1])


def iota(shape, dim):
    return lax.broadcasted_iota(jnp.int32, shape, dim)


def harmonic(a, b):
    return 2.0 * a * b / jnp.maximum(a + b, FACE_FLOOR)


def shift(x, amount, axis):
    return pltpu.roll(x, amount % x.shape[axis], axis)


def lookup(ids, table):
    level = list(table)
    for bit in range(4):
        odd = ((ids >> bit) & 1) == 1
        level = [jnp.where(odd, level[2 * k + 1], level[2 * k]) for k in range(len(level) // 2)]
    return level[0]


def exact_dot(a, b):
    return lax.dot_general(
        a, b, (((1,), (0,)), ((), ())), precision=lax.Precision.HIGHEST, preferred_element_type=F32
    )


def pieces(x, count):
    out = []
    for _ in range(count - 1):
        part = x.astype(BF16)
        out.append(part)
        x = x - part.astype(F32)
    return out + [x.astype(BF16)]


def pick_dot(x, ones):
    return sum(jnp.dot(part, ones, preferred_element_type=F32) for part in pieces(x, 3))


class Layout:
    def __init__(self):
        self.count = 0

    def take(self):
        self.count += 1
        return self.count - 1


def kernel(nx, ny, *refs):
    (mat_hbm, tab, sink_hbm, drain_hbm, inst_tile, inst_power, out_hbm, dyn_hbm) = refs[:8]
    (
        mat, sink, drain, out, dyn_out,
        lat, ver, fr, fc, fl, fv, dg, wg, src, drn, snk, t_, r_, e1_,
        cf_t, cf_e, cf_f, acc, acc_n, pk, cb, cbn,
        dest, slots, sout, tin1, tred, tin2, dense_a, dense_b, ts, th, dynr,
        sq_row, rq_row, sq_c, rq_c, sq_s, rq_s,
        fcs, frs, fvs, dgs, wgs, drn_s, dys, srs,
        cm, cmr, coef, ct, nb, s1, ls1, s2, ls2, cv, cvr, cvl, xt,
        ssem, rsem, lsem,
    ) = refs[8:]
    mx, my = lax.axis_index("gx"), lax.axis_index("gy")

    def at(dx, dy):
        return {"gx": lax.rem(mx + (dx + nx), nx), "gy": lax.rem(my + (dy + ny), ny)}

    partners = [(d, 0) for d in range(1, nx)] + [(0, d) for d in range(1, ny)] + list(DIAG)
    barrier = pltpu.get_barrier_semaphore()
    for d in partners:
        pl.semaphore_signal(barrier, inc=1, device_id=at(*d), device_id_type=MESH)

    fetch = [
        pltpu.make_async_copy(a, b, lsem.at[k])
        for k, (a, b) in enumerate(((mat_hbm, mat), (sink_hbm, sink), (drain_hbm, drain)))
    ]
    for c in fetch:
        c.start()

    numbers = Layout()
    started = []

    def send(a, b, to):
        k = numbers.take()
        copy = pltpu.make_async_remote_copy(
            src_ref=a, dst_ref=b, send_sem=ssem.at[k], recv_sem=rsem.at[k],
            device_id=at(*to), device_id_type=MESH,
        )
        copy.start()
        started.append(copy)
        return copy

    lane8 = iota((8, LN), 1)
    first_lane = lane8 == 0
    last_lane = lane8 == LN - 1
    low_half = lane8 < LN // 2

    devices = nx * ny
    chunks = inst_tile.shape[0]
    sub_d = iota((devices, LN), 0)
    lane_d = iota((devices, LN), 1)
    up_to = jnp.where(iota((LN, LN), 0) <= iota((LN, LN), 1), 1.0, 0.0).astype(BF16)
    for k in range(chunks):
        s = inst_tile[k : k + 1, :] >> 10
        owner = (s % ny) * nx + s // ny
        dest[:, k * LN : (k + 1) * LN] = jnp.where(sub_d == owner, 1.0, 0.0).astype(BF16)
    before = jnp.zeros((devices, 1), F32)
    slot_row = iota((64, LN), 0)
    for k in range(chunks):
        span = slice(k * LN, (k + 1) * LN)
        d = dest[:, span]
        within = jnp.dot(d, up_to, preferred_element_type=F32)
        rank = jnp.sum(d.astype(F32) * (within + before), axis=0, keepdims=True)
        before = before + within[:, LN - 1 : LN]
        at_slot = (slot_row & 31) == rank.astype(jnp.int32) - 1
        t = inst_tile[k : k + 1, :]
        ids = ((t & 992).astype(F32), (t & 31).astype(F32), jnp.zeros((1, LN), F32))
        for q, part in enumerate(pieces(inst_power[k : k + 1, :], 3)):
            value = jnp.where(slot_row < 32, part.astype(F32), ids[q])
            slots[q, :, span] = jnp.where(at_slot, value, 0.0).astype(BF16)
    total = None
    for q in range(3):
        term = lax.dot_general(
            dest[...], slots[q], (((1,), (1,)), ((), ())), preferred_element_type=F32
        )
        total = term if total is None else total + term
    sout[...] = jnp.concatenate([total, jnp.zeros((devices, LN - 64), F32)], axis=1)
    power_sum = jnp.zeros((8, LN), F32)
    for k in range(chunks // 8):
        power_sum = power_sum + inst_power[8 * k : 8 * k + 8, :]

    def bundle(j):
        return sout.at[pl.ds(pl.multiple_of(j * nx, nx), nx), :]

    pl.semaphore_wait(barrier, len(partners))
    tile_in = []
    for d in range(1, ny):
        tile_in.append(send(bundle(lax.rem(my + d, ny)), tin1.at[pl.ds(d * nx, nx)], (0, d)))
    tin1[0:nx, :] = bundle(my)[...]

    def pack(values):
        packed = jnp.zeros((8, LN), F32)
        for q, (a, b) in enumerate(values):
            both = shift(jnp.where(low_half, a, b), 16 * q + 8, 1)
            packed = jnp.where((lane8 >> 4) == q, both, packed)
        return packed

    halves = (slice(0, LN), slice(LN, N))

    def raw(rows):
        mats = [tuple(mat[l, rows, h].astype(F32) for h in halves) for l in range(NL)]
        return mats + [tuple(a[rows, h] for h in halves) for a in (sink, drain)]

    for c in fetch:
        c.wait()
    for side, rows in enumerate((slice(0, 8), slice(N - 8, N))):
        values = raw(rows)
        for q, (a, b) in enumerate(values):
            sq_row[side, q, 0] = a
            sq_row[side, q, 1] = b
        sq_c[side] = pack(values)
    margin_row = [send(sq_row.at[s], rq_row.at[s], (2 * s - 1, 0)) for s in range(2)]
    corner_dirs = ((-1, 0), (1, 0)) + DIAG
    margin_c = {
        d: (k, send(sq_c.at[0 if d[0] < 0 else 1], rq_c.at[k], d)) for k, d in enumerate(corner_dirs)
    }

    @pl.loop(0, N // 32)
    def _(a):
        for k in range(4):
            rows = pl.ds(pl.multiple_of(a * 32 + k * 8, 8), 8)
            pk[pl.ds(pl.multiple_of(a * 32 + k * 8 + SO, 8), 8), :] = pack(raw(rows))

    pk[0:SO, :] = jnp.zeros((SO, LN), F32)
    pk[SO + N :, :] = jnp.zeros((SL - N - SO, LN), F32)
    for k in range(SL // LN):
        span = slice(k * LN, (k + 1) * LN)
        block = pk[span, :].T
        for q in range(NQ):
            sq_s[0, 8 * q : 8 * q + 8, span] = block[16 * q + 8 : 16 * q + 16, :]
            sq_s[1, 8 * q : 8 * q + 8, span] = block[16 * q : 16 * q + 8, :]
    margin_we = [send(sq_s.at[s], rq_s.at[s], (0, 2 * s - 1)) for s in range(2)]

    col_n = iota((LN, LN), 1)
    row_n = iota((LN, LN), 0)
    for l in range(NL):
        for h in range(2):
            span = pl.ds((2 * l + h) * LN, LN)
            goal = l * 32 + 8 + h * 4 + (row_n >> 5)
            cb[span, :] = jnp.where(col_n == goal, 1.0, 0.0).astype(BF16)
            hit = ((row_n & 31) == 31) & (col_n == goal)
            if h == 0:
                hit = hit | ((row_n == 0) & (col_n == l * 32 + 7))
            cbn[span, :] = jnp.where(hit, 1.0, 0.0).astype(BF16)
    table = [[tab[q, k] for k in range(16)] for q in range(2)]

    zero8 = jnp.zeros((8, LN), F32)
    for ref, places in ((t_, (0, NR - 8)), (e1_, (0, NR - 8)), (fr, (0,)), (lat, (NR - 8,))):
        for l in range(NL):
            for h in range(2):
                for place in places:
                    ref[l, h, place : place + 8, :] = zero8

    @pl.loop(0, N // 8, init_carry=power_sum)
    def source_sum(k, source_sum):
        rows = pl.ds(pl.multiple_of(k * 8, 8), 8)
        into = pl.ds(pl.multiple_of(k * 8 + RO, 8), 8)
        for h in range(2):
            for l in range(NL):
                ids = mat[l, rows, halves[h]]
                lat[l, h, into, :] = lookup(ids, table[0])
                ver[l, h, into, :] = lookup(ids, table[1])
            snk[h, into, :] = sink[rows, halves[h]]
            d = drain[rows, halves[h]]
            drn[h, into, :] = d
            source_sum = source_sum + d
        return source_sum

    for c in tile_in:
        c.wait_recv()
    for x in range(nx):
        tred[x] = tin1[pl.ds(x, ny, stride=nx), :]
    tile_in2 = []
    for d in range(1, nx):
        x = lax.rem(mx + d, nx)
        tile_in2.append(send(tred.at[x], tin2.at[pl.ds(d * ny, ny)], (d, 0)))
    tin2[0:ny, :] = tred[mx]

    edge_n = jnp.where(mx == 0, 0.0, 1.0)
    edge_s = jnp.where(mx == nx - 1, 0.0, 1.0)
    edge_w = jnp.where(my == 0, 0.0, 1.0)
    edge_e = jnp.where(my == ny - 1, 0.0, 1.0)
    for c in margin_row:
        c.wait_recv()
    for slot, base, keep in ((1, RO - 8, edge_n), (0, RO + N, edge_s)):
        rows = slice(base, base + 8)
        for h in range(2):
            for l in range(NL):
                ids = rq_row[slot, l, h].astype(jnp.int32)
                lat[l, h, rows, :] = lookup(ids, table[0]) * keep
                ver[l, h, rows, :] = lookup(ids, table[1]) * keep
            snk[h, rows, :] = rq_row[slot, 4, h] * keep
            drn[h, rows, :] = rq_row[slot, 5, h] * keep
    for c in margin_we:
        c.wait_recv()
    for _, c in margin_c.values():
        c.wait_recv()

    def corner_block(dy):
        top, low = (rq_c[margin_c[(-dx, -dy)][0]] for dx in (-1, 1))
        pad = jnp.zeros((SO - 8, LN), F32)
        return jnp.concatenate([pad, top, low, pad], axis=0).T

    blocks = {dy: corner_block(dy) for dy in (-1, 0, 1)}

    def merge(body, corners):
        return jnp.concatenate(
            [
                jnp.where((lane8 >> 3) == SO // 8 - 1, corners, body[:, :LN]),
                body[:, LN : 2 * LN],
                jnp.where((lane8 >> 3) == SO // 8, corners, body[:, 2 * LN :]),
            ],
            axis=1,
        )

    def raw_strip(q, side):
        own, got = slice(8 * q, 8 * q + 8), slice(16 * q, 16 * q + 16)
        if side == 0:
            outside = merge(rq_s[1, own, :], blocks[-1][got, :][0:8, :])
            inside = merge(sq_s[0, own, :], blocks[0][got, :][8:16, :])
            return jnp.concatenate([outside, inside], axis=0)
        outside = merge(rq_s[0, own, :], blocks[1][got, :][8:16, :])
        inside = merge(sq_s[1, own, :], blocks[0][got, :][0:8, :])
        return jnp.concatenate([inside, outside], axis=0)

    sl_lane = iota((16, SL), 1)
    sl_row = iota((16, SL), 0)
    one = jnp.ones((16, SL), F32)
    keep_rows = jnp.where(sl_lane < SO, one * edge_n, jnp.where(sl_lane >= SO + N, one * edge_s, one))
    keep = (
        keep_rows * jnp.where(sl_row < 8, one * edge_w, one),
        keep_rows * jnp.where(sl_row >= 8, one * edge_e, one),
    )
    sides = range(2)
    for g in sides:
        lats, vers = [], []
        for l in range(NL):
            ids = raw_strip(l, g).astype(jnp.int32)
            lats.append(lookup(ids, table[0]) * keep[g])
            vers.append(lookup(ids, table[1]) * keep[g])
        sink_s = raw_strip(4, g) * keep[g]
        drn_s[g] = raw_strip(5, g) * keep[g]
        up = None
        for l in range(NL):
            c = harmonic(lats[l], shift(lats[l], -1, 0))
            r = harmonic(lats[l], shift(lats[l], -1, 1))
            fcs[l, g] = c
            frs[l, g] = r
            d = c + shift(c, 1, 0) + r + shift(r, 1, 1)
            if l > 0:
                d = d + up
            if l < NL - 1:
                up = harmonic(vers[l], vers[l + 1])
                fvs[l, g] = up
                d = d + up
            else:
                d = d + sink_s
            d = jnp.maximum(d, FACE_FLOOR)
            dgs[l, g] = d
            wgs[l, g] = DAMPING / d

    row_z = iota((8, SL), 0)

    def column_form(west, east, ref):
        z = jnp.zeros((8, SL), F32)
        for l in range(NL):
            z = jnp.where(row_z == 2 * l + 1, west[l], jnp.where(row_z == 2 * l, east[l], z))
        for k in range(SL // LN):
            block = jnp.concatenate([z[:, k * LN : (k + 1) * LN], jnp.zeros((LN - 8, LN), F32)], axis=0)
            ref[k * LN : (k + 1) * LN, :] = block.T

    def columns(ref, base):
        tile = ref[pl.ds(base + (SO - RO), 8), :]
        return [shift(tile, -(2 * l + 1), 1) for l in range(NL)]

    def edge_terms(v, ref):
        column_form(
            [(fcs[l, 0] * v[l][0])[7:8, :] for l in range(NL)],
            [fcs[l, 1][7:8, :] * v[l][1][8:9, :] for l in range(NL)],
            ref,
        )

    column_form([fcs[l, 0, 7:8, :] for l in range(NL)], [fcs[l, 1, 7:8, :] for l in range(NL)], cf_f)

    def faces(base, sums):
        bf = columns(cf_f, base)
        here, below = pl.ds(base, 8), pl.ds(base + 1, 8)
        vs = [[ver[l, h, here, :] for h in range(2)] for l in range(NL)]
        for l in range(NL):
            a0, a1 = lat[l, 0, here, :], lat[l, 1, here, :]
            ra0, ra1 = shift(a0, -1, 1), shift(a1, -1, 1)
            c0 = harmonic(a0, jnp.where(last_lane, ra1, ra0))
            c1 = jnp.where(last_lane, bf[l], harmonic(a1, ra1))
            rc0, rc1 = shift(c0, 1, 1), shift(c1, 1, 1)
            fc[l, 0, here, :] = c0
            fc[l, 1, here, :] = c1
            fl[l, 0, here, :] = jnp.where(first_lane, bf[l], rc0)
            fl[l, 1, here, :] = jnp.where(first_lane, rc0, rc1)
            for h, a in ((0, a0), (1, a1)):
                fr[l, h, here, :] = harmonic(a, lat[l, h, below, :])
            if sums is not None:
                sums[0][2 * l] += jnp.where(first_lane, bf[l], c0)
                sums[0][2 * l + 1] += c1
            for h in range(2):
                if l < NL - 1:
                    v = harmonic(vs[l][h], vs[l + 1][h])
                    fv[l, h, here, :] = v
                else:
                    v = snk[h, here, :]
                if sums is not None:
                    sums[1][2 * l + h] += v

    faces(RO - 8, None)
    faces(RO + N, None)

    @pl.loop(0, N // 32)
    def _(a):
        sums = [[zero8] * 8, [zero8] * 8]
        for k in range(4):
            faces(pl.multiple_of(RO + 32 * a + 8 * k, 8), sums)
        rows = pl.ds(pl.multiple_of(a * 8, 8), 8)
        for q in range(8):
            acc_n[rows, q * LN : (q + 1) * LN] = sums[0][q]
            acc[rows, q * LN : (q + 1) * LN] = sums[1][q]

    block_lane = lane8 & 31
    own_block = (block_lane >= 8) & (block_lane < 16)

    def block_rows(x):
        return x.reshape(8, 8, LN).sum(axis=1)

    def edge_sums(start):
        rows = [fr[l, h, pl.ds(start, 8, stride=32), :] for l in range(NL) for h in range(2)]
        return pick_dot(jnp.concatenate(rows, axis=1), cb[...])

    c_east = edge_sums(RO + 31)
    c_east_prev = edge_sums(RO - 1)
    c_north_wide = block_rows(pick_dot(acc_n[...], cbn[...]))
    c_north = jnp.where(own_block, c_north_wide, 0.0)
    c_north_prev = jnp.where(own_block, shift(c_north_wide, 1, 1), 0.0)
    up_sink = block_rows(pick_dot(acc[...], cb[...]))
    c_up = jnp.where(lane8 < 96, up_sink, 0.0)
    c_sink = jnp.where(lane8 >= 96, up_sink, 0.0)
    c_diag = c_east + c_east_prev + c_north + c_north_prev + c_up + shift(c_up, 32, 1) + c_sink
    for q, x in enumerate((c_east, c_north, c_up, c_diag, c_sink)):
        cm[q] = x
    cm_in = {d: (k, send(cm, cmr.at[k], d)) for k, d in enumerate(DIRS)}

    def sum_along_gx(it, *tiles):
        parts = len(tiles)
        for q, x in enumerate(tiles):
            s1[it, q] = x
        span = pl.ds(0, parts)
        return [send(s1.at[it, span], ls1.at[it, d - 1, span], (d, 0)) for d in range(1, nx)]

    def sum_along_gy(it, arriving, parts):
        span = pl.ds(0, parts)
        total = [s1[it, q] for q in range(parts)]
        for d in range(1, nx):
            arriving[d - 1].wait_recv()
            for q in range(parts):
                total[q] = total[q] + ls1[it, d - 1, q]
        for q in range(parts):
            s2[it, q] = total[q]
        return [send(s2.at[it, span], ls2.at[it, d - 1, span], (0, d)) for d in range(1, ny)]

    def sum_end(it, arriving, parts):
        total = [s2[it, q] for q in range(parts)]
        for d in range(1, ny):
            arriving[d - 1].wait_recv()
            for q in range(parts):
                total[q] = total[q] + ls2[it, d - 1, q]
        return [x.sum(axis=0, keepdims=True).sum(axis=1, keepdims=True) for x in total]

    sums_gx = sum_along_gx(0, source_sum, c_diag, c_sink)

    def diagonal(base):
        here, above = pl.ds(base, 8), pl.ds(base - 1, 8)
        for l in range(NL):
            for h in range(2):
                d = fr[l, h, above, :] + fr[l, h, here, :] + fl[l, h, here, :] + fc[l, h, here, :]
                if l > 0:
                    d = d + fv[l - 1, h, here, :]
                if l < NL - 1:
                    d = d + fv[l, h, here, :]
                else:
                    d = d + snk[h, here, :]
                d = jnp.maximum(d, FACE_FLOOR)
                dg[l, h, here, :] = d
                wg[l, h, here, :] = DAMPING / d

    diagonal(RO - 8)
    diagonal(RO + N)

    @pl.loop(0, N // 32)
    def _(a):
        for k in range(4):
            diagonal(pl.multiple_of(RO + 32 * a + 8 * k, 8))

    for c in tile_in2:
        c.wait_recv()
    quarter = devices // 4
    lane_q = iota((quarter, LN), 1)
    power = jnp.zeros((quarter, LN), F32)
    ids = power
    for k in range(4):
        part = tin2[k * quarter : (k + 1) * quarter, :]
        mine = (lane_q >> 5) == k
        power = jnp.where(mine, shift(part, 32 * k, 1), power)
        ids = jnp.where(mine, shift(part, 32 * k - 32, 1), ids)
    ids = ids.astype(jnp.int32)
    powers = [part.astype(F32) for part in pieces(power, 3)]
    sub32 = iota((32, LN), 0)
    for k in range(quarter):
        span = slice(k * LN, (k + 1) * LN)
        one_id = ids[k : k + 1, :]
        dense_a[:, span] = jnp.where(sub32 == (one_id >> 5), 1.0, 0.0).astype(BF16)
        hit = sub32 == (one_id & 31)
        for q in range(3):
            dense_b[q, :, span] = jnp.where(hit, powers[q][k : k + 1, :], 0.0).astype(BF16)
    total = None
    for q in range(3):
        term = lax.dot_general(
            dense_a[...], dense_b[q], (((1,), (1,)), ((), ())), preferred_element_type=F32
        )
        total = term if total is None else total + term
    total = jnp.concatenate([total * (1.0 / 64.0), jnp.zeros((32, LN - 32), F32)], axis=1)
    total_t = jnp.concatenate([total, jnp.zeros((LN - 32, LN), F32)], axis=0).T
    sub8 = iota((8, LN), 0)

    def stack(*rows):
        out8 = zero8
        for k, x in enumerate(rows):
            out8 = jnp.where(sub8 == k, x, out8)
        return out8

    ts[...] = stack(total_t[0:1, :], total_t[31:32, :], total[0:1, :], total[31:32, :])
    th_in = {d: (k, send(ts, th.at[k], d)) for k, d in enumerate(DIRS)}
    spread_cols = jnp.where(iota((LN, N), 0) == (iota((LN, N), 1) >> 3), 1.0, 0.0).astype(BF16)
    wide = pick_dot(total, spread_cols)
    for h in range(2):
        dynr[h, 8:40, :] = wide[:, halves[h]]

    def couple(ref, base, edge, live):
        here, above, below = pl.ds(base, 8), pl.ds(base - 1, 8), pl.ds(base + 1, 8)
        res = [[None, None] for _ in range(NL)]
        mid = [[ref[l, h, here, :] for h in range(2)] for l in range(live)]
        for l in range(live):
            a0, a1 = mid[l]
            f0, f1 = fc[l, 0, here, :], fc[l, 1, here, :]
            ra0, ra1 = shift(a0, -1, 1), shift(a1, -1, 1)
            p0, p1 = shift(f0 * a0, 1, 1), shift(f1 * a1, 1, 1)
            lateral = (
                f0 * jnp.where(last_lane, ra1, ra0) + jnp.where(first_lane, edge[l], p0),
                jnp.where(last_lane, edge[l], f1 * ra1) + jnp.where(first_lane, p0, p1),
            )
            for h in range(2):
                res[l][h] = (
                    lateral[h]
                    + fr[l, h, above, :] * ref[l, h, above, :]
                    + fr[l, h, here, :] * ref[l, h, below, :]
                )
        for l in range(live):
            for h in range(2):
                for face, to in ((l - 1, l - 1), (l, l + 1)):
                    if 0 <= to < NL:
                        term = fv[face, h, here, :] * mid[l][h]
                        res[to][h] = term if res[to][h] is None else res[to][h] + term
        return mid, res

    def strip_couple(v, g, live):
        res = []
        for l in range(live):
            p, r = fcs[l, g] * v[l], frs[l, g]
            res.append(
                fcs[l, g] * shift(v[l], -1, 0) + shift(p, 1, 0) + r * shift(v[l], -1, 1) + shift(r * v[l], 1, 1)
            )
        res += [None] * (NL - live)
        for l in range(live):
            for face, to in ((l - 1, l - 1), (l, l + 1)):
                if 0 <= to < NL:
                    term = fvs[face, g] * v[l]
                    res[to] = term if res[to] is None else res[to] + term
        return res

    def dyn_rows(base, h):
        return dynr[h, pl.ds(base // 8 + 6, 1), :]

    def over_rows(body, margins=True, carry=None):
        if margins:
            body(RO - 8, None, -1, 3)
            body(RO + N, None, 8, 0)

        @pl.loop(0, N // 32)
        def _(a):
            sums = [zero8] * 8
            for k in range(4):
                body(pl.multiple_of(RO + 32 * a + 8 * k, 8), sums, a, k)
            rows = pl.ds(pl.multiple_of(a * 8, 8), 8)
            for q in range(8):
                if sums[q] is not zero8:
                    acc[rows, q * LN : (q + 1) * LN] = sums[q]

    lane16 = iota((16, LN), 1)
    lane24 = iota((24, LN), 1)

    def sweep_neighbours(x):
        return (
            coef[1] * shift(x, -1, 0) + coef[2] * shift(x, 1, 0)
            + coef[3] * shift(x, -1, 1) + coef[4] * shift(x, 1, 1)
            + coef[5] * shift(x, -32, 1) + coef[6] * shift(x, 32, 1)
        )

    def coarse_sweeps(right):
        rw = coef[0] * right
        x = rw
        for _ in range(CJ - 1):
            x = (1.0 - DAMPING) * x + rw + sweep_neighbours(x)
        return x

    def assemble(own, other):
        rows = []
        for dx in (-1, 0, 1):
            centre = own if dx == 0 else other((dx, 0))
            rows.append(centre + shift(other((dx, -1)), -8, 1) + shift(other((dx, 1)), 8, 1))
        return jnp.concatenate(rows, axis=0)

    def send_coarse(it, own):
        ct[it] = own
        return {d: (k, send(ct.at[it], nb.at[it, k], d)) for k, d in enumerate(DIRS)}

    def first_residual(base, sums, a, k):
        here = pl.ds(base, 8)
        for h in range(2):
            r = dyn_rows(base, h) + drn[h, here, :]
            src[h, here, :] = r
            r_[0, h, here, :] = r
            e1_[0, h, here, :] = wg[0, h, here, :] * r
            if sums is not None:
                sums[h] += r

    over_rows(first_residual, margins=False)
    own_c = block_rows(pick_dot(acc[:, 0 : 2 * LN], cb[0 : 2 * LN, :]))
    side = send_coarse(0, own_c)
    sums_gy = sum_along_gy(0, sums_gx, 3)

    @pl.loop(0, N // 32)
    def _(a):
        for k in range(4):
            for h in range(2):
                dyn_out[pl.ds(pl.multiple_of(a * 32 + k * 8, 8), 8), halves[h]] = jnp.broadcast_to(
                    dynr[h, pl.ds(8 + 4 * a + k, 1), :], (8, LN)
                )

    dyn_copy = pltpu.make_async_copy(dyn_out, dyn_hbm, lsem.at[0])
    dyn_copy.start()
    for _, c in th_in.values():
        c.wait_recv()

    def rim(d, k):
        return th[th_in[(-d[0], -d[1])][0], k : k + 1, :]

    wide_rims = pick_dot(stack(rim((-1, 0), 3) * edge_n, rim((1, 0), 2) * edge_s), spread_cols)
    for h in range(2):
        dynr[h, 0:8, :] = jnp.broadcast_to(wide_rims[0:1, halves[h]], (8, LN))
        dynr[h, 40:48, :] = jnp.broadcast_to(wide_rims[1:2, halves[h]], (8, LN))
    body = stack(rim((0, -1), 1), ts[0:1, :], ts[1:2, :], rim((0, 1), 0))
    top = stack(rim((-1, -1), 1), rim((-1, 0), 0), rim((-1, 0), 1), rim((-1, 1), 0))
    low = stack(rim((1, -1), 1), rim((1, 0), 0), rim((1, 0), 1), rim((1, 1), 0))
    tall = jnp.where(
        lane8 == 0,
        shift(top, -31, 1),
        jnp.where(lane8 == 33, shift(low, 33, 1), jnp.where(lane8 < 33, shift(body, 1, 1), 0.0)),
    )
    spread_rows = jnp.where(iota((LN, SL), 0) == ((iota((LN, SL), 1) - (SO - 8)) >> 3), 1.0, 0.0).astype(BF16)
    tall = pick_dot(tall, spread_rows)
    for g in sides:
        dyn_s = jnp.where(sl_row < 8, tall[2 * g : 2 * g + 1, :], tall[2 * g + 1 : 2 * g + 2, :]) * keep[g]
        dys[g] = dyn_s
        srs[g] = dyn_s + drn_s[g]
    first_residual(RO - 8, None, -1, 3)
    first_residual(RO + N, None, 8, 0)

    rs = [[srs[g] for g in sides]]
    e1s = [[wgs[0, g] * srs[g] for g in sides]]
    live = 1
    zeros_s = jnp.zeros((16, SL), F32)
    edge_terms(e1s + [[zeros_s, zeros_s]] * (NL - 1), cf_e)

    ts_old = None
    balance = diag_total = sink_total = adjoint = None
    sweeps = OUTER * INNER
    for it in range(sweeps):
        first, last = it == 0, it == sweeps - 1
        fresh = (it + 1) % INNER == 0

        def second_sweep(base, sums, a, k):
            here = pl.ds(base, 8)
            mid, res = couple(e1_, base, columns(cf_e, base), live)
            for l in range(NL):
                for h in range(2):
                    if l < live:
                        u = (1.0 - DAMPING) * mid[l][h] + wg[l, h, here, :] * (r_[l, h, here, :] + res[l][h])
                    elif res[l][h] is not None:
                        u = wg[l, h, here, :] * res[l][h]
                    else:
                        u = zero8
                    if not first:
                        u = u + t_[l, h, here, :]
                    t_[l, h, here, :] = u

        over_rows(second_sweep, margins=not last)

        if not last:
            us = [[None, None] for _ in range(NL)]
            for g in sides:
                res = strip_couple([e1s[l][g] for l in range(live)], g, live)
                for l in range(NL):
                    if l < live:
                        u = (1.0 - DAMPING) * e1s[l][g] + wgs[l, g] * (rs[l][g] + res[l])
                    elif res[l] is not None:
                        u = wgs[l, g] * res[l]
                    else:
                        u = zeros_s
                    us[l][g] = u if first else ts_old[l][g] + u
            edge_terms(us, cf_t)

            def half_residual(base, sums, a, k):
                here = pl.ds(base, 8)
                mid, res = couple(t_, base, columns(cf_t, base), NL)
                for l in range(NL):
                    for h in range(2):
                        r = res[l][h] - dg[l, h, here, :] * mid[l][h]
                        if l == 0 and not fresh:
                            r = r + src[h, here, :]
                        r_[l, h, here, :] = r
                        if sums is not None:
                            sums[2 * l + h] += r

            over_rows(half_residual)
            next_c = block_rows(pick_dot(acc[...], cb[...]))

        if first:
            for _, c in cm_in.values():
                c.wait_recv()
            w_east, w_north, w_up, w_diag, w_sink = (
                assemble(cm[q], lambda d, q=q: cmr[cm_in[(-d[0], -d[1])][0], q]) for q in range(5)
            )
            gain = jnp.where((lane24 & 31) < 24, DAMPING / jnp.maximum(w_diag, 1e-30), 0.0)
            coef[0] = gain
            coef[1] = gain * w_east
            coef[2] = gain * shift(w_east, 1, 0)
            coef[3] = gain * w_north
            coef[4] = gain * shift(w_north, 1, 1)
            coef[5] = gain * w_up
            coef[6] = gain * shift(w_up, 32, 1)
            adjoint = jnp.where(own_block, coarse_sweeps(w_sink)[8:16, :], 0.0)
        if not last and not fresh:
            next_gx = sum_along_gx(it + 1, next_c - adjoint * own_c)

        for _, c in side.values():
            c.wait_recv()
        x = coarse_sweeps(assemble(own_c, lambda d: nb[it, side[(-d[0], -d[1])][0]]))
        sums = sum_end(it, sums_gy, 3 if first else 1)
        if first:
            diag_total, sink_total = sums[1], sums[2]
        total = sums[0]
        if not first and it % INNER != 0:
            total = total - balance * sink_total
        balance = BALANCE_WEIGHT * total / diag_total
        x = x + balance

        for l in range(NL):
            for h in range(2):
                at_col = l * 32 + 8 + h * 4
                cv[l, h] = jnp.take_along_axis(x, at_col + (lane24 >> 5), axis=1)
                if not last:
                    cvr[l, h] = jnp.take_along_axis(x, at_col + ((lane24 + 1) >> 5), axis=1)
                    cvl[l, h] = jnp.take_along_axis(x, at_col + ((lane24 - 1) >> 5), axis=1)

        if last:
            writes = []
            for part in range(4):

                @pl.loop(2 * part, 2 * part + 2)
                def _(a):
                    for l in range(NL):
                        for h in range(2):
                            add = cv[l, h, pl.ds(8 + a, 1), :]
                            for k in range(4):
                                rows = pl.ds(pl.multiple_of(32 * a + 8 * k, 8), 8)
                                here = pl.ds(pl.multiple_of(RO + 32 * a + 8 * k, 8), 8)
                                out[l, rows, halves[h]] = t_[l, h, here, :] + add

                span = pl.ds(64 * part, 64)
                writes.append(
                    pltpu.make_async_copy(out.at[:, span, :], out_hbm.at[:, span, :], lsem.at[3 + part])
                )
                writes[-1].start()
            break

        if fresh:

            def new_source(base, sums, a, k):
                here = pl.ds(base, 8)
                for h in range(2):
                    u = t_[0, h, here, :] + cv[0, h, pl.ds(8 + a, 1), :]
                    s = dyn_rows(base, h) + drn[h, here, :] * jnp.exp(DRAIN_SLOPE * u)
                    src[h, here, :] = s
                    if sums is not None:
                        sums[h] += s

            over_rows(new_source)
            next_c = next_c + block_rows(pick_dot(acc[:, 0 : 2 * LN], cb[0 : 2 * LN, :]))
        moved = (x - sweep_neighbours(x) * (1.0 / DAMPING))[8:16, :] * c_diag
        own_c = next_c - jnp.where(own_block, moved, 0.0)
        side = send_coarse(it + 1, own_c)
        sums_gx = sum_along_gx(it + 1, own_c) if fresh else next_gx

        def whole_residual(base, sums, a, k):
            here, above = pl.ds(base, 8), pl.ds(base - 1, 8)
            block = pl.ds(8 + a, 1)
            xs = [[cv[l, h, block, :] for h in range(2)] for l in range(NL)]
            for h in range(2):
                flow = None
                for l in range(NL):
                    v = xs[l][h]
                    t_[l, h, here, :] = t_[l, h, here, :] + v
                    r = r_[l, h, here, :]
                    if l == 0 and fresh:
                        r = r + src[h, here, :]
                    r = r - fc[l, h, here, :] * (v - cvr[l, h, block, :])
                    r = r - fl[l, h, here, :] * (v - cvl[l, h, block, :])
                    if k == 0:
                        step = v - cv[l, h, pl.ds(7 + a, 1), :]
                        r = r - jnp.where(sub8 == 0, fr[l, h, above, :] * step, 0.0)
                    if k == 3:
                        step = v - cv[l, h, pl.ds(9 + a, 1), :]
                        r = r - jnp.where(sub8 == 7, fr[l, h, here, :] * step, 0.0)
                    if l > 0:
                        r = r + flow
                    if l < NL - 1:
                        flow = fv[l, h, here, :] * (v - xs[l + 1][h])
                        r = r - flow
                    else:
                        r = r - snk[h, here, :] * v
                    r_[l, h, here, :] = r
                    e1_[l, h, here, :] = wg[l, h, here, :] * r

        over_rows(whole_residual)

        xt[...] = jnp.concatenate([x, jnp.zeros((LN - 24, LN), F32)], axis=0).T
        picked = jnp.concatenate(
            [xt[l * 32 + c : l * 32 + c + 1, :] for l in range(NL) for c in (7, 8, 15, 16)], axis=0
        )
        picked = jnp.concatenate(
            [jnp.take_along_axis(picked, 6 + 4 * k + (lane16 >> 5), axis=1) for k in range(SL // LN)], axis=1
        )
        live = NL
        ts_old = [[None, None] for _ in range(NL)]
        rs = [[None, None] for _ in range(NL)]
        e1s = [[None, None] for _ in range(NL)]
        for g in sides:
            for l in range(NL):
                k = 4 * l + 2 * g
                ts_old[l][g] = us[l][g] + jnp.where(sl_row < 8, picked[k : k + 1, :], picked[k + 1 : k + 2, :])
            if fresh:
                srs[g] = dys[g] + drn_s[g] * jnp.exp(DRAIN_SLOPE * ts_old[0][g])
            res = strip_couple([ts_old[l][g] for l in range(NL)], g, NL)
            for l in range(NL):
                r = res[l] - dgs[l, g] * ts_old[l][g]
                if l == 0:
                    r = r + srs[g]
                rs[l][g] = r
                e1s[l][g] = wgs[l, g] * r
        edge_terms(e1s, cf_e)
        sums_gy = sum_along_gy(it + 1, sums_gx, 1)

    for c in started:
        c.wait_send()
    dyn_copy.wait()
    for c in writes:
        c.wait()


def hand_over(a, b, to_a, to_b, sem):
    copies = [
        pltpu.make_async_copy(a.at[l], to_a.at[l], sem.at[l]) for l in range(NL)
    ] + [pltpu.make_async_copy(b, to_b, sem.at[NL])]
    for c in copies:
        c.start()
    for c in copies:
        c.wait()


def n_copies(nx, ny):
    setup = (ny - 1) + 2 + 6 + 2 + (nx - 1) + 8 + 8
    return setup + OUTER * INNER * (8 + (nx - 1) + (ny - 1))


def solution(mesh):
    nx, ny = mesh.shape["gx"], mesh.shape["gy"]
    its = OUTER * INNER
    devices = nx * ny

    def step(material, material_table, sink_cond, drain_current, instance_tile, instance_power):
        n_inst = instance_tile.shape[0]
        field = pltpu.VMEM((NL, 2, NR, LN), F32)
        single = pltpu.VMEM((2, NR, LN), F32)
        vm = lambda *shape: pltpu.VMEM(shape, F32)
        half = lambda *shape: pltpu.VMEM(shape, BF16)
        copies = n_copies(nx, ny)
        scratch = [
            pltpu.VMEM((NL, N, N), jnp.int32), vm(N, N), vm(N, N), vm(NL, N, N), vm(N, N),
            field, field, field, field, field, pltpu.VMEM((NL - 1, 2, NR, LN), F32), field, field,
            single, single, single, field, field, field,
            vm(SL, LN), vm(SL, LN), vm(SL, LN), vm(64, 8 * LN), vm(64, 8 * LN), vm(SL, LN),
            half(8 * LN, LN), half(8 * LN, LN),
            half(devices, n_inst), half(3, 64, n_inst), vm(devices, LN), vm(devices, LN),
            vm(nx, ny, LN), vm(devices, LN), half(32, 32 * devices), half(3, 32, 32 * devices),
            vm(8, LN), vm(8, 8, LN), vm(2, 48, LN),
            vm(2, NQ, 2, 8, LN), vm(2, NQ, 2, 8, LN), vm(2, 8, LN), vm(6, 8, LN),
            vm(2, 8 * NQ, SL), vm(2, 8 * NQ, SL),
            vm(NL, 2, 16, SL), vm(NL, 2, 16, SL), vm(NL - 1, 2, 16, SL), vm(NL, 2, 16, SL), vm(NL, 2, 16, SL),
            vm(2, 16, SL), vm(2, 16, SL), vm(2, 16, SL),
            vm(5, 8, LN), vm(8, 5, 8, LN), vm(7, 24, LN), vm(its, 8, LN), vm(its, 8, 8, LN),
            vm(its, 3, 8, LN), vm(its, nx - 1, 3, 8, LN), vm(its, 3, 8, LN), vm(its, ny - 1, 3, 8, LN),
            vm(NL, 2, 24, LN), vm(NL, 2, 24, LN), vm(NL, 2, 24, LN), vm(LN, LN),
            pltpu.SemaphoreType.DMA((copies,)), pltpu.SemaphoreType.DMA((copies,)), pltpu.SemaphoreType.DMA((7,)),
        ]
        vmem = pl.BlockSpec(memory_space=pltpu.VMEM)
        smem = pl.BlockSpec(memory_space=pltpu.SMEM)
        hbm = pl.BlockSpec(memory_space=pl.ANY)
        shapes = (jax.ShapeDtypeStruct((NL, N, N), F32), jax.ShapeDtypeStruct((N, N), F32))
        results = pl.pallas_call(
            functools.partial(kernel, nx, ny),
            out_shape=shapes,
            in_specs=[hbm, smem, hbm, hbm, vmem, vmem],
            out_specs=(hbm, hbm),
            scratch_shapes=scratch,
            compiler_params=pltpu.CompilerParams(
                collective_id=0, has_side_effects=True, vmem_limit_bytes=56 * 1024 * 1024
            ),
        )(
            material,
            material_table,
            sink_cond,
            drain_current,
            instance_tile.reshape(n_inst // LN, LN),
            instance_power.reshape(n_inst // LN, LN),
        )
        return pl.pallas_call(
            hand_over,
            out_shape=shapes,
            in_specs=[vmem, vmem],
            out_specs=(hbm, hbm),
            scratch_shapes=[pltpu.SemaphoreType.DMA((NL + 1,))],
        )(*results)

    return jax.shard_map(
        step,
        mesh=mesh,
        in_specs=(
            P(None, "gx", "gy"),
            P(),
            P("gx", "gy"),
            P("gx", "gy"),
            P(("gx", "gy")),
            P(("gx", "gy")),
        ),
        out_specs=(P(None, "gx", "gy"), P("gx", "gy")),
        check_vma=False,
    )
```

```python
import functools

import jax
import jax.numpy as jnp
from jax import lax
from jax.experimental import pallas as pl
from jax.experimental.pallas import tpu as pltpu
from jax.sharding import PartitionSpec as P

MESH = pl.DeviceIdType.MESH
F32 = jnp.float32
BF16 = jnp.bfloat16

NL = 4
N = 256
LN = 128
RO = 16
NR = N + 2 * RO
NQ = 6
SL = 384
SO = 64
OUTER = 2
INNER = 2
CJ = 8
DAMPING = 0.8
DRAIN_SLOPE = 0.5
FACE_FLOOR = 0.5
BALANCE_WEIGHT = 0.5
DIRS = ((-1, -1), (-1, 0), (-1, 1), (0, -1), (0, 1), (1, -1), (1, 0), (1, 1))
DIAG = tuple(d for d in DIRS if d[0] and d[1])
OFF_LINE = tuple(d for d in DIRS if d[1])


def iota(shape, dim):
    return lax.broadcasted_iota(jnp.int32, shape, dim)


def harmonic(a, b):
    return 2.0 * a * b / jnp.maximum(a + b, FACE_FLOOR)


def shift(x, amount, axis):
    return pltpu.roll(x, amount % x.shape[axis], axis)


def lookup(ids, table):
    level = list(table)
    for bit in range(4):
        odd = ((ids >> bit) & 1) == 1
        level = [jnp.where(odd, level[2 * k + 1], level[2 * k]) for k in range(len(level) // 2)]
    return level[0]


def exact_dot(a, b):
    return lax.dot_general(
        a, b, (((1,), (0,)), ((), ())), precision=lax.Precision.HIGHEST, preferred_element_type=F32
    )


def pieces(x, count):
    out = []
    for _ in range(count - 1):
        part = x.astype(BF16)
        out.append(part)
        x = x - part.astype(F32)
    return out + [x.astype(BF16)]


def pick_dot(x, ones):
    return sum(jnp.dot(part, ones, preferred_element_type=F32) for part in pieces(x, 3))


class Layout:
    def __init__(self):
        self.count = 0

    def take(self):
        self.count += 1
        return self.count - 1


def kernel(nx, ny, *refs):
    (mat_hbm, tab_hbm, sink_hbm, drain_hbm, tile_hbm, power_hbm, out, dyn_out) = refs[:8]
    (
        mat, sink, drain, tab, inst_tile, inst_power,
        lat, ver, fr, fc, fl, fv, dg, wg, src, drn, snk, t_, r_, e1_,
        cf_t, cf_e, cf_f, acc, acc_n, pk, cb, cbn,
        dest, slots, sout, tin1, tred, tin2, dense_a, dense_b, ts, th, dynr,
        sq_row, rq_row, sq_c, rq_c, sq_s, rq_s,
        fcs, frs, fvs, dgs, wgs, drn_s, dys, srs, sks, gs, gr,
        cm, cmr, coef, ct, nb, s1, ls1, s2, ls2, cv, cvr, cvl, xt,
        ssem, rsem, lsem,
    ) = refs[8:]
    mx, my = lax.axis_index("gx"), lax.axis_index("gy")

    def at(dx, dy):
        return {"gx": lax.rem(mx + (dx + nx), nx), "gy": lax.rem(my + (dy + ny), ny)}

    fetch_small = [
        pltpu.make_async_copy(a, b, lsem.at[3 + k])
        for k, (a, b) in enumerate(((tile_hbm, inst_tile), (power_hbm, inst_power), (tab_hbm, tab)))
    ]
    for c in fetch_small:
        c.start()

    partners = [(d, 0) for d in range(1, nx)] + [(0, d) for d in range(1, ny)] + list(DIAG)
    barrier = pltpu.get_barrier_semaphore()
    for d in partners:
        pl.semaphore_signal(barrier, inc=1, device_id=at(*d), device_id_type=MESH)

    fetch = [
        pltpu.make_async_copy(a, b, lsem.at[k])
        for k, (a, b) in enumerate(((mat_hbm, mat), (sink_hbm, sink), (drain_hbm, drain)))
    ]
    for c in fetch:
        c.start()

    numbers = Layout()
    started = []

    def send(a, b, to):
        k = numbers.take()
        copy = pltpu.make_async_remote_copy(
            src_ref=a, dst_ref=b, send_sem=ssem.at[k], recv_sem=rsem.at[k],
            device_id=at(*to), device_id_type=MESH,
        )
        copy.start()
        started.append(copy)
        return copy

    lane8 = iota((8, LN), 1)
    first_lane = lane8 == 0
    last_lane = lane8 == LN - 1
    low_half = lane8 < LN // 2

    devices = nx * ny
    chunks = inst_tile.shape[0]
    for c in fetch_small:
        c.wait()
    sub_d = iota((devices, LN), 0)
    lane_d = iota((devices, LN), 1)
    up_to = jnp.where(iota((LN, LN), 0) <= iota((LN, LN), 1), 1.0, 0.0).astype(BF16)
    for k in range(chunks):
        s = inst_tile[k : k + 1, :] >> 10
        owner = (s % ny) * nx + s // ny
        dest[:, k * LN : (k + 1) * LN] = jnp.where(sub_d == owner, 1.0, 0.0).astype(BF16)
    before = jnp.zeros((devices, 1), F32)
    slot_row = iota((64, LN), 0)
    for k in range(chunks):
        span = slice(k * LN, (k + 1) * LN)
        d = dest[:, span]
        within = jnp.dot(d, up_to, preferred_element_type=F32)
        rank = jnp.sum(d.astype(F32) * (within + before), axis=0, keepdims=True)
        before = before + within[:, LN - 1 : LN]
        at_slot = (slot_row & 31) == rank.astype(jnp.int32) - 1
        t = inst_tile[k : k + 1, :]
        ids = ((t & 992).astype(F32), (t & 31).astype(F32), jnp.zeros((1, LN), F32))
        for q, part in enumerate(pieces(inst_power[k : k + 1, :], 3)):
            value = jnp.where(slot_row < 32, part.astype(F32), ids[q])
            slots[q, :, span] = jnp.where(at_slot, value, 0.0).astype(BF16)
    total = None
    for q in range(3):
        term = lax.dot_general(
            dest[...], slots[q], (((1,), (1,)), ((), ())), preferred_element_type=F32
        )
        total = term if total is None else total + term
    sout[...] = jnp.concatenate([total, jnp.zeros((devices, LN - 64), F32)], axis=1)
    power_sum = jnp.zeros((8, LN), F32)
    for k in range(chunks // 8):
        power_sum = power_sum + inst_power[8 * k : 8 * k + 8, :]

    def bundle(j):
        return sout.at[pl.ds(pl.multiple_of(j * nx, nx), nx), :]

    pl.semaphore_wait(barrier, len(partners))
    tile_in = []
    for d in range(1, ny):
        tile_in.append(send(bundle(lax.rem(my + d, ny)), tin1.at[pl.ds(d * nx, nx)], (0, d)))
    tin1[0:nx, :] = bundle(my)[...]

    def pack(values):
        packed = jnp.zeros((8, LN), F32)
        for q, (a, b) in enumerate(values):
            both = shift(jnp.where(low_half, a, b), 16 * q + 8, 1)
            packed = jnp.where((lane8 >> 4) == q, both, packed)
        return packed

    halves = (slice(0, LN), slice(LN, N))

    def raw(rows):
        mats = [tuple(mat[l, rows, h].astype(F32) for h in halves) for l in range(NL)]
        return mats + [tuple(a[rows, h] for h in halves) for a in (sink, drain)]

    for c in fetch:
        c.wait()
    for side, rows in enumerate((slice(0, 8), slice(N - 8, N))):
        values = raw(rows)
        for q, (a, b) in enumerate(values):
            sq_row[side, q, 0] = a
            sq_row[side, q, 1] = b
        sq_c[side] = pack(values)
    margin_row = [send(sq_row.at[s], rq_row.at[s], (2 * s - 1, 0)) for s in range(2)]
    corner_dirs = ((-1, 0), (1, 0)) + DIAG
    margin_c = {
        d: (k, send(sq_c.at[0 if d[0] < 0 else 1], rq_c.at[k], d)) for k, d in enumerate(corner_dirs)
    }

    @pl.loop(0, N // 32)
    def _(a):
        for k in range(4):
            rows = pl.ds(pl.multiple_of(a * 32 + k * 8, 8), 8)
            pk[pl.ds(pl.multiple_of(a * 32 + k * 8 + SO, 8), 8), :] = pack(raw(rows))

    pk[0:SO, :] = jnp.zeros((SO, LN), F32)
    pk[SO + N :, :] = jnp.zeros((SL - N - SO, LN), F32)
    for k in range(SL // LN):
        span = slice(k * LN, (k + 1) * LN)
        block = pk[span, :].T
        for q in range(NQ):
            sq_s[0, 8 * q : 8 * q + 8, span] = block[16 * q + 8 : 16 * q + 16, :]
            sq_s[1, 8 * q : 8 * q + 8, span] = block[16 * q : 16 * q + 8, :]
    margin_we = [send(sq_s.at[s], rq_s.at[s], (0, 2 * s - 1)) for s in range(2)]

    col_n = iota((LN, LN), 1)
    row_n = iota((LN, LN), 0)
    for l in range(NL):
        for h in range(2):
            span = pl.ds((2 * l + h) * LN, LN)
            goal = l * 32 + 8 + h * 4 + (row_n >> 5)
            cb[span, :] = jnp.where(col_n == goal, 1.0, 0.0).astype(BF16)
            hit = ((row_n & 31) == 31) & (col_n == goal)
            if h == 0:
                hit = hit | ((row_n == 0) & (col_n == l * 32 + 7))
            cbn[span, :] = jnp.where(hit, 1.0, 0.0).astype(BF16)
    table = [[tab[q, k] for k in range(16)] for q in range(2)]

    zero8 = jnp.zeros((8, LN), F32)
    for ref, places in ((t_, (0, NR - 8)), (e1_, (0, 8, NR - 16, NR - 8)), (fr, (0,)), (lat, (NR - 8,))):
        for l in range(NL):
            for h in range(2):
                for place in places:
                    ref[l, h, place : place + 8, :] = zero8

    @pl.loop(0, N // 32, init_carry=power_sum)
    def source_sum(a, source_sum):
        for k in range(4):
            rows = pl.ds(pl.multiple_of(a * 32 + k * 8, 8), 8)
            into = pl.ds(pl.multiple_of(a * 32 + k * 8 + RO, 8), 8)
            for h in range(2):
                for l in range(NL):
                    ids = mat[l, rows, halves[h]]
                    lat[l, h, into, :] = lookup(ids, table[0])
                    ver[l, h, into, :] = lookup(ids, table[1])
                snk[h, into, :] = sink[rows, halves[h]]
                d = drain[rows, halves[h]]
                drn[h, into, :] = d
                source_sum = source_sum + d
        return source_sum

    for c in tile_in:
        c.wait_recv()
    for x in range(nx):
        tred[x] = tin1[pl.ds(x, ny, stride=nx), :]
    tile_in2 = []
    for d in range(1, nx):
        x = lax.rem(mx + d, nx)
        tile_in2.append(send(tred.at[x], tin2.at[pl.ds(d * ny, ny)], (d, 0)))
    tin2[0:ny, :] = tred[mx]

    edge_n = jnp.where(mx == 0, 0.0, 1.0)
    edge_s = jnp.where(mx == nx - 1, 0.0, 1.0)
    edge_w = jnp.where(my == 0, 0.0, 1.0)
    edge_e = jnp.where(my == ny - 1, 0.0, 1.0)
    for c in margin_row:
        c.wait_recv()
    for slot, base, keep in ((1, RO - 8, edge_n), (0, RO + N, edge_s)):
        rows = slice(base, base + 8)
        for h in range(2):
            for l in range(NL):
                ids = rq_row[slot, l, h].astype(jnp.int32)
                lat[l, h, rows, :] = lookup(ids, table[0]) * keep
                ver[l, h, rows, :] = lookup(ids, table[1]) * keep
            snk[h, rows, :] = rq_row[slot, 4, h] * keep
            drn[h, rows, :] = rq_row[slot, 5, h] * keep
    for c in margin_we:
        c.wait_recv()
    for _, c in margin_c.values():
        c.wait_recv()

    def corner_block(dy):
        top, low = (rq_c[margin_c[(-dx, -dy)][0]] for dx in (-1, 1))
        pad = jnp.zeros((SO - 8, LN), F32)
        return jnp.concatenate([pad, top, low, pad], axis=0).T

    blocks = {dy: corner_block(dy) for dy in (-1, 0, 1)}

    def merge(body, corners):
        return jnp.concatenate(
            [
                jnp.where((lane8 >> 3) == SO // 8 - 1, corners, body[:, :LN]),
                body[:, LN : 2 * LN],
                jnp.where((lane8 >> 3) == SO // 8, corners, body[:, 2 * LN :]),
            ],
            axis=1,
        )

    def raw_strip(q, side):
        own, got = slice(8 * q, 8 * q + 8), slice(16 * q, 16 * q + 16)
        if side == 0:
            outside = merge(rq_s[1, own, :], blocks[-1][got, :][0:8, :])
            inside = merge(sq_s[0, own, :], blocks[0][got, :][8:16, :])
            return jnp.concatenate([outside, inside], axis=0)
        outside = merge(rq_s[0, own, :], blocks[1][got, :][8:16, :])
        inside = merge(sq_s[1, own, :], blocks[0][got, :][0:8, :])
        return jnp.concatenate([inside, outside], axis=0)

    sl_lane = iota((16, SL), 1)
    sl_row = iota((16, SL), 0)
    one = jnp.ones((16, SL), F32)
    keep_rows = jnp.where(sl_lane < SO, one * edge_n, jnp.where(sl_lane >= SO + N, one * edge_s, one))
    keep = (
        keep_rows * jnp.where(sl_row < 8, one * edge_w, one),
        keep_rows * jnp.where(sl_row >= 8, one * edge_e, one),
    )
    sides = range(2)
    for g in sides:
        lats, vers = [], []
        for l in range(NL):
            ids = raw_strip(l, g).astype(jnp.int32)
            lats.append(lookup(ids, table[0]) * keep[g])
            vers.append(lookup(ids, table[1]) * keep[g])
        sink_s = raw_strip(4, g) * keep[g]
        sks[g] = sink_s
        drn_s[g] = raw_strip(5, g) * keep[g]
        up = None
        for l in range(NL):
            c = harmonic(lats[l], shift(lats[l], -1, 0))
            r = harmonic(lats[l], shift(lats[l], -1, 1))
            fcs[l, g] = c
            frs[l, g] = r
            d = c + shift(c, 1, 0) + r + shift(r, 1, 1)
            if l > 0:
                d = d + up
            if l < NL - 1:
                up = harmonic(vers[l], vers[l + 1])
                fvs[l, g] = up
                d = d + up
            else:
                d = d + sink_s
            d = jnp.maximum(d, FACE_FLOOR)
            dgs[l, g] = d
            wgs[l, g] = DAMPING / d

    row_z = iota((8, SL), 0)

    def column_form(west, east, ref):
        z = jnp.zeros((8, SL), F32)
        for l in range(NL):
            if west[l] is not None:
                z = jnp.where(row_z == 2 * l + 1, west[l], jnp.where(row_z == 2 * l, east[l], z))
        for k in range(SL // LN):
            block = jnp.concatenate([z[:, k * LN : (k + 1) * LN], jnp.zeros((LN - 8, LN), F32)], axis=0)
            ref[k * LN : (k + 1) * LN, :] = block.T

    def columns(ref, base):
        tile = ref[pl.ds(base + (SO - RO), 8), :]
        return [shift(tile, -(2 * l + 1), 1) for l in range(NL)]

    def edge_terms(v, ref):
        column_form(
            [(fcs[l, 0] * v[l][0])[7:8, :] for l in range(NL)],
            [fcs[l, 1][7:8, :] * v[l][1][8:9, :] for l in range(NL)],
            ref,
        )

    column_form([fcs[l, 0, 7:8, :] for l in range(NL)], [fcs[l, 1, 7:8, :] for l in range(NL)], cf_f)

    def faces(base, sums):
        bf = columns(cf_f, base)
        here, below = pl.ds(base, 8), pl.ds(base + 1, 8)
        vs = [[ver[l, h, here, :] for h in range(2)] for l in range(NL)]
        for l in range(NL):
            a0, a1 = lat[l, 0, here, :], lat[l, 1, here, :]
            ra0, ra1 = shift(a0, -1, 1), shift(a1, -1, 1)
            c0 = harmonic(a0, jnp.where(last_lane, ra1, ra0))
            c1 = jnp.where(last_lane, bf[l], harmonic(a1, ra1))
            rc0, rc1 = shift(c0, 1, 1), shift(c1, 1, 1)
            fc[l, 0, here, :] = c0
            fc[l, 1, here, :] = c1
            fl[l, 0, here, :] = jnp.where(first_lane, bf[l], rc0)
            fl[l, 1, here, :] = jnp.where(first_lane, rc0, rc1)
            for h, a in ((0, a0), (1, a1)):
                fr[l, h, here, :] = harmonic(a, lat[l, h, below, :])
            if sums is not None:
                sums[0][2 * l] += jnp.where(first_lane, bf[l], c0)
                sums[0][2 * l + 1] += c1
            for h in range(2):
                if l < NL - 1:
                    v = harmonic(vs[l][h], vs[l + 1][h])
                    fv[l, h, here, :] = v
                else:
                    v = snk[h, here, :]
                if sums is not None:
                    sums[1][2 * l + h] += v

    faces(RO - 8, None)
    faces(RO + N, None)

    @pl.loop(0, N // 32)
    def _(a):
        sums = [[zero8] * 8, [zero8] * 8]
        for k in range(4):
            faces(pl.multiple_of(RO + 32 * a + 8 * k, 8), sums)
        rows = pl.ds(pl.multiple_of(a * 8, 8), 8)
        for q in range(8):
            acc_n[rows, q * LN : (q + 1) * LN] = sums[0][q]
            acc[rows, q * LN : (q + 1) * LN] = sums[1][q]

    for c in tile_in2:
        c.wait_recv()
    quarter = devices // 4
    lane_q = iota((quarter, LN), 1)
    power = jnp.zeros((quarter, LN), F32)
    ids = power
    for k in range(4):
        part = tin2[k * quarter : (k + 1) * quarter, :]
        mine = (lane_q >> 5) == k
        power = jnp.where(mine, shift(part, 32 * k, 1), power)
        ids = jnp.where(mine, shift(part, 32 * k - 32, 1), ids)
    ids = ids.astype(jnp.int32)
    powers = [part.astype(F32) for part in pieces(power, 3)]
    sub32 = iota((32, LN), 0)
    for k in range(quarter):
        span = slice(k * LN, (k + 1) * LN)
        one_id = ids[k : k + 1, :]
        dense_a[:, span] = jnp.where(sub32 == (one_id >> 5), 1.0, 0.0).astype(BF16)
        hit = sub32 == (one_id & 31)
        for q in range(3):
            dense_b[q, :, span] = jnp.where(hit, powers[q][k : k + 1, :], 0.0).astype(BF16)
    total = None
    for q in range(3):
        term = lax.dot_general(
            dense_a[...], dense_b[q], (((1,), (1,)), ((), ())), preferred_element_type=F32
        )
        total = term if total is None else total + term
    total = jnp.concatenate([total * (1.0 / 64.0), jnp.zeros((32, LN - 32), F32)], axis=1)
    total_t = jnp.concatenate([total, jnp.zeros((LN - 32, LN), F32)], axis=0).T
    sub8 = iota((8, LN), 0)

    def stack(*rows):
        out8 = zero8
        for k, x in enumerate(rows):
            out8 = jnp.where(sub8 == k, x, out8)
        return out8

    ts[...] = stack(total_t[0:1, :], total_t[31:32, :], total[0:1, :], total[31:32, :])
    th_in = {d: (k, send(ts, th.at[k], d)) for k, d in enumerate(DIRS)}
    spread_cols = jnp.where(iota((LN, N), 0) == (iota((LN, N), 1) >> 3), 1.0, 0.0).astype(BF16)
    wide = pick_dot(total, spread_cols)
    for h in range(2):
        dynr[h, 8:40, :] = wide[:, halves[h]]

    block_lane = lane8 & 31
    own_block = (block_lane >= 8) & (block_lane < 16)

    def block_rows(x):
        return x.reshape(8, 8, LN).sum(axis=1)

    def edge_sums(start):
        rows = [fr[l, h, pl.ds(start, 8, stride=32), :] for l in range(NL) for h in range(2)]
        return pick_dot(jnp.concatenate(rows, axis=1), cb[...])

    c_east = edge_sums(RO + 31)
    c_east_prev = edge_sums(RO - 1)
    c_north_wide = block_rows(pick_dot(acc_n[...], cbn[...]))
    c_north = jnp.where(own_block, c_north_wide, 0.0)
    c_north_prev = jnp.where(own_block, shift(c_north_wide, 1, 1), 0.0)
    up_sink = block_rows(pick_dot(acc[...], cb[...]))
    c_up = jnp.where(lane8 < 96, up_sink, 0.0)
    c_sink = jnp.where(lane8 >= 96, up_sink, 0.0)
    c_diag = c_east + c_east_prev + c_north + c_north_prev + c_up + shift(c_up, 32, 1) + c_sink
    for q, x in enumerate((c_east, c_north, c_up, c_diag, c_sink)):
        cm[q] = x
    cm_in = {d: (k, send(cm, cmr.at[k], d)) for k, d in enumerate(DIRS)}

    def sum_along_gx(it, *tiles):
        parts = len(tiles)
        for q, x in enumerate(tiles):
            s1[it, q] = x
        span = pl.ds(0, parts)
        return [send(s1.at[it, span], ls1.at[it, d - 1, span], (d, 0)) for d in range(1, nx)]

    def sum_along_gy(it, arriving, parts):
        span = pl.ds(0, parts)
        total = [s1[it, q] for q in range(parts)]
        for d in range(1, nx):
            arriving[d - 1].wait_recv()
            for q in range(parts):
                total[q] = total[q] + ls1[it, d - 1, q]
        for q in range(parts):
            s2[it, q] = total[q]
        return [send(s2.at[it, span], ls2.at[it, d - 1, span], (0, d)) for d in range(1, ny)]

    def sum_end(it, arriving, parts):
        total = [s2[it, q] for q in range(parts)]
        for d in range(1, ny):
            arriving[d - 1].wait_recv()
            for q in range(parts):
                total[q] = total[q] + ls2[it, d - 1, q]
        return [x.sum(axis=0, keepdims=True).sum(axis=1, keepdims=True) for x in total]

    sums_gx = sum_along_gx(0, source_sum, c_diag, c_sink)

    def diagonal(base):
        here, above = pl.ds(base, 8), pl.ds(base - 1, 8)
        for l in range(NL):
            for h in range(2):
                d = fr[l, h, above, :] + fr[l, h, here, :] + fl[l, h, here, :] + fc[l, h, here, :]
                if l > 0:
                    d = d + fv[l - 1, h, here, :]
                if l < NL - 1:
                    d = d + fv[l, h, here, :]
                else:
                    d = d + snk[h, here, :]
                d = jnp.maximum(d, FACE_FLOOR)
                dg[l, h, here, :] = d
                wg[l, h, here, :] = DAMPING / d

    diagonal(RO - 8)
    diagonal(RO + N)

    @pl.loop(0, N // 32)
    def _(a):
        for k in range(4):
            diagonal(pl.multiple_of(RO + 32 * a + 8 * k, 8))

    def couple(ref, base, edge, live):
        here, above, below = pl.ds(base, 8), pl.ds(base - 1, 8), pl.ds(base + 1, 8)
        res = [[None, None] for _ in range(NL)]
        mid = [[ref[l, h, here, :] for h in range(2)] for l in range(live)]
        for l in range(live):
            a0, a1 = mid[l]
            f0, f1 = fc[l, 0, here, :], fc[l, 1, here, :]
            ra0, ra1 = shift(a0, -1, 1), shift(a1, -1, 1)
            p0, p1 = shift(f0 * a0, 1, 1), shift(f1 * a1, 1, 1)
            lateral = (
                f0 * jnp.where(last_lane, ra1, ra0) + jnp.where(first_lane, edge[l], p0),
                jnp.where(last_lane, edge[l], f1 * ra1) + jnp.where(first_lane, p0, p1),
            )
            for h in range(2):
                res[l][h] = (
                    lateral[h]
                    + fr[l, h, above, :] * ref[l, h, above, :]
                    + fr[l, h, here, :] * ref[l, h, below, :]
                )
        for l in range(live):
            for h in range(2):
                for face, to in ((l - 1, l - 1), (l, l + 1)):
                    if 0 <= to < NL:
                        term = fv[face, h, here, :] * mid[l][h]
                        res[to][h] = term if res[to][h] is None else res[to][h] + term
        return mid, res

    def strip_couple(v, g, live):
        res = []
        for l in range(live):
            p, r = fcs[l, g] * v[l], frs[l, g]
            res.append(
                fcs[l, g] * shift(v[l], -1, 0) + shift(p, 1, 0) + r * shift(v[l], -1, 1) + shift(r * v[l], 1, 1)
            )
        res += [None] * (NL - live)
        for l in range(live):
            for face, to in ((l - 1, l - 1), (l, l + 1)):
                if 0 <= to < NL:
                    term = fvs[face, g] * v[l]
                    res[to] = term if res[to] is None else res[to] + term
        return res

    def dyn_rows(base, h):
        return dynr[h, pl.ds(base // 8 + 6, 1), :]

    def over_rows(body, margins=True, carry=None):
        if margins:
            body(RO - 8, None, -1, 3)
            body(RO + N, None, 8, 0)

        @pl.loop(0, N // 64)
        def _(pair):
            for a in (2 * pair, 2 * pair + 1):
                sums = [zero8] * 8
                for k in range(4):
                    body(pl.multiple_of(RO + 32 * a + 8 * k, 8), sums, a, k)
                rows = pl.ds(pl.multiple_of(a * 8, 8), 8)
                for q in range(8):
                    if sums[q] is not zero8:
                        acc[rows, q * LN : (q + 1) * LN] = sums[q]

    lane16 = iota((16, LN), 1)
    lane24 = iota((24, LN), 1)

    def sweep_neighbours(x):
        return (
            coef[1] * shift(x, -1, 0) + coef[2] * shift(x, 1, 0)
            + coef[3] * shift(x, -1, 1) + coef[4] * shift(x, 1, 1)
            + coef[5] * shift(x, -32, 1) + coef[6] * shift(x, 32, 1)
        )

    def coarse_sweeps(right):
        rw = coef[0] * right
        x = rw
        for _ in range(CJ - 1):
            x = (1.0 - DAMPING) * x + rw + sweep_neighbours(x)
        return x

    def assemble(own, other):
        rows = []
        for dx in (-1, 0, 1):
            centre = own if dx == 0 else other((dx, 0))
            rows.append(centre + shift(other((dx, -1)), -8, 1) + shift(other((dx, 1)), 8, 1))
        return jnp.concatenate(rows, axis=0)

    def send_coarse(it, own):
        ct[it] = own
        return {d: (k, send(ct.at[it], nb.at[it, k], d)) for k, d in enumerate(DIRS)}

    def first_residual(base, sums, a, k):
        here = pl.ds(base, 8)
        for h in range(2):
            r = dyn_rows(base, h) + drn[h, here, :]
            src[h, here, :] = r
            r_[0, h, here, :] = r
            e1_[0, h, here, :] = wg[0, h, here, :] * r
            if sums is not None:
                sums[h] += r

    over_rows(first_residual, margins=False)
    own_c = block_rows(pick_dot(acc[:, 0 : 2 * LN], cb[0 : 2 * LN, :]))
    side = send_coarse(0, own_c)

    def second_sweep(base, live, edge, first):
        here = pl.ds(base, 8)
        mid, res = couple(e1_, base, edge, live)
        for l in range(NL):
            for h in range(2):
                if l < live:
                    u = (1.0 - DAMPING) * mid[l][h] + wg[l, h, here, :] * (r_[l, h, here, :] + res[l][h])
                elif res[l][h] is not None:
                    u = wg[l, h, here, :] * res[l][h]
                else:
                    u = zero8
                if not first:
                    u = u + t_[l, h, here, :]
                t_[l, h, here, :] = u

    over_rows(lambda base, sums, a, k: second_sweep(base, 1, [zero8], True), margins=False)

    snk_e1 = [wgs[NL - 1, g] * sks[g] for g in sides]
    column_form(
        [None] * (NL - 1) + [(fcs[NL - 1, 0] * snk_e1[0])[7:8, :]],
        [None] * (NL - 1) + [fcs[NL - 1, 1][7:8, :] * snk_e1[1][8:9, :]],
        cf_t,
    )

    def sink_first(base, sums, a, k):
        here = pl.ds(base, 8)
        for h in range(2):
            gs[h, here, :] = wg[NL - 1, h, here, :] * snk[h, here, :]

    over_rows(sink_first)

    def sink_second(base, sums, a, k):
        here, above, below = pl.ds(base, 8), pl.ds(base - 1, 8), pl.ds(base + 1, 8)
        top = NL - 1
        edge = columns(cf_t, base)[top]
        a0, a1 = gs[0, here, :], gs[1, here, :]
        f0, f1 = fc[top, 0, here, :], fc[top, 1, here, :]
        ra0, ra1 = shift(a0, -1, 1), shift(a1, -1, 1)
        p0, p1 = shift(f0 * a0, 1, 1), shift(f1 * a1, 1, 1)
        lateral = (
            f0 * jnp.where(last_lane, ra1, ra0) + jnp.where(first_lane, edge, p0),
            jnp.where(last_lane, edge, f1 * ra1) + jnp.where(first_lane, p0, p1),
        )
        for h, e in ((0, a0), (1, a1)):
            flow = (
                lateral[h]
                + fr[top, h, above, :] * gs[h, above, :]
                + fr[top, h, here, :] * gs[h, below, :]
            )
            gr[1, h, here, :] = (1.0 - DAMPING) * e + wg[top, h, here, :] * (snk[h, here, :] + flow)
            gr[0, h, here, :] = wg[top - 1, h, here, :] * (fv[top - 1, h, here, :] * e)

    over_rows(sink_second, margins=False)
    sums_gy = sum_along_gy(0, sums_gx, 3)

    @pl.loop(0, N // 32)
    def _(a):
        for k in range(4):
            for h in range(2):
                dyn_out[pl.ds(pl.multiple_of(a * 32 + k * 8, 8), 8), halves[h]] = jnp.broadcast_to(
                    dynr[h, pl.ds(8 + 4 * a + k, 1), :], (8, LN)
                )
    for _, c in th_in.values():
        c.wait_recv()

    def rim(d, k):
        return th[th_in[(-d[0], -d[1])][0], k : k + 1, :]

    wide_rims = pick_dot(stack(rim((-1, 0), 3) * edge_n, rim((1, 0), 2) * edge_s), spread_cols)
    for h in range(2):
        dynr[h, 0:8, :] = jnp.broadcast_to(wide_rims[0:1, halves[h]], (8, LN))
        dynr[h, 40:48, :] = jnp.broadcast_to(wide_rims[1:2, halves[h]], (8, LN))
    body = stack(rim((0, -1), 1), ts[0:1, :], ts[1:2, :], rim((0, 1), 0))
    top = stack(rim((-1, -1), 1), rim((-1, 0), 0), rim((-1, 0), 1), rim((-1, 1), 0))
    low = stack(rim((1, -1), 1), rim((1, 0), 0), rim((1, 0), 1), rim((1, 1), 0))
    tall = jnp.where(
        lane8 == 0,
        shift(top, -31, 1),
        jnp.where(lane8 == 33, shift(low, 33, 1), jnp.where(lane8 < 33, shift(body, 1, 1), 0.0)),
    )
    spread_rows = jnp.where(iota((LN, SL), 0) == ((iota((LN, SL), 1) - (SO - 8)) >> 3), 1.0, 0.0).astype(BF16)
    tall = pick_dot(tall, spread_rows)
    for g in sides:
        dyn_s = jnp.where(sl_row < 8, tall[2 * g : 2 * g + 1, :], tall[2 * g + 1 : 2 * g + 2, :]) * keep[g]
        dys[g] = dyn_s
        srs[g] = dyn_s + drn_s[g]
    first_residual(RO - 8, None, -1, 3)
    first_residual(RO + N, None, 8, 0)

    rs = [[srs[g] for g in sides]]
    e1s = [[wgs[0, g] * srs[g] for g in sides]]
    live = 1
    zeros_s = jnp.zeros((16, SL), F32)
    edge_terms(e1s + [[zeros_s, zeros_s]] * (NL - 1), cf_e)
    second_sweep(RO - 8, 1, columns(cf_e, RO - 8), True)
    second_sweep(RO + N, 1, columns(cf_e, RO + N), True)

    def over_edges(base, sums, a, k):
        here = pl.ds(base, 8)
        edge = columns(cf_e, base)[0]
        for h, lane in ((0, first_lane), (1, last_lane)):
            t_[0, h, here, :] = t_[0, h, here, :] + jnp.where(lane, wg[0, h, here, :] * edge, 0.0)

    over_rows(over_edges, margins=False)
    for h in range(2):
        for row, beyond, face in ((RO, RO - 1, RO - 1), (RO + N - 1, RO + N, RO + N - 1)):
            t_[0, h, row : row + 1, :] = t_[0, h, row : row + 1, :] + wg[0, h, row : row + 1, :] * (
                fr[0, h, face : face + 1, :] * e1_[0, h, beyond : beyond + 1, :]
            )

    for _, c in cm_in.values():
        c.wait_recv()
    w_east, w_north, w_up, w_diag, w_sink = (
        assemble(cm[q], lambda d, q=q: cmr[cm_in[(-d[0], -d[1])][0], q]) for q in range(5)
    )
    gain = jnp.where((lane24 & 31) < 24, DAMPING / jnp.maximum(w_diag, 1e-30), 0.0)
    coef[0] = gain
    coef[1] = gain * w_east
    coef[2] = gain * shift(w_east, 1, 0)
    coef[3] = gain * w_north
    coef[4] = gain * shift(w_north, 1, 1)
    coef[5] = gain * w_up
    coef[6] = gain * shift(w_up, 32, 1)
    adjoint = coarse_sweeps(w_sink)
    own_adjoint = jnp.where(own_block, adjoint[8:16, :], 0.0)
    sums_gx = sum_along_gx(1, own_adjoint * own_c)

    ts_old = None
    balance = diag_total = sink_total = source_total = None
    sweeps = OUTER * INNER
    for it in range(sweeps):
        first, last = it == 0, it == sweeps - 1
        fresh = (it + 1) % INNER == 0

        if not first:
            over_rows(
                lambda base, sums, a, k: second_sweep(base, NL, columns(cf_e, base), False), margins=not last
            )

        if not last:
            us = [[None, None] for _ in range(NL)]
            for g in sides:
                res = strip_couple([e1s[l][g] for l in range(live)], g, live)
                for l in range(NL):
                    if l < live:
                        u = (1.0 - DAMPING) * e1s[l][g] + wgs[l, g] * (rs[l][g] + res[l])
                    elif res[l] is not None:
                        u = wgs[l, g] * res[l]
                    else:
                        u = zeros_s
                    us[l][g] = u if first else ts_old[l][g] + u
            edge_terms(us, cf_t)

            def half_residual(base, sums, a, k):
                here = pl.ds(base, 8)
                mid, res = couple(t_, base, columns(cf_t, base), NL)
                for l in range(NL):
                    for h in range(2):
                        r = res[l][h] - dg[l, h, here, :] * mid[l][h]
                        if l == 0 and not fresh:
                            r = r + src[h, here, :]
                        r_[l, h, here, :] = r
                        if sums is not None:
                            sums[2 * l + h] += r

            over_rows(half_residual)
            if it == 2:
                sums_gy = sum_along_gy(2, sums_gx, 2)
            next_c = block_rows(pick_dot(acc[...], cb[...]))

        for _, c in side.values():
            c.wait_recv()
        x = coarse_sweeps(assemble(own_c, lambda d: nb[it, side[(-d[0], -d[1])][0]]))
        if first:
            source_total, diag_total, sink_total = sum_end(0, sums_gy, 3)
        elif it == 1:
            source_total = source_total - sum_end(1, sums_gy, 1)[0] - balance * sink_total
        elif last:
            source_total, less = sum_end(2, sums_gy, 2)
            former = BALANCE_WEIGHT * source_total / diag_total
            source_total = source_total - less - former * sink_total
            x = x + former * (1.0 - adjoint)
        if it != 2:
            balance = BALANCE_WEIGHT * source_total / diag_total
            x = x + balance

        for l in range(NL):
            for h in range(2):
                at_col = l * 32 + 8 + h * 4
                cv[l, h] = jnp.take_along_axis(x, at_col + (lane24 >> 5), axis=1)
                if not last:
                    cvr[l, h] = jnp.take_along_axis(x, at_col + ((lane24 + 1) >> 5), axis=1)
                    cvl[l, h] = jnp.take_along_axis(x, at_col + ((lane24 - 1) >> 5), axis=1)

        if last:

            @pl.loop(0, N // 32)
            def _(a):
                for l in range(NL):
                    for h in range(2):
                        add = cv[l, h, pl.ds(8 + a, 1), :]
                        for k in range(4):
                            rows = pl.ds(pl.multiple_of(32 * a + 8 * k, 8), 8)
                            here = pl.ds(pl.multiple_of(RO + 32 * a + 8 * k, 8), 8)
                            u = t_[l, h, here, :] + add
                            if l >= NL - 2:
                                u = u - former * gr[l - (NL - 2), h, here, :]
                            out[l, rows, halves[h]] = u

            break

        if fresh:

            def new_source(base, sums, a, k):
                here = pl.ds(base, 8)
                for h in range(2):
                    u = t_[0, h, here, :] + cv[0, h, pl.ds(8 + a, 1), :]
                    s = dyn_rows(base, h) + drn[h, here, :] * jnp.exp(DRAIN_SLOPE * u)
                    src[h, here, :] = s
                    if sums is not None:
                        sums[h] += s

            over_rows(new_source)
            next_c = next_c + block_rows(pick_dot(acc[:, 0 : 2 * LN], cb[0 : 2 * LN, :]))
        moved = (x - sweep_neighbours(x) * (1.0 / DAMPING))[8:16, :] * c_diag
        own_c = next_c - jnp.where(own_block, moved, 0.0)
        side = send_coarse(it + 1, own_c)
        if first:
            sums_gy = sum_along_gy(1, sums_gx, 1)

        def whole_residual(base, sums, a, k):
            here, above = pl.ds(base, 8), pl.ds(base - 1, 8)
            block = pl.ds(8 + a, 1)
            xs = [[cv[l, h, block, :] for h in range(2)] for l in range(NL)]
            for h in range(2):
                flow = None
                for l in range(NL):
                    v = xs[l][h]
                    t_[l, h, here, :] = t_[l, h, here, :] + v
                    r = r_[l, h, here, :]
                    if l == 0 and fresh:
                        r = r + src[h, here, :]
                    r = r - fc[l, h, here, :] * (v - cvr[l, h, block, :])
                    r = r - fl[l, h, here, :] * (v - cvl[l, h, block, :])
                    if k == 0:
                        step = v - cv[l, h, pl.ds(7 + a, 1), :]
                        r = r - jnp.where(sub8 == 0, fr[l, h, above, :] * step, 0.0)
                    if k == 3:
                        step = v - cv[l, h, pl.ds(9 + a, 1), :]
                        r = r - jnp.where(sub8 == 7, fr[l, h, here, :] * step, 0.0)
                    if l > 0:
                        r = r + flow
                    if l < NL - 1:
                        flow = fv[l, h, here, :] * (v - xs[l + 1][h])
                        r = r - flow
                    else:
                        r = r - snk[h, here, :] * v
                    r_[l, h, here, :] = r
                    e1_[l, h, here, :] = wg[l, h, here, :] * r
                    if it == 1 and l >= NL - 2 and sums is not None:
                        sums[0] += gr[l - (NL - 2), h, here, :] * r

        over_rows(whole_residual)
        if it == 1:
            response = acc[0:8, 0:LN]
            for a in range(1, 8):
                response = response + acc[8 * a : 8 * a + 8, 0:LN]
            sums_gx = sum_along_gx(2, own_c, response + own_adjoint * own_c)

        xt[...] = jnp.concatenate([x, jnp.zeros((LN - 24, LN), F32)], axis=0).T
        picked = jnp.concatenate(
            [xt[l * 32 + c : l * 32 + c + 1, :] for l in range(NL) for c in (7, 8, 15, 16)], axis=0
        )
        picked = jnp.concatenate(
            [jnp.take_along_axis(picked, 6 + 4 * k + (lane16 >> 5), axis=1) for k in range(SL // LN)], axis=1
        )
        live = NL
        ts_old = [[None, None] for _ in range(NL)]
        rs = [[None, None] for _ in range(NL)]
        e1s = [[None, None] for _ in range(NL)]
        for g in sides:
            for l in range(NL):
                k = 4 * l + 2 * g
                ts_old[l][g] = us[l][g] + jnp.where(sl_row < 8, picked[k : k + 1, :], picked[k + 1 : k + 2, :])
            if fresh:
                srs[g] = dys[g] + drn_s[g] * jnp.exp(DRAIN_SLOPE * ts_old[0][g])
            res = strip_couple([ts_old[l][g] for l in range(NL)], g, NL)
            for l in range(NL):
                r = res[l] - dgs[l, g] * ts_old[l][g]
                if l == 0:
                    r = r + srs[g]
                rs[l][g] = r
                e1s[l][g] = wgs[l, g] * r
        edge_terms(e1s, cf_e)

    for c in started:
        c.wait_send()


def hand_over(a, b, to_a, to_b, sem):
    copies = [
        pltpu.make_async_copy(a.at[l], to_a.at[l], sem.at[l]) for l in range(NL)
    ] + [pltpu.make_async_copy(b, to_b, sem.at[NL])]
    for c in copies:
        c.start()
    for c in copies:
        c.wait()


def n_copies(nx, ny):
    setup = (ny - 1) + 2 + 6 + 2 + (nx - 1) + 8 + 8
    return setup + OUTER * INNER * 8 + 3 * (nx - 1 + ny - 1)


def solution(mesh):
    nx, ny = mesh.shape["gx"], mesh.shape["gy"]
    its = OUTER * INNER
    devices = nx * ny

    def step(material, material_table, sink_cond, drain_current, instance_tile, instance_power):
        n_inst = instance_tile.shape[0]
        field = pltpu.VMEM((NL, 2, NR, LN), F32)
        single = pltpu.VMEM((2, NR, LN), F32)
        vm = lambda *shape: pltpu.VMEM(shape, F32)
        half = lambda *shape: pltpu.VMEM(shape, BF16)
        copies = n_copies(nx, ny)
        scratch = [
            pltpu.VMEM((NL, N, N), jnp.int32), vm(N, N), vm(N, N),
            pltpu.SMEM((2, 16), F32), pltpu.VMEM((n_inst // LN, LN), jnp.int32), vm(n_inst // LN, LN),
            field, field, field, field, field, pltpu.VMEM((NL - 1, 2, NR, LN), F32), field, field,
            single, single, single, field, field, field,
            vm(SL, LN), vm(SL, LN), vm(SL, LN), vm(64, 8 * LN), vm(64, 8 * LN), vm(SL, LN),
            half(8 * LN, LN), half(8 * LN, LN),
            half(devices, n_inst), half(3, 64, n_inst), vm(devices, LN), vm(devices, LN),
            vm(nx, ny, LN), vm(devices, LN), half(32, 32 * devices), half(3, 32, 32 * devices),
            vm(8, LN), vm(8, 8, LN), vm(2, 48, LN),
            vm(2, NQ, 2, 8, LN), vm(2, NQ, 2, 8, LN), vm(2, 8, LN), vm(6, 8, LN),
            vm(2, 8 * NQ, SL), vm(2, 8 * NQ, SL),
            vm(NL, 2, 16, SL), vm(NL, 2, 16, SL), vm(NL - 1, 2, 16, SL), vm(NL, 2, 16, SL), vm(NL, 2, 16, SL),
            vm(2, 16, SL), vm(2, 16, SL), vm(2, 16, SL), vm(2, 16, SL), single, pltpu.VMEM((2, 2, NR, LN), F32),
            vm(5, 8, LN), vm(8, 5, 8, LN), vm(7, 24, LN), vm(its, 8, LN), vm(its, 8, 8, LN),
            vm(3, 3, 8, LN), vm(3, nx - 1, 3, 8, LN), vm(3, 3, 8, LN), vm(3, ny - 1, 3, 8, LN),
            vm(NL, 2, 24, LN), vm(NL, 2, 24, LN), vm(NL, 2, 24, LN), vm(LN, LN),
            pltpu.SemaphoreType.DMA((copies,)), pltpu.SemaphoreType.DMA((copies,)), pltpu.SemaphoreType.DMA((6,)),
        ]
        vmem = pl.BlockSpec(memory_space=pltpu.VMEM)
        hbm = pl.BlockSpec(memory_space=pltpu.HBM)
        shapes = (jax.ShapeDtypeStruct((NL, N, N), F32), jax.ShapeDtypeStruct((N, N), F32))
        inside = (vm(NL, N, N), vm(N, N))
        results = pl.pallas_call(
            functools.partial(kernel, nx, ny),
            out_shape=inside,
            in_specs=[hbm] * 6,
            out_specs=(vmem, vmem),
            scratch_shapes=scratch,
            compiler_params=pltpu.CompilerParams(
                collective_id=0, has_side_effects=True, vmem_limit_bytes=56 * 1024 * 1024
            ),
        )(
            material,
            material_table,
            sink_cond,
            drain_current,
            instance_tile.reshape(n_inst // LN, LN),
            instance_power.reshape(n_inst // LN, LN),
        )
        return pl.pallas_call(
            hand_over,
            out_shape=shapes,
            in_specs=[pl.BlockSpec(memory_space=pl.ANY)] * 2,
            out_specs=(hbm, hbm),
            compiler_params=pltpu.CompilerParams(vmem_limit_bytes=1024 * 1024),
            scratch_shapes=[pltpu.SemaphoreType.DMA((NL + 1,))],
        )(*results)

    return jax.shard_map(
        step,
        mesh=mesh,
        in_specs=(
            P(None, "gx", "gy"),
            P(),
            P("gx", "gy"),
            P("gx", "gy"),
            P(("gx", "gy")),
            P(("gx", "gy")),
        ),
        out_specs=(P(None, "gx", "gy"), P("gx", "gy")),
        check_vma=False,
    )
```

```python
import functools

import jax
import jax.numpy as jnp
from jax import lax
from jax.experimental import pallas as pl
from jax.experimental.pallas import tpu as pltpu
from jax.sharding import PartitionSpec as P

MESH = pl.DeviceIdType.MESH
F32 = jnp.float32
BF16 = jnp.bfloat16

NL = 4
N = 256
LN = 128
RO = 16
NR = N + 2 * RO
NQ = 6
SL = 384
SO = 64
OUTER = 2
INNER = 2
CJ = 8
DAMPING = 0.8
DRAIN_SLOPE = 0.5
FACE_FLOOR = 0.5
BALANCE_WEIGHT = 0.5
DIRS = ((-1, -1), (-1, 0), (-1, 1), (0, -1), (0, 1), (1, -1), (1, 0), (1, 1))
DIAG = tuple(d for d in DIRS if d[0] and d[1])
OFF_LINE = tuple(d for d in DIRS if d[1])


def iota(shape, dim):
    return lax.broadcasted_iota(jnp.int32, shape, dim)


def harmonic(a, b):
    return 2.0 * a * b / jnp.maximum(a + b, FACE_FLOOR)


def shift(x, amount, axis):
    return pltpu.roll(x, amount % x.shape[axis], axis)


def lookup(ids, table):
    level = list(table)
    for bit in range(4):
        odd = ((ids >> bit) & 1) == 1
        level = [jnp.where(odd, level[2 * k + 1], level[2 * k]) for k in range(len(level) // 2)]
    return level[0]


def exact_dot(a, b):
    return lax.dot_general(
        a, b, (((1,), (0,)), ((), ())), precision=lax.Precision.HIGHEST, preferred_element_type=F32
    )


def pieces(x, count):
    out = []
    for _ in range(count - 1):
        part = x.astype(BF16)
        out.append(part)
        x = x - part.astype(F32)
    return out + [x.astype(BF16)]


def pick_dot(x, ones):
    return sum(jnp.dot(part, ones, preferred_element_type=F32) for part in pieces(x, 3))


class Layout:
    def __init__(self):
        self.count = 0

    def take(self):
        self.count += 1
        return self.count - 1


def kernel(nx, ny, *refs):
    (mat_hbm, tab_hbm, sink_hbm, drain_hbm, tile_hbm, power_hbm, out, dyn_out) = refs[:8]
    (
        mat, sink, drain, tab, inst_tile, inst_power,
        lat, ver, fr, fc, fl, fv, dg, wg, src, drn, snk, t_, r_, e1_,
        cf_t, cf_e, cf_f, acc, acc_n, pk, cb, cbn,
        dest, slots, sout, tin1, tred, tin2, dense_a, dense_b, ts, th, dynr,
        sq_row, rq_row, sq_c, rq_c, sq_s, rq_s,
        fcs, frs, fvs, dgs, wgs, drn_s, dys, srs, sks, gs, gr,
        cm, cmr, coef, ct, nb, s1, ls1, s2, ls2, cv, cvr, cvl, xt,
        ssem, rsem, lsem,
    ) = refs[8:]
    mx, my = lax.axis_index("gx"), lax.axis_index("gy")

    def at(dx, dy):
        return {"gx": lax.rem(mx + (dx + nx), nx), "gy": lax.rem(my + (dy + ny), ny)}

    fetch_small = [
        pltpu.make_async_copy(a, b, lsem.at[3 + k])
        for k, (a, b) in enumerate(((tile_hbm, inst_tile), (power_hbm, inst_power), (tab_hbm, tab)))
    ]
    for c in fetch_small:
        c.start()

    partners = [(d, 0) for d in range(1, nx)] + [(0, d) for d in range(1, ny)] + list(DIAG)
    barrier = pltpu.get_barrier_semaphore()
    for d in partners:
        pl.semaphore_signal(barrier, inc=1, device_id=at(*d), device_id_type=MESH)

    fetch = [
        pltpu.make_async_copy(a, b, lsem.at[k])
        for k, (a, b) in enumerate(((mat_hbm, mat), (sink_hbm, sink), (drain_hbm, drain)))
    ]
    for c in fetch:
        c.start()

    numbers = Layout()
    started = []

    def send(a, b, to):
        k = numbers.take()
        copy = pltpu.make_async_remote_copy(
            src_ref=a, dst_ref=b, send_sem=ssem.at[k], recv_sem=rsem.at[k],
            device_id=at(*to), device_id_type=MESH,
        )
        copy.start()
        started.append(copy)
        return copy

    lane8 = iota((8, LN), 1)
    first_lane = lane8 == 0
    last_lane = lane8 == LN - 1
    low_half = lane8 < LN // 2

    devices = nx * ny
    chunks = inst_tile.shape[0]
    for c in fetch_small:
        c.wait()
    sub_d = iota((devices, LN), 0)
    lane_d = iota((devices, LN), 1)
    up_to = jnp.where(iota((LN, LN), 0) <= iota((LN, LN), 1), 1.0, 0.0).astype(BF16)
    for k in range(chunks):
        s = inst_tile[k : k + 1, :] >> 10
        owner = (s % ny) * nx + s // ny
        dest[:, k * LN : (k + 1) * LN] = jnp.where(sub_d == owner, 1.0, 0.0).astype(BF16)
    before = jnp.zeros((devices, LN), F32)
    all_ones = jnp.ones((LN, LN), BF16)
    slot_row = iota((64, LN), 0)
    for k in range(chunks):
        span = slice(k * LN, (k + 1) * LN)
        d = dest[:, span]
        within = jnp.dot(d, up_to, preferred_element_type=F32)
        rank = jnp.sum(d.astype(F32) * (within + before), axis=0, keepdims=True)
        before = before + jnp.dot(d, all_ones, preferred_element_type=F32)
        at_slot = (slot_row & 31) == rank.astype(jnp.int32) - 1
        t = inst_tile[k : k + 1, :]
        ids = ((t & 992).astype(F32), (t & 31).astype(F32), jnp.zeros((1, LN), F32))
        for q, part in enumerate(pieces(inst_power[k : k + 1, :], 3)):
            value = jnp.where(slot_row < 32, part.astype(F32), ids[q])
            slots[q, :, span] = jnp.where(at_slot, value, 0.0).astype(BF16)
    total = None
    for q in range(3):
        term = lax.dot_general(
            dest[...], slots[q], (((1,), (1,)), ((), ())), preferred_element_type=F32
        )
        total = term if total is None else total + term
    sout[...] = jnp.concatenate([total, jnp.zeros((devices, LN - 64), F32)], axis=1)
    power_sum = jnp.zeros((8, LN), F32)
    for k in range(chunks // 8):
        power_sum = power_sum + inst_power[8 * k : 8 * k + 8, :]

    def bundle(j):
        return sout.at[pl.ds(pl.multiple_of(j * nx, nx), nx), :]

    pl.semaphore_wait(barrier, len(partners))
    tile_in = []
    for d in range(1, ny):
        tile_in.append(send(bundle(lax.rem(my + d, ny)), tin1.at[pl.ds(d * nx, nx)], (0, d)))
    tin1[0:nx, :] = bundle(my)[...]

    def pack(values):
        packed = jnp.zeros((8, LN), F32)
        for q, (a, b) in enumerate(values):
            both = shift(jnp.where(low_half, a, b), 16 * q + 8, 1)
            packed = jnp.where((lane8 >> 4) == q, both, packed)
        return packed

    halves = (slice(0, LN), slice(LN, N))

    def raw(rows):
        mats = [tuple(mat[l, rows, h].astype(F32) for h in halves) for l in range(NL)]
        return mats + [tuple(a[rows, h] for h in halves) for a in (sink, drain)]

    for c in fetch:
        c.wait()
    for side, rows in enumerate((slice(0, 8), slice(N - 8, N))):
        values = raw(rows)
        for q, (a, b) in enumerate(values):
            sq_row[side, q, 0] = a
            sq_row[side, q, 1] = b
        sq_c[side] = pack(values)
    margin_row = [send(sq_row.at[s], rq_row.at[s], (2 * s - 1, 0)) for s in range(2)]
    corner_dirs = ((-1, 0), (1, 0)) + DIAG
    margin_c = {
        d: (k, send(sq_c.at[0 if d[0] < 0 else 1], rq_c.at[k], d)) for k, d in enumerate(corner_dirs)
    }

    @pl.loop(0, N // 32)
    def _(a):
        for k in range(4):
            rows = pl.ds(pl.multiple_of(a * 32 + k * 8, 8), 8)
            pk[pl.ds(pl.multiple_of(a * 32 + k * 8 + SO, 8), 8), :] = pack(raw(rows))

    pk[0:SO, :] = jnp.zeros((SO, LN), F32)
    pk[SO + N :, :] = jnp.zeros((SL - N - SO, LN), F32)
    for k in range(SL // LN):
        span = slice(k * LN, (k + 1) * LN)
        block = pk[span, :].T
        for q in range(NQ):
            sq_s[0, 8 * q : 8 * q + 8, span] = block[16 * q + 8 : 16 * q + 16, :]
            sq_s[1, 8 * q : 8 * q + 8, span] = block[16 * q : 16 * q + 8, :]
    margin_we = [send(sq_s.at[s], rq_s.at[s], (0, 2 * s - 1)) for s in range(2)]

    col_n = iota((LN, LN), 1)
    row_n = iota((LN, LN), 0)
    for l in range(NL):
        for h in range(2):
            span = pl.ds((2 * l + h) * LN, LN)
            goal = l * 32 + 8 + h * 4 + (row_n >> 5)
            cb[span, :] = jnp.where(col_n == goal, 1.0, 0.0).astype(BF16)
            hit = ((row_n & 31) == 31) & (col_n == goal)
            if h == 0:
                hit = hit | ((row_n == 0) & (col_n == l * 32 + 7))
            cbn[span, :] = jnp.where(hit, 1.0, 0.0).astype(BF16)
    table = [[tab[q, k] for k in range(16)] for q in range(2)]

    zero8 = jnp.zeros((8, LN), F32)
    for ref, places in ((t_, (0, NR - 8)), (e1_, (0, 8, NR - 16, NR - 8)), (fr, (0,)), (lat, (NR - 16, NR - 8))):
        for l in range(NL):
            for h in range(2):
                for place in places:
                    ref[l, h, place : place + 8, :] = zero8

    @pl.loop(0, N // 32, init_carry=power_sum)
    def source_sum(a, source_sum):
        for k in range(4):
            rows = pl.ds(pl.multiple_of(a * 32 + k * 8, 8), 8)
            into = pl.ds(pl.multiple_of(a * 32 + k * 8 + RO, 8), 8)
            for h in range(2):
                for l in range(NL):
                    ids = mat[l, rows, halves[h]]
                    lat[l, h, into, :] = lookup(ids, table[0])
                    ver[l, h, into, :] = lookup(ids, table[1])
                snk[h, into, :] = sink[rows, halves[h]]
                d = drain[rows, halves[h]]
                drn[h, into, :] = d
                source_sum = source_sum + d
        return source_sum

    def row_faces(base):
        here, below = pl.ds(base, 8), pl.ds(base + 1, 8)
        for l in range(NL):
            for h in range(2):
                fr[l, h, here, :] = harmonic(lat[l, h, here, :], lat[l, h, below, :])

    def layer_faces(base, sums):
        here = pl.ds(base, 8)
        for h in range(2):
            vs = [ver[l, h, here, :] for l in range(NL)]
            for l in range(NL):
                if l < NL - 1:
                    v = harmonic(vs[l], vs[l + 1])
                    fv[l, h, here, :] = v
                else:
                    v = snk[h, here, :]
                if sums is not None:
                    sums[2 * l + h] += v

    @pl.loop(0, N // 32)
    def _(a):
        sums = [zero8] * 8
        for k in range(4):
            base = pl.multiple_of(RO + 32 * a + 8 * k, 8)
            row_faces(base)
            layer_faces(base, sums)
        rows = pl.ds(pl.multiple_of(a * 8, 8), 8)
        for q in range(8):
            acc[rows, q * LN : (q + 1) * LN] = sums[q]

    for c in tile_in:
        c.wait_recv()
    for x in range(nx):
        tred[x] = tin1[pl.ds(x, ny, stride=nx), :]
    tile_in2 = []
    for d in range(1, nx):
        x = lax.rem(mx + d, nx)
        tile_in2.append(send(tred.at[x], tin2.at[pl.ds(d * ny, ny)], (d, 0)))
    tin2[0:ny, :] = tred[mx]

    edge_n = jnp.where(mx == 0, 0.0, 1.0)
    edge_s = jnp.where(mx == nx - 1, 0.0, 1.0)
    edge_w = jnp.where(my == 0, 0.0, 1.0)
    edge_e = jnp.where(my == ny - 1, 0.0, 1.0)
    for c in margin_row:
        c.wait_recv()
    for slot, base, keep in ((1, RO - 8, edge_n), (0, RO + N, edge_s)):
        rows = slice(base, base + 8)
        for h in range(2):
            for l in range(NL):
                ids = rq_row[slot, l, h].astype(jnp.int32)
                lat[l, h, rows, :] = lookup(ids, table[0]) * keep
                ver[l, h, rows, :] = lookup(ids, table[1]) * keep
            snk[h, rows, :] = rq_row[slot, 4, h] * keep
            drn[h, rows, :] = rq_row[slot, 5, h] * keep
    for c in margin_we:
        c.wait_recv()
    for _, c in margin_c.values():
        c.wait_recv()

    def corner_block(dy):
        top, low = (rq_c[margin_c[(-dx, -dy)][0]] for dx in (-1, 1))
        pad = jnp.zeros((SO - 8, LN), F32)
        return jnp.concatenate([pad, top, low, pad], axis=0).T

    blocks = {dy: corner_block(dy) for dy in (-1, 0, 1)}

    def merge(body, corners):
        return jnp.concatenate(
            [
                jnp.where((lane8 >> 3) == SO // 8 - 1, corners, body[:, :LN]),
                body[:, LN : 2 * LN],
                jnp.where((lane8 >> 3) == SO // 8, corners, body[:, 2 * LN :]),
            ],
            axis=1,
        )

    def raw_strip(q, side):
        own, got = slice(8 * q, 8 * q + 8), slice(16 * q, 16 * q + 16)
        if side == 0:
            outside = merge(rq_s[1, own, :], blocks[-1][got, :][0:8, :])
            inside = merge(sq_s[0, own, :], blocks[0][got, :][8:16, :])
            return jnp.concatenate([outside, inside], axis=0)
        outside = merge(rq_s[0, own, :], blocks[1][got, :][8:16, :])
        inside = merge(sq_s[1, own, :], blocks[0][got, :][0:8, :])
        return jnp.concatenate([inside, outside], axis=0)

    sl_lane = iota((16, SL), 1)
    sl_row = iota((16, SL), 0)
    one = jnp.ones((16, SL), F32)
    keep_rows = jnp.where(sl_lane < SO, one * edge_n, jnp.where(sl_lane >= SO + N, one * edge_s, one))
    keep = (
        keep_rows * jnp.where(sl_row < 8, one * edge_w, one),
        keep_rows * jnp.where(sl_row >= 8, one * edge_e, one),
    )
    sides = range(2)
    for g in sides:
        lats, vers = [], []
        for l in range(NL):
            ids = raw_strip(l, g).astype(jnp.int32)
            lats.append(lookup(ids, table[0]) * keep[g])
            vers.append(lookup(ids, table[1]) * keep[g])
        sink_s = raw_strip(4, g) * keep[g]
        sks[g] = sink_s
        drn_s[g] = raw_strip(5, g) * keep[g]
        up = None
        for l in range(NL):
            c = harmonic(lats[l], shift(lats[l], -1, 0))
            r = harmonic(lats[l], shift(lats[l], -1, 1))
            fcs[l, g] = c
            frs[l, g] = r
            d = c + shift(c, 1, 0) + r + shift(r, 1, 1)
            if l > 0:
                d = d + up
            if l < NL - 1:
                up = harmonic(vers[l], vers[l + 1])
                fvs[l, g] = up
                d = d + up
            else:
                d = d + sink_s
            d = jnp.maximum(d, FACE_FLOOR)
            dgs[l, g] = d
            wgs[l, g] = DAMPING / d

    row_z = iota((8, SL), 0)

    def column_form(west, east, ref):
        z = jnp.zeros((8, SL), F32)
        for l in range(NL):
            if west[l] is not None:
                z = jnp.where(row_z == 2 * l + 1, west[l], jnp.where(row_z == 2 * l, east[l], z))
        for k in range(SL // LN):
            block = jnp.concatenate([z[:, k * LN : (k + 1) * LN], jnp.zeros((LN - 8, LN), F32)], axis=0)
            ref[k * LN : (k + 1) * LN, :] = block.T

    def columns(ref, base):
        tile = ref[pl.ds(base + (SO - RO), 8), :]
        return [shift(tile, -(2 * l + 1), 1) for l in range(NL)]

    def edge_terms(v, ref):
        column_form(
            [(fcs[l, 0] * v[l][0])[7:8, :] for l in range(NL)],
            [fcs[l, 1][7:8, :] * v[l][1][8:9, :] for l in range(NL)],
            ref,
        )

    column_form([fcs[l, 0, 7:8, :] for l in range(NL)], [fcs[l, 1, 7:8, :] for l in range(NL)], cf_f)

    def column_faces(base, sums):
        bf = columns(cf_f, base)
        here = pl.ds(base, 8)
        for l in range(NL):
            a0, a1 = lat[l, 0, here, :], lat[l, 1, here, :]
            ra0, ra1 = shift(a0, -1, 1), shift(a1, -1, 1)
            c0 = harmonic(a0, jnp.where(last_lane, ra1, ra0))
            c1 = jnp.where(last_lane, bf[l], harmonic(a1, ra1))
            rc0, rc1 = shift(c0, 1, 1), shift(c1, 1, 1)
            fc[l, 0, here, :] = c0
            fc[l, 1, here, :] = c1
            fl[l, 0, here, :] = jnp.where(first_lane, bf[l], rc0)
            fl[l, 1, here, :] = jnp.where(first_lane, rc0, rc1)
            if sums is not None:
                sums[2 * l] += jnp.where(first_lane, bf[l], c0)
                sums[2 * l + 1] += c1

    for base in (RO - 8, RO + N):
        column_faces(base, None)
        row_faces(base)
        layer_faces(base, None)
    row_faces(RO + N - 8)

    @pl.loop(0, N // 64)
    def _(pair):
        for a in (2 * pair, 2 * pair + 1):
            sums = [zero8] * 8
            for k in range(4):
                column_faces(pl.multiple_of(RO + 32 * a + 8 * k, 8), sums)
            rows = pl.ds(pl.multiple_of(a * 8, 8), 8)
            for q in range(8):
                acc_n[rows, q * LN : (q + 1) * LN] = sums[q]

    block_lane = lane8 & 31
    own_block = (block_lane >= 8) & (block_lane < 16)

    def block_rows(x):
        return x.reshape(8, 8, LN).sum(axis=1)

    def edge_sums(start):
        rows = [fr[l, h, pl.ds(start, 8, stride=32), :] for l in range(NL) for h in range(2)]
        return pick_dot(jnp.concatenate(rows, axis=1), cb[...])

    c_east = edge_sums(RO + 31)
    c_east_prev = edge_sums(RO - 1)
    c_north_wide = block_rows(pick_dot(acc_n[...], cbn[...]))
    c_north = jnp.where(own_block, c_north_wide, 0.0)
    c_north_prev = jnp.where(own_block, shift(c_north_wide, 1, 1), 0.0)
    up_sink = block_rows(pick_dot(acc[...], cb[...]))
    c_up = jnp.where(lane8 < 96, up_sink, 0.0)
    c_sink = jnp.where(lane8 >= 96, up_sink, 0.0)
    c_diag = c_east + c_east_prev + c_north + c_north_prev + c_up + shift(c_up, 32, 1) + c_sink
    tile = zero8
    for q, x in enumerate((c_east, c_north, c_up + c_sink, c_diag)):
        tile = tile + shift(jnp.where(own_block, x, 0.0), 8 * q, 1)
    cm[...] = tile
    cm_in = {d: (k, send(cm, cmr.at[k], d)) for k, d in enumerate(DIRS)}

    sub8 = iota((8, LN), 0)

    def stack(*rows):
        out8 = zero8
        for k, x in enumerate(rows):
            out8 = jnp.where(sub8 == k, x, out8)
        return out8

    def sum_along_gx(it, *tiles):
        s1[it] = stack(*(x.sum(axis=0, keepdims=True) for x in tiles))
        return [send(s1.at[it], ls1.at[it, d - 1], (d, 0)) for d in range(1, nx)]

    def sum_along_gy(it, arriving):
        total = s1[it]
        for d in range(1, nx):
            arriving[d - 1].wait_recv()
            total = total + ls1[it, d - 1]
        s2[it] = total
        return [send(s2.at[it], ls2.at[it, d - 1], (0, d)) for d in range(1, ny)]

    def sum_end(it, arriving, parts):
        total = s2[it]
        for d in range(1, ny):
            arriving[d - 1].wait_recv()
            total = total + ls2[it, d - 1]
        total = total.sum(axis=1, keepdims=True)
        return [total[q : q + 1, :] for q in range(parts)]

    sums_gx = sum_along_gx(0, source_sum, c_diag, c_sink)

    for c in tile_in2:
        c.wait_recv()
    quarter = devices // 4
    lane_q = iota((quarter, LN), 1)
    power = jnp.zeros((quarter, LN), F32)
    ids = power
    for k in range(4):
        part = tin2[k * quarter : (k + 1) * quarter, :]
        mine = (lane_q >> 5) == k
        power = jnp.where(mine, shift(part, 32 * k, 1), power)
        ids = jnp.where(mine, shift(part, 32 * k - 32, 1), ids)
    ids = ids.astype(jnp.int32)
    powers = [part.astype(F32) for part in pieces(power, 3)]
    sub32 = iota((32, LN), 0)
    for k in range(quarter):
        span = slice(k * LN, (k + 1) * LN)
        one_id = ids[k : k + 1, :]
        dense_a[:, span] = jnp.where(sub32 == (one_id >> 5), 1.0, 0.0).astype(BF16)
        hit = sub32 == (one_id & 31)
        for q in range(3):
            dense_b[q, :, span] = jnp.where(hit, powers[q][k : k + 1, :], 0.0).astype(BF16)
    total = None
    for q in range(3):
        term = lax.dot_general(
            dense_a[...], dense_b[q], (((1,), (1,)), ((), ())), preferred_element_type=F32
        )
        total = term if total is None else total + term
    total = jnp.concatenate([total * (1.0 / 64.0), jnp.zeros((32, LN - 32), F32)], axis=1)
    total_t = jnp.concatenate([total, jnp.zeros((LN - 32, LN), F32)], axis=0).T
    ts[...] = stack(total_t[0:1, :], total_t[31:32, :], total[0:1, :], total[31:32, :])
    th_in = {d: (k, send(ts, th.at[k], d)) for k, d in enumerate(DIRS)}
    spread_cols = jnp.where(iota((LN, N), 0) == (iota((LN, N), 1) >> 3), 1.0, 0.0).astype(BF16)
    wide = pick_dot(total, spread_cols)
    for h in range(2):
        dynr[h, 8:40, :] = wide[:, halves[h]]

    def diagonal(base):
        here, above = pl.ds(base, 8), pl.ds(base - 1, 8)
        for l in range(NL):
            for h in range(2):
                d = fr[l, h, above, :] + fr[l, h, here, :] + fl[l, h, here, :] + fc[l, h, here, :]
                if l > 0:
                    d = d + fv[l - 1, h, here, :]
                if l < NL - 1:
                    d = d + fv[l, h, here, :]
                else:
                    d = d + snk[h, here, :]
                d = jnp.maximum(d, FACE_FLOOR)
                dg[l, h, here, :] = d
                wg[l, h, here, :] = DAMPING / d

    diagonal(RO - 8)
    diagonal(RO + N)

    @pl.loop(0, N // 32)
    def _(a):
        for k in range(4):
            diagonal(pl.multiple_of(RO + 32 * a + 8 * k, 8))

    def couple(ref, base, edge, live):
        here, above, below = pl.ds(base, 8), pl.ds(base - 1, 8), pl.ds(base + 1, 8)
        res = [[None, None] for _ in range(NL)]
        mid = [[ref[l, h, here, :] for h in range(2)] for l in range(live)]
        for l in range(live):
            a0, a1 = mid[l]
            f0, f1 = fc[l, 0, here, :], fc[l, 1, here, :]
            ra0, ra1 = shift(a0, -1, 1), shift(a1, -1, 1)
            p0, p1 = shift(f0 * a0, 1, 1), shift(f1 * a1, 1, 1)
            lateral = (
                f0 * jnp.where(last_lane, ra1, ra0) + jnp.where(first_lane, edge[l], p0),
                jnp.where(last_lane, edge[l], f1 * ra1) + jnp.where(first_lane, p0, p1),
            )
            for h in range(2):
                res[l][h] = (
                    lateral[h]
                    + fr[l, h, above, :] * ref[l, h, above, :]
                    + fr[l, h, here, :] * ref[l, h, below, :]
                )
        for l in range(live):
            for h in range(2):
                for face, to in ((l - 1, l - 1), (l, l + 1)):
                    if 0 <= to < NL:
                        term = fv[face, h, here, :] * mid[l][h]
                        res[to][h] = term if res[to][h] is None else res[to][h] + term
        return mid, res

    def strip_couple(v, g, live):
        res = []
        for l in range(live):
            p, r = fcs[l, g] * v[l], frs[l, g]
            res.append(
                fcs[l, g] * shift(v[l], -1, 0) + shift(p, 1, 0) + r * shift(v[l], -1, 1) + shift(r * v[l], 1, 1)
            )
        res += [None] * (NL - live)
        for l in range(live):
            for face, to in ((l - 1, l - 1), (l, l + 1)):
                if 0 <= to < NL:
                    term = fvs[face, g] * v[l]
                    res[to] = term if res[to] is None else res[to] + term
        return res

    def dyn_rows(base, h):
        return dynr[h, pl.ds(base // 8 + 6, 1), :]

    def over_rows(body, margins=True, carry=None):
        if margins:
            body(RO - 8, None, -1, 3)
            body(RO + N, None, 8, 0)

        @pl.loop(0, N // 128)
        def _(pair):
            for a in (4 * pair, 4 * pair + 1, 4 * pair + 2, 4 * pair + 3):
                sums = [zero8] * 8
                for k in range(4):
                    body(pl.multiple_of(RO + 32 * a + 8 * k, 8), sums, a, k)
                rows = pl.ds(pl.multiple_of(a * 8, 8), 8)
                for q in range(8):
                    if sums[q] is not zero8:
                        acc[rows, q * LN : (q + 1) * LN] = sums[q]

    lane16 = iota((16, LN), 1)
    lane24 = iota((24, LN), 1)

    def sweep_neighbours(x):
        lanes = [shift(x, by, 1) for by in (-1, 1, -32, 32)]
        rows = coef[1] * shift(x, -1, 0) + coef[2] * shift(x, 1, 0)
        return rows, (coef[3] * lanes[0] + coef[4] * lanes[1]) + (coef[5] * lanes[2] + coef[6] * lanes[3])

    def coarse_sweeps(right):
        rw = coef[0] * right
        x = rw
        for _ in range(CJ - 1):
            rows, lanes = sweep_neighbours(x)
            x = ((1.0 - DAMPING) * x + rw + rows) + lanes
        return x

    def assemble(own, other):
        rows = []
        for dx in (-1, 0, 1):
            centre = own if dx == 0 else other((dx, 0))
            rows.append(centre + shift(other((dx, -1)), -8, 1) + shift(other((dx, 1)), 8, 1))
        return jnp.concatenate(rows, axis=0)

    def send_coarse(it, own):
        ct[it] = own
        return {d: (k, send(ct.at[it], nb.at[it, k], d)) for k, d in enumerate(DIRS)}

    def first_residual(base, sums, a, k):
        here = pl.ds(base, 8)
        for h in range(2):
            r = dyn_rows(base, h) + drn[h, here, :]
            src[h, here, :] = r
            r_[0, h, here, :] = r
            e1_[0, h, here, :] = wg[0, h, here, :] * r
            if sums is not None:
                sums[h] += r

    over_rows(first_residual, margins=False)
    own_c = block_rows(pick_dot(acc[:, 0 : 2 * LN], cb[0 : 2 * LN, :]))
    side = send_coarse(0, own_c)

    def second_sweep(base, live, edge, first):
        here = pl.ds(base, 8)
        mid, res = couple(e1_, base, edge, live)
        for l in range(NL):
            for h in range(2):
                if l < live:
                    u = (1.0 - DAMPING) * mid[l][h] + wg[l, h, here, :] * (r_[l, h, here, :] + res[l][h])
                elif res[l][h] is not None:
                    u = wg[l, h, here, :] * res[l][h]
                else:
                    u = zero8
                if not first:
                    u = u + t_[l, h, here, :]
                t_[l, h, here, :] = u

    over_rows(lambda base, sums, a, k: second_sweep(base, 1, [zero8], True), margins=False)

    snk_e1 = [wgs[NL - 1, g] * sks[g] for g in sides]
    column_form(
        [None] * (NL - 1) + [(fcs[NL - 1, 0] * snk_e1[0])[7:8, :]],
        [None] * (NL - 1) + [fcs[NL - 1, 1][7:8, :] * snk_e1[1][8:9, :]],
        cf_t,
    )

    def sink_first(base, sums, a, k):
        here = pl.ds(base, 8)
        for h in range(2):
            gs[h, here, :] = wg[NL - 1, h, here, :] * snk[h, here, :]

    over_rows(sink_first)

    def sink_second(base, sums, a, k):
        here, above, below = pl.ds(base, 8), pl.ds(base - 1, 8), pl.ds(base + 1, 8)
        top = NL - 1
        edge = columns(cf_t, base)[top]
        a0, a1 = gs[0, here, :], gs[1, here, :]
        f0, f1 = fc[top, 0, here, :], fc[top, 1, here, :]
        ra0, ra1 = shift(a0, -1, 1), shift(a1, -1, 1)
        p0, p1 = shift(f0 * a0, 1, 1), shift(f1 * a1, 1, 1)
        lateral = (
            f0 * jnp.where(last_lane, ra1, ra0) + jnp.where(first_lane, edge, p0),
            jnp.where(last_lane, edge, f1 * ra1) + jnp.where(first_lane, p0, p1),
        )
        for h, e in ((0, a0), (1, a1)):
            flow = (
                lateral[h]
                + fr[top, h, above, :] * gs[h, above, :]
                + fr[top, h, here, :] * gs[h, below, :]
            )
            gr[1, h, here, :] = (1.0 - DAMPING) * e + wg[top, h, here, :] * (snk[h, here, :] + flow)
            gr[0, h, here, :] = wg[top - 1, h, here, :] * (fv[top - 1, h, here, :] * e)

    over_rows(sink_second, margins=False)
    first_gy = sum_along_gy(0, sums_gx)

    for _, c in cm_in.values():
        c.wait_recv()
    def coupling(q):
        def of(tile):
            return jnp.where((lane8 >> 3) & 3 == (q + 1) % 4, tile, 0.0)

        rows = []
        for dx in (-1, 0, 1):
            tiles = [cm[...] if (dx, dy) == (0, 0) else cmr[cm_in[(-dx, -dy)][0]] for dy in (-1, 0, 1)]
            rows.append(sum(shift(of(tile), 8 * (dy - q), 1) for dy, tile in zip((-1, 0, 1), tiles, strict=True)))
        return jnp.concatenate(rows, axis=0)

    w_east, w_north, w_up, w_diag = (coupling(q) for q in range(4))
    w_sink = jnp.where(lane24 >= 96, w_up, 0.0)
    w_up = jnp.where(lane24 < 96, w_up, 0.0)
    gain = jnp.where((lane24 & 31) < 24, DAMPING / jnp.maximum(w_diag, 1e-30), 0.0)
    coef[0] = gain
    coef[1] = gain * w_east
    coef[2] = gain * shift(w_east, 1, 0)
    coef[3] = gain * w_north
    coef[4] = gain * shift(w_north, 1, 1)
    coef[5] = gain * w_up
    coef[6] = gain * shift(w_up, 32, 1)
    adjoint = coarse_sweeps(w_sink)
    own_adjoint = jnp.where(own_block, adjoint[8:16, :], 0.0)
    sums_gx = sum_along_gx(1, own_adjoint * own_c)

    @pl.loop(0, N // 32)
    def _(a):
        for k in range(4):
            for h in range(2):
                dyn_out[pl.ds(pl.multiple_of(a * 32 + k * 8, 8), 8), halves[h]] = jnp.broadcast_to(
                    dynr[h, pl.ds(8 + 4 * a + k, 1), :], (8, LN)
                )
    for _, c in th_in.values():
        c.wait_recv()

    def rim(d, k):
        return th[th_in[(-d[0], -d[1])][0], k : k + 1, :]

    wide_rims = pick_dot(stack(rim((-1, 0), 3) * edge_n, rim((1, 0), 2) * edge_s), spread_cols)
    for h in range(2):
        dynr[h, 0:8, :] = jnp.broadcast_to(wide_rims[0:1, halves[h]], (8, LN))
        dynr[h, 40:48, :] = jnp.broadcast_to(wide_rims[1:2, halves[h]], (8, LN))
    body = stack(rim((0, -1), 1), ts[0:1, :], ts[1:2, :], rim((0, 1), 0))
    top = stack(rim((-1, -1), 1), rim((-1, 0), 0), rim((-1, 0), 1), rim((-1, 1), 0))
    low = stack(rim((1, -1), 1), rim((1, 0), 0), rim((1, 0), 1), rim((1, 1), 0))
    tall = jnp.where(
        lane8 == 0,
        shift(top, -31, 1),
        jnp.where(lane8 == 33, shift(low, 33, 1), jnp.where(lane8 < 33, shift(body, 1, 1), 0.0)),
    )
    spread_rows = jnp.where(iota((LN, SL), 0) == ((iota((LN, SL), 1) - (SO - 8)) >> 3), 1.0, 0.0).astype(BF16)
    tall = pick_dot(tall, spread_rows)
    for g in sides:
        dyn_s = jnp.where(sl_row < 8, tall[2 * g : 2 * g + 1, :], tall[2 * g + 1 : 2 * g + 2, :]) * keep[g]
        dys[g] = dyn_s
        srs[g] = dyn_s + drn_s[g]
    first_residual(RO - 8, None, -1, 3)
    first_residual(RO + N, None, 8, 0)

    rs = [[srs[g] for g in sides]]
    e1s = [[wgs[0, g] * srs[g] for g in sides]]
    live = 1
    zeros_s = jnp.zeros((16, SL), F32)
    edge_terms(e1s + [[zeros_s, zeros_s]] * (NL - 1), cf_e)
    second_sweep(RO - 8, 1, columns(cf_e, RO - 8), True)
    second_sweep(RO + N, 1, columns(cf_e, RO + N), True)

    def over_edges(base, sums, a, k):
        here = pl.ds(base, 8)
        edge = columns(cf_e, base)[0]
        for h, lane in ((0, first_lane), (1, last_lane)):
            t_[0, h, here, :] = t_[0, h, here, :] + jnp.where(lane, wg[0, h, here, :] * edge, 0.0)

    over_rows(over_edges, margins=False)
    for h in range(2):
        for row, beyond, face in ((RO, RO - 1, RO - 1), (RO + N - 1, RO + N, RO + N - 1)):
            t_[0, h, row : row + 1, :] = t_[0, h, row : row + 1, :] + wg[0, h, row : row + 1, :] * (
                fr[0, h, face : face + 1, :] * e1_[0, h, beyond : beyond + 1, :]
            )

    ts_old = None
    former = diag_total = sink_total = source_total = None
    sweeps = OUTER * INNER
    for it in range(sweeps):
        first, last = it == 0, it == sweeps - 1
        fresh = (it + 1) % INNER == 0

        if not first:
            over_rows(
                lambda base, sums, a, k: second_sweep(base, NL, columns(cf_e, base), False), margins=not last
            )

        if not last:
            us = [[None, None] for _ in range(NL)]
            for g in sides:
                res = strip_couple([e1s[l][g] for l in range(live)], g, live)
                for l in range(NL):
                    if l < live:
                        u = (1.0 - DAMPING) * e1s[l][g] + wgs[l, g] * (rs[l][g] + res[l])
                    elif res[l] is not None:
                        u = wgs[l, g] * res[l]
                    else:
                        u = zeros_s
                    us[l][g] = u if first else ts_old[l][g] + u
            edge_terms(us, cf_t)

            held = 2 if first else NL
            def half_residual(base, sums, a, k):
                here = pl.ds(base, 8)
                mid, res = couple(t_, base, columns(cf_t, base), held)
                for l in range(NL):
                    for h in range(2):
                        r = zero8 if res[l][h] is None else res[l][h]
                        if l < held:
                            r = r - dg[l, h, here, :] * mid[l][h]
                        if l == 0 and not fresh:
                            r = r + src[h, here, :]
                        r_[l, h, here, :] = r
                        if sums is not None:
                            sums[2 * l + h] += r

            over_rows(half_residual)
            if it == 2:
                sums_gy = sum_along_gy(2, sums_gx)
            next_c = block_rows(pick_dot(acc[...], cb[...]))

        if last:
            for c in started[: -len(DIRS)]:
                c.wait_send()
        for _, c in side.values():
            c.wait_recv()
        x = coarse_sweeps(assemble(own_c, lambda d: nb[it, side[(-d[0], -d[1])][0]]))
        if it == 1:
            source_total = source_total - sum_end(1, sums_gy, 1)[0] - former * sink_total
            x = x + former * (1.0 - adjoint)
        elif last:
            source_total, less = sum_end(2, sums_gy, 2)
            former = BALANCE_WEIGHT * source_total / diag_total
            source_total = source_total - less - former * sink_total
            x = x + former * (1.0 - adjoint)
        if it % INNER == 1:
            x = x + BALANCE_WEIGHT * source_total / diag_total

        def send_next(total_c):
            moved = (x - sum(sweep_neighbours(x)) * (1.0 / DAMPING))[8:16, :] * c_diag
            own = total_c - jnp.where(own_block, moved, 0.0)
            return own, send_coarse(it + 1, own)

        if not last and not fresh:
            own_c, side = send_next(next_c)

        for l in range(NL):
            for h in range(2):
                at_col = l * 32 + 8 + h * 4
                cv[l, h] = jnp.take_along_axis(x, at_col + (lane24 >> 5), axis=1)
                if not last:
                    cvr[l, h] = jnp.take_along_axis(x, at_col + ((lane24 + 1) >> 5), axis=1)
                    cvl[l, h] = jnp.take_along_axis(x, at_col + ((lane24 - 1) >> 5), axis=1)

        if last:

            @pl.loop(0, N // 32)
            def _(a):
                for l in range(NL):
                    for h in range(2):
                        add = cv[l, h, pl.ds(8 + a, 1), :]
                        for k in range(4):
                            rows = pl.ds(pl.multiple_of(32 * a + 8 * k, 8), 8)
                            here = pl.ds(pl.multiple_of(RO + 32 * a + 8 * k, 8), 8)
                            u = t_[l, h, here, :] + add
                            if l >= NL - 2:
                                u = u - former * gr[l - (NL - 2), h, here, :]
                            out[l, rows, halves[h]] = u

            break

        if fresh:

            def new_source(base, sums, a, k):
                here = pl.ds(base, 8)
                for h in range(2):
                    u = t_[0, h, here, :] + cv[0, h, pl.ds(8 + a, 1), :]
                    s = dyn_rows(base, h) + drn[h, here, :] * jnp.exp(DRAIN_SLOPE * u)
                    src[h, here, :] = s
                    if sums is not None:
                        sums[h] += s

            over_rows(new_source)
            next_c = next_c + block_rows(pick_dot(acc[:, 0 : 2 * LN], cb[0 : 2 * LN, :]))
            own_c, side = send_next(next_c)
        if first:
            sums_gy = sum_along_gy(1, sums_gx)

        def whole_residual(base, sums, a, k):
            here, above = pl.ds(base, 8), pl.ds(base - 1, 8)
            block = pl.ds(8 + a, 1)
            xs = [[cv[l, h, block, :] for h in range(2)] for l in range(NL)]
            for h in range(2):
                flow = None
                for l in range(NL):
                    v = xs[l][h]
                    t_[l, h, here, :] = t_[l, h, here, :] + v
                    r = r_[l, h, here, :]
                    if l == 0 and fresh:
                        r = r + src[h, here, :]
                    r = r - fc[l, h, here, :] * (v - cvr[l, h, block, :])
                    r = r - fl[l, h, here, :] * (v - cvl[l, h, block, :])
                    if k == 0:
                        step = v - cv[l, h, pl.ds(7 + a, 1), :]
                        r = r - jnp.where(sub8 == 0, fr[l, h, above, :] * step, 0.0)
                    if k == 3:
                        step = v - cv[l, h, pl.ds(9 + a, 1), :]
                        r = r - jnp.where(sub8 == 7, fr[l, h, here, :] * step, 0.0)
                    if l > 0:
                        r = r + flow
                    if l < NL - 1:
                        flow = fv[l, h, here, :] * (v - xs[l + 1][h])
                        r = r - flow
                    else:
                        r = r - snk[h, here, :] * v
                    r_[l, h, here, :] = r
                    e1_[l, h, here, :] = wg[l, h, here, :] * r
                    if it == 1 and l >= NL - 2 and sums is not None:
                        sums[0] += gr[l - (NL - 2), h, here, :] * r

        over_rows(whole_residual)
        if it == 1:
            response = acc[0:8, 0:LN]
            for a in range(1, 8):
                response = response + acc[8 * a : 8 * a + 8, 0:LN]
            sums_gx = sum_along_gx(2, own_c, response + own_adjoint * own_c)

        xt[...] = jnp.concatenate([x, jnp.zeros((LN - 24, LN), F32)], axis=0).T
        picked = jnp.concatenate(
            [xt[l * 32 + c : l * 32 + c + 1, :] for l in range(NL) for c in (7, 8, 15, 16)], axis=0
        )
        picked = jnp.concatenate(
            [jnp.take_along_axis(picked, 6 + 4 * k + (lane16 >> 5), axis=1) for k in range(SL // LN)], axis=1
        )
        live = NL
        ts_old = [[None, None] for _ in range(NL)]
        rs = [[None, None] for _ in range(NL)]
        e1s = [[None, None] for _ in range(NL)]
        for g in sides:
            for l in range(NL):
                k = 4 * l + 2 * g
                ts_old[l][g] = us[l][g] + jnp.where(sl_row < 8, picked[k : k + 1, :], picked[k + 1 : k + 2, :])
            if fresh:
                srs[g] = dys[g] + drn_s[g] * jnp.exp(DRAIN_SLOPE * ts_old[0][g])
            res = strip_couple([ts_old[l][g] for l in range(NL)], g, NL)
            for l in range(NL):
                r = res[l] - dgs[l, g] * ts_old[l][g]
                if l == 0:
                    r = r + srs[g]
                rs[l][g] = r
                e1s[l][g] = wgs[l, g] * r
        if first:
            source_total, diag_total, sink_total = sum_end(0, first_gy, 3)
            former = BALANCE_WEIGHT * source_total / diag_total

            def sink_part(base, sums, a, k):
                here = pl.ds(base, 8)
                for h in range(2):
                    r = r_[NL - 1, h, here, :] - former * snk[h, here, :]
                    r_[NL - 1, h, here, :] = r
                    e1_[NL - 1, h, here, :] = wg[NL - 1, h, here, :] * r

            over_rows(sink_part)
            for g in sides:
                rs[NL - 1][g] = rs[NL - 1][g] - former * sks[g]
                e1s[NL - 1][g] = wgs[NL - 1, g] * rs[NL - 1][g]
        edge_terms(e1s, cf_e)

    for c in started[-len(DIRS) :]:
        c.wait_send()


def hand_over(a, b, to_a, to_b, sem):
    copies = [
        pltpu.make_async_copy(a.at[l], to_a.at[l], sem.at[l]) for l in range(NL)
    ] + [pltpu.make_async_copy(b, to_b, sem.at[NL])]
    for c in copies:
        c.start()
    for c in copies:
        c.wait()


def n_copies(nx, ny):
    setup = (ny - 1) + 2 + 6 + 2 + (nx - 1) + 8 + 8
    return setup + OUTER * INNER * 8 + 3 * (nx - 1 + ny - 1)


def solution(mesh):
    nx, ny = mesh.shape["gx"], mesh.shape["gy"]
    its = OUTER * INNER
    devices = nx * ny

    def step(material, material_table, sink_cond, drain_current, instance_tile, instance_power):
        n_inst = instance_tile.shape[0]
        field = pltpu.VMEM((NL, 2, NR, LN), F32)
        single = pltpu.VMEM((2, NR, LN), F32)
        vm = lambda *shape: pltpu.VMEM(shape, F32)
        half = lambda *shape: pltpu.VMEM(shape, BF16)
        copies = n_copies(nx, ny)
        scratch = [
            pltpu.VMEM((NL, N, N), jnp.int32), vm(N, N), vm(N, N),
            pltpu.SMEM((2, 16), F32), pltpu.VMEM((n_inst // LN, LN), jnp.int32), vm(n_inst // LN, LN),
            field, field, field, field, field, pltpu.VMEM((NL - 1, 2, NR, LN), F32), field, field,
            single, single, single, field, field, field,
            vm(SL, LN), vm(SL, LN), vm(SL, LN), vm(64, 8 * LN), vm(64, 8 * LN), vm(SL, LN),
            half(8 * LN, LN), half(8 * LN, LN),
            half(devices, n_inst), half(3, 64, n_inst), vm(devices, LN), vm(devices, LN),
            vm(nx, ny, LN), vm(devices, LN), half(32, 32 * devices), half(3, 32, 32 * devices),
            vm(8, LN), vm(8, 8, LN), vm(2, 48, LN),
            vm(2, NQ, 2, 8, LN), vm(2, NQ, 2, 8, LN), vm(2, 8, LN), vm(6, 8, LN),
            vm(2, 8 * NQ, SL), vm(2, 8 * NQ, SL),
            vm(NL, 2, 16, SL), vm(NL, 2, 16, SL), vm(NL - 1, 2, 16, SL), vm(NL, 2, 16, SL), vm(NL, 2, 16, SL),
            vm(2, 16, SL), vm(2, 16, SL), vm(2, 16, SL), vm(2, 16, SL), single, pltpu.VMEM((2, 2, NR, LN), F32),
            vm(8, LN), vm(8, 8, LN), vm(7, 24, LN), vm(its, 8, LN), vm(its, 8, 8, LN),
            vm(3, 8, LN), vm(3, nx - 1, 8, LN), vm(3, 8, LN), vm(3, ny - 1, 8, LN),
            vm(NL, 2, 24, LN), vm(NL, 2, 24, LN), vm(NL, 2, 24, LN), vm(LN, LN),
            pltpu.SemaphoreType.DMA((copies,)), pltpu.SemaphoreType.DMA((copies,)), pltpu.SemaphoreType.DMA((6,)),
        ]
        vmem = pl.BlockSpec(memory_space=pltpu.VMEM)
        hbm = pl.BlockSpec(memory_space=pltpu.HBM)
        shapes = (jax.ShapeDtypeStruct((NL, N, N), F32), jax.ShapeDtypeStruct((N, N), F32))
        inside = (vm(NL, N, N), vm(N, N))
        results = pl.pallas_call(
            functools.partial(kernel, nx, ny),
            out_shape=inside,
            in_specs=[hbm] * 6,
            out_specs=(vmem, vmem),
            scratch_shapes=scratch,
            compiler_params=pltpu.CompilerParams(
                collective_id=0, has_side_effects=True, vmem_limit_bytes=56 * 1024 * 1024
            ),
        )(
            material,
            material_table,
            sink_cond,
            drain_current,
            instance_tile.reshape(n_inst // LN, LN),
            instance_power.reshape(n_inst // LN, LN),
        )
        return pl.pallas_call(
            hand_over,
            out_shape=shapes,
            in_specs=[pl.BlockSpec(memory_space=pl.ANY)] * 2,
            out_specs=(hbm, hbm),
            compiler_params=pltpu.CompilerParams(vmem_limit_bytes=1024 * 1024),
            scratch_shapes=[pltpu.SemaphoreType.DMA((NL + 1,))],
        )(*results)

    return jax.shard_map(
        step,
        mesh=mesh,
        in_specs=(
            P(None, "gx", "gy"),
            P(),
            P("gx", "gy"),
            P("gx", "gy"),
            P(("gx", "gy")),
            P(("gx", "gy")),
        ),
        out_specs=(P(None, "gx", "gy"), P("gx", "gy")),
        check_vma=False,
    )
```

```python
import functools

import jax
import jax.numpy as jnp
from jax import lax
from jax.experimental import pallas as pl
from jax.experimental.pallas import tpu as pltpu
from jax.sharding import PartitionSpec as P

MESH = pl.DeviceIdType.MESH
F32 = jnp.float32
BF16 = jnp.bfloat16

NL = 4
N = 256
LN = 128
RO = 16
NR = N + 2 * RO
NQ = 6
SL = 384
SO = 64
OUTER = 2
INNER = 2
CJ = 8
DAMPING = 0.8
DRAIN_SLOPE = 0.5
FACE_FLOOR = 0.5
BALANCE_WEIGHT = 0.5
DIRS = ((-1, -1), (-1, 0), (-1, 1), (0, -1), (0, 1), (1, -1), (1, 0), (1, 1))
DIAG = tuple(d for d in DIRS if d[0] and d[1])
OFF_LINE = tuple(d for d in DIRS if d[1])


def iota(shape, dim):
    return lax.broadcasted_iota(jnp.int32, shape, dim)


def harmonic(a, b):
    return 2.0 * a * b / jnp.maximum(a + b, FACE_FLOOR)


def shift(x, amount, axis):
    return pltpu.roll(x, amount % x.shape[axis], axis)


def lookup(ids, table):
    level = list(table)
    for bit in range(4):
        odd = ((ids >> bit) & 1) == 1
        level = [jnp.where(odd, level[2 * k + 1], level[2 * k]) for k in range(len(level) // 2)]
    return level[0]


def exact_dot(a, b):
    return lax.dot_general(
        a, b, (((1,), (0,)), ((), ())), precision=lax.Precision.HIGHEST, preferred_element_type=F32
    )


def pieces(x, count):
    out = []
    for _ in range(count - 1):
        part = x.astype(BF16)
        out.append(part)
        x = x - part.astype(F32)
    return out + [x.astype(BF16)]


def pick_dot(x, ones):
    return sum(jnp.dot(part, ones, preferred_element_type=F32) for part in pieces(x, 3))


class Layout:
    def __init__(self):
        self.count = 0

    def take(self):
        self.count += 1
        return self.count - 1


def kernel(nx, ny, *refs):
    (mat_hbm, tab_hbm, sink_hbm, drain_hbm, tile_hbm, power_hbm, out, dyn_out) = refs[:8]
    (
        mat, sink, drain, tab, inst_tile, inst_power,
        lat, ver, fr, fc, fl, fv, dg, wg, src, drn, snk, t_, r_, e1_,
        cf_t, cf_e, cf_f, acc, acc_n, pk, cb, cbn,
        dest, slots, sout, tin1, tred, tin2, dense_a, dense_b, ts, th, dynr,
        sq_row, rq_row, sq_c, rq_c, sq_s, rq_s,
        fcs, frs, fvs, dgs, wgs, drn_s, dys, srs, sks, gs, gr,
        cm, cmr, coef, ct, nb, s1, ls1, s2, ls2, cv, cvr, cvl, xt,
        ssem, rsem, lsem,
    ) = refs[8:]
    mx, my = lax.axis_index("gx"), lax.axis_index("gy")

    def at(dx, dy):
        return {"gx": lax.rem(mx + (dx + nx), nx), "gy": lax.rem(my + (dy + ny), ny)}

    fetch_small = [
        pltpu.make_async_copy(a, b, lsem.at[3 + k])
        for k, (a, b) in enumerate(((tile_hbm, inst_tile), (power_hbm, inst_power), (tab_hbm, tab)))
    ]
    for c in fetch_small:
        c.start()

    partners = [(d, 0) for d in range(1, nx)] + [(0, d) for d in range(1, ny)] + list(DIAG)
    barrier = pltpu.get_barrier_semaphore()
    for d in partners:
        pl.semaphore_signal(barrier, inc=1, device_id=at(*d), device_id_type=MESH)

    fetch = [
        pltpu.make_async_copy(a, b, lsem.at[k])
        for k, (a, b) in enumerate(((mat_hbm, mat), (sink_hbm, sink), (drain_hbm, drain)))
    ]
    for c in fetch:
        c.start()

    numbers = Layout()
    started = []

    def send(a, b, to):
        k = numbers.take()
        copy = pltpu.make_async_remote_copy(
            src_ref=a, dst_ref=b, send_sem=ssem.at[k], recv_sem=rsem.at[k],
            device_id=at(*to), device_id_type=MESH,
        )
        copy.start()
        started.append(copy)
        return copy

    lane8 = iota((8, LN), 1)
    first_lane = lane8 == 0
    last_lane = lane8 == LN - 1
    low_half = lane8 < LN // 2

    devices = nx * ny
    chunks = inst_tile.shape[0]
    for c in fetch_small:
        c.wait()
    sub_d = iota((devices, LN), 0)
    lane_d = iota((devices, LN), 1)
    up_to = jnp.where(iota((LN, LN), 0) <= iota((LN, LN), 1), 1.0, 0.0).astype(BF16)
    for k in range(chunks):
        s = inst_tile[k : k + 1, :] >> 10
        owner = (s % ny) * nx + s // ny
        dest[:, k * LN : (k + 1) * LN] = jnp.where(sub_d == owner, 1.0, 0.0).astype(BF16)
    before = jnp.zeros((devices, LN), F32)
    all_ones = jnp.ones((LN, LN), BF16)
    slot_row = iota((64, LN), 0)
    for k in range(chunks):
        span = slice(k * LN, (k + 1) * LN)
        d = dest[:, span]
        within = jnp.dot(d, up_to, preferred_element_type=F32)
        rank = jnp.sum(d.astype(F32) * (within + before), axis=0, keepdims=True)
        before = before + jnp.dot(d, all_ones, preferred_element_type=F32)
        at_slot = (slot_row & 31) == rank.astype(jnp.int32) - 1
        t = inst_tile[k : k + 1, :]
        ids = ((t & 992).astype(F32), (t & 31).astype(F32), jnp.zeros((1, LN), F32))
        for q, part in enumerate(pieces(inst_power[k : k + 1, :], 3)):
            value = jnp.where(slot_row < 32, part.astype(F32), ids[q])
            slots[q, :, span] = jnp.where(at_slot, value, 0.0).astype(BF16)
    total = None
    for q in range(3):
        term = lax.dot_general(
            dest[...], slots[q], (((1,), (1,)), ((), ())), preferred_element_type=F32
        )
        total = term if total is None else total + term
    sout[...] = jnp.concatenate([total, jnp.zeros((devices, LN - 64), F32)], axis=1)
    power_sum = jnp.zeros((8, LN), F32)
    for k in range(chunks // 8):
        power_sum = power_sum + inst_power[8 * k : 8 * k + 8, :]

    def bundle(j):
        return sout.at[pl.ds(pl.multiple_of(j * nx, nx), nx), :]

    pl.semaphore_wait(barrier, len(partners))
    tile_in = []
    for d in range(1, ny):
        tile_in.append(send(bundle(lax.rem(my + d, ny)), tin1.at[pl.ds(d * nx, nx)], (0, d)))
    tin1[0:nx, :] = bundle(my)[...]

    def pack(values):
        packed = jnp.zeros((8, LN), F32)
        for q, (a, b) in enumerate(values):
            both = shift(jnp.where(low_half, a, b), 16 * q + 8, 1)
            packed = jnp.where((lane8 >> 4) == q, both, packed)
        return packed

    halves = (slice(0, LN), slice(LN, N))

    def raw(rows):
        mats = [tuple(mat[l, rows, h].astype(F32) for h in halves) for l in range(NL)]
        return mats + [tuple(a[rows, h] for h in halves) for a in (sink, drain)]

    for c in fetch:
        c.wait()
    for side, rows in enumerate((slice(0, 8), slice(N - 8, N))):
        values = raw(rows)
        for q, (a, b) in enumerate(values):
            sq_row[side, q, 0] = a
            sq_row[side, q, 1] = b
        sq_c[side] = pack(values)
    margin_row = [send(sq_row.at[s], rq_row.at[s], (2 * s - 1, 0)) for s in range(2)]
    corner_dirs = ((-1, 0), (1, 0)) + DIAG
    margin_c = {
        d: (k, send(sq_c.at[0 if d[0] < 0 else 1], rq_c.at[k], d)) for k, d in enumerate(corner_dirs)
    }

    @pl.loop(0, N // 32)
    def _(a):
        for k in range(4):
            rows = pl.ds(pl.multiple_of(a * 32 + k * 8, 8), 8)
            pk[pl.ds(pl.multiple_of(a * 32 + k * 8 + SO, 8), 8), :] = pack(raw(rows))

    pk[0:SO, :] = jnp.zeros((SO, LN), F32)
    pk[SO + N :, :] = jnp.zeros((SL - N - SO, LN), F32)
    for k in range(SL // LN):
        span = slice(k * LN, (k + 1) * LN)
        block = pk[span, :].T
        for q in range(NQ):
            sq_s[0, 8 * q : 8 * q + 8, span] = block[16 * q + 8 : 16 * q + 16, :]
            sq_s[1, 8 * q : 8 * q + 8, span] = block[16 * q : 16 * q + 8, :]
    margin_we = [send(sq_s.at[s], rq_s.at[s], (0, 2 * s - 1)) for s in range(2)]

    col_n = iota((LN, LN), 1)
    row_n = iota((LN, LN), 0)
    for l in range(NL):
        for h in range(2):
            span = pl.ds((2 * l + h) * LN, LN)
            goal = l * 32 + 8 + h * 4 + (row_n >> 5)
            cb[span, :] = jnp.where(col_n == goal, 1.0, 0.0).astype(BF16)
            hit = ((row_n & 31) == 31) & (col_n == goal)
            if h == 0:
                hit = hit | ((row_n == 0) & (col_n == l * 32 + 7))
            cbn[span, :] = jnp.where(hit, 1.0, 0.0).astype(BF16)
    table = [[tab[q, k] for k in range(16)] for q in range(2)]

    zero8 = jnp.zeros((8, LN), F32)
    for ref, places in ((t_, (0, NR - 8)), (e1_, (0, 8, NR - 16, NR - 8)), (fr, (0,)), (lat, (NR - 16, NR - 8))):
        for l in range(NL):
            for h in range(2):
                for place in places:
                    ref[l, h, place : place + 8, :] = zero8

    @pl.loop(0, N // 32, init_carry=power_sum)
    def source_sum(a, source_sum):
        for k in range(4):
            rows = pl.ds(pl.multiple_of(a * 32 + k * 8, 8), 8)
            into = pl.ds(pl.multiple_of(a * 32 + k * 8 + RO, 8), 8)
            for h in range(2):
                for l in range(NL):
                    ids = mat[l, rows, halves[h]]
                    lat[l, h, into, :] = lookup(ids, table[0])
                    ver[l, h, into, :] = lookup(ids, table[1])
                snk[h, into, :] = sink[rows, halves[h]]
                d = drain[rows, halves[h]]
                drn[h, into, :] = d
                source_sum = source_sum + d
        return source_sum

    def row_faces(base):
        here, below = pl.ds(base, 8), pl.ds(base + 1, 8)
        for l in range(NL):
            for h in range(2):
                fr[l, h, here, :] = harmonic(lat[l, h, here, :], lat[l, h, below, :])

    def layer_faces(base, sums):
        here = pl.ds(base, 8)
        for h in range(2):
            vs = [ver[l, h, here, :] for l in range(NL)]
            for l in range(NL):
                if l < NL - 1:
                    v = harmonic(vs[l], vs[l + 1])
                    fv[l, h, here, :] = v
                else:
                    v = snk[h, here, :]
                if sums is not None:
                    sums[2 * l + h] += v

    def column_faces(base, sums):
        here = pl.ds(base, 8)
        for l in range(NL):
            a0, a1 = lat[l, 0, here, :], lat[l, 1, here, :]
            ra0, ra1 = shift(a0, -1, 1), shift(a1, -1, 1)
            c0 = harmonic(a0, jnp.where(last_lane, ra1, ra0))
            c1 = harmonic(a1, ra1)
            rc0, rc1 = shift(c0, 1, 1), shift(c1, 1, 1)
            fc[l, 0, here, :] = c0
            fc[l, 1, here, :] = c1
            fl[l, 0, here, :] = rc0
            fl[l, 1, here, :] = jnp.where(first_lane, rc0, rc1)
            if sums is not None:
                sums[2 * l] += c0
                sums[2 * l + 1] += c1

    @pl.loop(0, N // 64)
    def _(pair):
        for a in (2 * pair, 2 * pair + 1):
            sums, sums_n = [zero8] * 8, [zero8] * 8
            for k in range(4):
                base = pl.multiple_of(RO + 32 * a + 8 * k, 8)
                row_faces(base)
                layer_faces(base, sums)
                column_faces(base, sums_n)
            rows = pl.ds(pl.multiple_of(a * 8, 8), 8)
            for q in range(8):
                acc[rows, q * LN : (q + 1) * LN] = sums[q]
                acc_n[rows, q * LN : (q + 1) * LN] = sums_n[q]

    for c in tile_in:
        c.wait_recv()
    for x in range(nx):
        tred[x] = tin1[pl.ds(x, ny, stride=nx), :]
    tile_in2 = []
    for d in range(1, nx):
        x = lax.rem(mx + d, nx)
        tile_in2.append(send(tred.at[x], tin2.at[pl.ds(d * ny, ny)], (d, 0)))
    tin2[0:ny, :] = tred[mx]

    edge_n = jnp.where(mx == 0, 0.0, 1.0)
    edge_s = jnp.where(mx == nx - 1, 0.0, 1.0)
    edge_w = jnp.where(my == 0, 0.0, 1.0)
    edge_e = jnp.where(my == ny - 1, 0.0, 1.0)
    for c in margin_row:
        c.wait_recv()
    for slot, base, keep in ((1, RO - 8, edge_n), (0, RO + N, edge_s)):
        rows = slice(base, base + 8)
        for h in range(2):
            for l in range(NL):
                ids = rq_row[slot, l, h].astype(jnp.int32)
                lat[l, h, rows, :] = lookup(ids, table[0]) * keep
                ver[l, h, rows, :] = lookup(ids, table[1]) * keep
            snk[h, rows, :] = rq_row[slot, 4, h] * keep
            drn[h, rows, :] = rq_row[slot, 5, h] * keep
    for c in margin_we:
        c.wait_recv()
    for _, c in margin_c.values():
        c.wait_recv()

    def corner_block(dy):
        top, low = (rq_c[margin_c[(-dx, -dy)][0]] for dx in (-1, 1))
        pad = jnp.zeros((SO - 8, LN), F32)
        return jnp.concatenate([pad, top, low, pad], axis=0).T

    blocks = {dy: corner_block(dy) for dy in (-1, 0, 1)}

    def merge(body, corners):
        return jnp.concatenate(
            [
                jnp.where((lane8 >> 3) == SO // 8 - 1, corners, body[:, :LN]),
                body[:, LN : 2 * LN],
                jnp.where((lane8 >> 3) == SO // 8, corners, body[:, 2 * LN :]),
            ],
            axis=1,
        )

    def raw_strip(q, side):
        own, got = slice(8 * q, 8 * q + 8), slice(16 * q, 16 * q + 16)
        if side == 0:
            outside = merge(rq_s[1, own, :], blocks[-1][got, :][0:8, :])
            inside = merge(sq_s[0, own, :], blocks[0][got, :][8:16, :])
            return jnp.concatenate([outside, inside], axis=0)
        outside = merge(rq_s[0, own, :], blocks[1][got, :][8:16, :])
        inside = merge(sq_s[1, own, :], blocks[0][got, :][0:8, :])
        return jnp.concatenate([inside, outside], axis=0)

    sl_lane = iota((16, SL), 1)
    sl_row = iota((16, SL), 0)
    one = jnp.ones((16, SL), F32)
    keep_rows = jnp.where(sl_lane < SO, one * edge_n, jnp.where(sl_lane >= SO + N, one * edge_s, one))
    keep = (
        keep_rows * jnp.where(sl_row < 8, one * edge_w, one),
        keep_rows * jnp.where(sl_row >= 8, one * edge_e, one),
    )
    sides = range(2)
    for g in sides:
        lats, vers = [], []
        for l in range(NL):
            ids = raw_strip(l, g).astype(jnp.int32)
            lats.append(lookup(ids, table[0]) * keep[g])
            vers.append(lookup(ids, table[1]) * keep[g])
        sink_s = raw_strip(4, g) * keep[g]
        sks[g] = sink_s
        drn_s[g] = raw_strip(5, g) * keep[g]
        up = None
        for l in range(NL):
            c = harmonic(lats[l], shift(lats[l], -1, 0))
            r = harmonic(lats[l], shift(lats[l], -1, 1))
            fcs[l, g] = c
            frs[l, g] = r
            d = c + shift(c, 1, 0) + r + shift(r, 1, 1)
            if l > 0:
                d = d + up
            if l < NL - 1:
                up = harmonic(vers[l], vers[l + 1])
                fvs[l, g] = up
                d = d + up
            else:
                d = d + sink_s
            d = jnp.maximum(d, FACE_FLOOR)
            dgs[l, g] = d
            wgs[l, g] = DAMPING / d

    row_z = iota((8, SL), 0)

    def column_form(west, east, ref):
        z = jnp.zeros((8, SL), F32)
        for l in range(NL):
            if west[l] is not None:
                z = jnp.where(row_z == 2 * l + 1, west[l], jnp.where(row_z == 2 * l, east[l], z))
        for k in range(SL // LN):
            block = jnp.concatenate([z[:, k * LN : (k + 1) * LN], jnp.zeros((LN - 8, LN), F32)], axis=0)
            ref[k * LN : (k + 1) * LN, :] = block.T

    def columns(ref, base):
        tile = ref[pl.ds(base + (SO - RO), 8), :]
        return [shift(tile, -(2 * l + 1), 1) for l in range(NL)]

    def edge_terms(v, ref):
        column_form(
            [(fcs[l, 0] * v[l][0])[7:8, :] for l in range(NL)],
            [fcs[l, 1][7:8, :] * v[l][1][8:9, :] for l in range(NL)],
            ref,
        )

    column_form([fcs[l, 0, 7:8, :] for l in range(NL)], [fcs[l, 1, 7:8, :] for l in range(NL)], cf_f)

    def edge_faces(base, sums):
        bf = columns(cf_f, base)
        here = pl.ds(base, 8)
        for l in range(NL):
            fc[l, 1, here, :] = jnp.where(last_lane, bf[l], fc[l, 1, here, :])
            fl[l, 0, here, :] = jnp.where(first_lane, bf[l], fl[l, 0, here, :])
            if sums is not None:
                sums[l] += bf[l]

    for base in (RO - 8, RO + N):
        column_faces(base, None)
        row_faces(base)
        layer_faces(base, None)
        edge_faces(base, None)
    row_faces(RO + N - 8)

    @pl.loop(0, N // 64)
    def _(pair):
        for a in (2 * pair, 2 * pair + 1):
            sums = [zero8] * NL
            for k in range(4):
                edge_faces(pl.multiple_of(RO + 32 * a + 8 * k, 8), sums)
            rows = pl.ds(pl.multiple_of(a * 8, 8), 8)
            for l in range(NL):
                for h, lane in ((0, first_lane), (1, last_lane)):
                    span = slice((2 * l + h) * LN, (2 * l + h + 1) * LN)
                    acc_n[rows, span] = jnp.where(lane, sums[l], acc_n[rows, span])

    block_lane = lane8 & 31
    own_block = (block_lane >= 8) & (block_lane < 16)

    def block_rows(x):
        return x.reshape(8, 8, LN).sum(axis=1)

    def edge_sums(start):
        rows = [fr[l, h, pl.ds(start, 8, stride=32), :] for l in range(NL) for h in range(2)]
        return pick_dot(jnp.concatenate(rows, axis=1), cb[...])

    c_east = edge_sums(RO + 31)
    c_east_prev = edge_sums(RO - 1)
    c_north_wide = block_rows(pick_dot(acc_n[...], cbn[...]))
    c_north = jnp.where(own_block, c_north_wide, 0.0)
    c_north_prev = jnp.where(own_block, shift(c_north_wide, 1, 1), 0.0)
    up_sink = block_rows(pick_dot(acc[...], cb[...]))
    c_up = jnp.where(lane8 < 96, up_sink, 0.0)
    c_sink = jnp.where(lane8 >= 96, up_sink, 0.0)
    c_diag = c_east + c_east_prev + c_north + c_north_prev + c_up + shift(c_up, 32, 1) + c_sink
    tile = zero8
    for q, x in enumerate((c_east, c_north, c_up + c_sink, c_diag)):
        tile = tile + shift(jnp.where(own_block, x, 0.0), 8 * q, 1)
    cm[...] = tile
    cm_in = {d: (k, send(cm, cmr.at[k], d)) for k, d in enumerate(DIRS)}

    sub8 = iota((8, LN), 0)

    def stack(*rows):
        out8 = zero8
        for k, x in enumerate(rows):
            out8 = jnp.where(sub8 == k, x, out8)
        return out8

    def sum_along_gx(it, *tiles):
        s1[it] = stack(*(x.sum(axis=0, keepdims=True) for x in tiles))
        return [send(s1.at[it], ls1.at[it, d - 1], (d, 0)) for d in range(1, nx)]

    def sum_along_gy(it, arriving):
        total = s1[it]
        for d in range(1, nx):
            arriving[d - 1].wait_recv()
            total = total + ls1[it, d - 1]
        s2[it] = total
        return [send(s2.at[it], ls2.at[it, d - 1], (0, d)) for d in range(1, ny)]

    def sum_end(it, arriving, parts):
        total = s2[it]
        for d in range(1, ny):
            arriving[d - 1].wait_recv()
            total = total + ls2[it, d - 1]
        total = total.sum(axis=1, keepdims=True)
        return [total[q : q + 1, :] for q in range(parts)]

    sums_gx = sum_along_gx(0, source_sum, c_diag, c_sink)

    for c in tile_in2:
        c.wait_recv()
    quarter = devices // 4
    lane_q = iota((quarter, LN), 1)
    power = jnp.zeros((quarter, LN), F32)
    ids = power
    for k in range(4):
        part = tin2[k * quarter : (k + 1) * quarter, :]
        mine = (lane_q >> 5) == k
        power = jnp.where(mine, shift(part, 32 * k, 1), power)
        ids = jnp.where(mine, shift(part, 32 * k - 32, 1), ids)
    ids = ids.astype(jnp.int32)
    powers = [part.astype(F32) for part in pieces(power, 3)]
    sub32 = iota((32, LN), 0)
    for k in range(quarter):
        span = slice(k * LN, (k + 1) * LN)
        one_id = ids[k : k + 1, :]
        dense_a[:, span] = jnp.where(sub32 == (one_id >> 5), 1.0, 0.0).astype(BF16)
        hit = sub32 == (one_id & 31)
        for q in range(3):
            dense_b[q, :, span] = jnp.where(hit, powers[q][k : k + 1, :], 0.0).astype(BF16)
    total = None
    for q in range(3):
        term = lax.dot_general(
            dense_a[...], dense_b[q], (((1,), (1,)), ((), ())), preferred_element_type=F32
        )
        total = term if total is None else total + term
    total = jnp.concatenate([total * (1.0 / 64.0), jnp.zeros((32, LN - 32), F32)], axis=1)
    total_t = jnp.concatenate([total, jnp.zeros((LN - 32, LN), F32)], axis=0).T
    ts[...] = stack(total_t[0:1, :], total_t[31:32, :], total[0:1, :], total[31:32, :])
    th_in = {d: (k, send(ts, th.at[k], d)) for k, d in enumerate(DIRS)}
    spread_cols = jnp.where(iota((LN, N), 0) == (iota((LN, N), 1) >> 3), 1.0, 0.0).astype(BF16)
    wide = pick_dot(total, spread_cols)
    for h in range(2):
        dynr[h, 8:40, :] = wide[:, halves[h]]

    def diagonal(base):
        here, above = pl.ds(base, 8), pl.ds(base - 1, 8)
        for l in range(NL):
            for h in range(2):
                d = fr[l, h, above, :] + fr[l, h, here, :] + fl[l, h, here, :] + fc[l, h, here, :]
                if l > 0:
                    d = d + fv[l - 1, h, here, :]
                if l < NL - 1:
                    d = d + fv[l, h, here, :]
                else:
                    d = d + snk[h, here, :]
                d = jnp.maximum(d, FACE_FLOOR)
                dg[l, h, here, :] = d
                wg[l, h, here, :] = DAMPING / d

    diagonal(RO - 8)
    diagonal(RO + N)

    @pl.loop(0, N // 32)
    def _(a):
        for k in range(4):
            diagonal(pl.multiple_of(RO + 32 * a + 8 * k, 8))

    def couple(ref, base, edge, live):
        here, above, below = pl.ds(base, 8), pl.ds(base - 1, 8), pl.ds(base + 1, 8)
        res = [[None, None] for _ in range(NL)]
        mid = [[ref[l, h, here, :] for h in range(2)] for l in range(live)]
        for l in range(live):
            a0, a1 = mid[l]
            f0, f1 = fc[l, 0, here, :], fc[l, 1, here, :]
            ra0, ra1 = shift(a0, -1, 1), shift(a1, -1, 1)
            p0, p1 = shift(f0 * a0, 1, 1), shift(f1 * a1, 1, 1)
            lateral = (
                f0 * jnp.where(last_lane, ra1, ra0) + jnp.where(first_lane, edge[l], p0),
                jnp.where(last_lane, edge[l], f1 * ra1) + jnp.where(first_lane, p0, p1),
            )
            for h in range(2):
                res[l][h] = (
                    lateral[h]
                    + fr[l, h, above, :] * ref[l, h, above, :]
                    + fr[l, h, here, :] * ref[l, h, below, :]
                )
        for l in range(live):
            for h in range(2):
                for face, to in ((l - 1, l - 1), (l, l + 1)):
                    if 0 <= to < NL:
                        term = fv[face, h, here, :] * mid[l][h]
                        res[to][h] = term if res[to][h] is None else res[to][h] + term
        return mid, res

    def strip_couple(v, g, live):
        res = []
        for l in range(live):
            p, r = fcs[l, g] * v[l], frs[l, g]
            res.append(
                fcs[l, g] * shift(v[l], -1, 0) + shift(p, 1, 0) + r * shift(v[l], -1, 1) + shift(r * v[l], 1, 1)
            )
        res += [None] * (NL - live)
        for l in range(live):
            for face, to in ((l - 1, l - 1), (l, l + 1)):
                if 0 <= to < NL:
                    term = fvs[face, g] * v[l]
                    res[to] = term if res[to] is None else res[to] + term
        return res

    def dyn_rows(base, h):
        return dynr[h, pl.ds(base // 8 + 6, 1), :]

    def over_rows(body, margins=True, carry=None):
        if margins:
            body(RO - 8, None, -1, 3)
            body(RO + N, None, 8, 0)

        @pl.loop(0, N // 128)
        def _(pair):
            for a in (4 * pair, 4 * pair + 1, 4 * pair + 2, 4 * pair + 3):
                sums = [zero8] * 8
                for k in range(4):
                    body(pl.multiple_of(RO + 32 * a + 8 * k, 8), sums, a, k)
                rows = pl.ds(pl.multiple_of(a * 8, 8), 8)
                for q in range(8):
                    if sums[q] is not zero8:
                        acc[rows, q * LN : (q + 1) * LN] = sums[q]

    lane16 = iota((16, LN), 1)
    lane24 = iota((24, LN), 1)

    def sweep_neighbours(x):
        lanes = [shift(x, by, 1) for by in (-1, 1, -32, 32)]
        rows = coef[1] * shift(x, -1, 0) + coef[2] * shift(x, 1, 0)
        return rows, (coef[3] * lanes[0] + coef[4] * lanes[1]) + (coef[5] * lanes[2] + coef[6] * lanes[3])

    def coarse_sweeps(right):
        rw = coef[0] * right
        x = rw
        for _ in range(CJ - 1):
            rows, lanes = sweep_neighbours(x)
            x = ((1.0 - DAMPING) * x + rw + rows) + lanes
        return x

    def assemble(own, other):
        rows = []
        for dx in (-1, 0, 1):
            centre = own if dx == 0 else other((dx, 0))
            rows.append(centre + shift(other((dx, -1)), -8, 1) + shift(other((dx, 1)), 8, 1))
        return jnp.concatenate(rows, axis=0)

    def send_coarse(it, own):
        ct[it] = own
        return {d: (k, send(ct.at[it], nb.at[it, k], d)) for k, d in enumerate(DIRS)}

    def first_residual(base, sums, a, k):
        here = pl.ds(base, 8)
        for h in range(2):
            r = dyn_rows(base, h) + drn[h, here, :]
            src[h, here, :] = r
            r_[0, h, here, :] = r
            e1_[0, h, here, :] = wg[0, h, here, :] * r
            if sums is not None:
                sums[h] += r

    over_rows(first_residual, margins=False)
    own_c = block_rows(pick_dot(acc[:, 0 : 2 * LN], cb[0 : 2 * LN, :]))
    side = send_coarse(0, own_c)

    def second_sweep(base, live, edge, first):
        here = pl.ds(base, 8)
        mid, res = couple(e1_, base, edge, live)
        for l in range(NL):
            for h in range(2):
                if l < live:
                    u = (1.0 - DAMPING) * mid[l][h] + wg[l, h, here, :] * (r_[l, h, here, :] + res[l][h])
                elif res[l][h] is not None:
                    u = wg[l, h, here, :] * res[l][h]
                else:
                    u = zero8
                if not first:
                    u = u + t_[l, h, here, :]
                t_[l, h, here, :] = u

    over_rows(lambda base, sums, a, k: second_sweep(base, 1, [zero8], True), margins=False)

    snk_e1 = [wgs[NL - 1, g] * sks[g] for g in sides]
    column_form(
        [None] * (NL - 1) + [(fcs[NL - 1, 0] * snk_e1[0])[7:8, :]],
        [None] * (NL - 1) + [fcs[NL - 1, 1][7:8, :] * snk_e1[1][8:9, :]],
        cf_t,
    )

    def sink_first(base, sums, a, k):
        here = pl.ds(base, 8)
        for h in range(2):
            gs[h, here, :] = wg[NL - 1, h, here, :] * snk[h, here, :]

    over_rows(sink_first)

    def sink_second(base, sums, a, k):
        here, above, below = pl.ds(base, 8), pl.ds(base - 1, 8), pl.ds(base + 1, 8)
        top = NL - 1
        edge = columns(cf_t, base)[top]
        a0, a1 = gs[0, here, :], gs[1, here, :]
        f0, f1 = fc[top, 0, here, :], fc[top, 1, here, :]
        ra0, ra1 = shift(a0, -1, 1), shift(a1, -1, 1)
        p0, p1 = shift(f0 * a0, 1, 1), shift(f1 * a1, 1, 1)
        lateral = (
            f0 * jnp.where(last_lane, ra1, ra0) + jnp.where(first_lane, edge, p0),
            jnp.where(last_lane, edge, f1 * ra1) + jnp.where(first_lane, p0, p1),
        )
        for h, e in ((0, a0), (1, a1)):
            flow = (
                lateral[h]
                + fr[top, h, above, :] * gs[h, above, :]
                + fr[top, h, here, :] * gs[h, below, :]
            )
            gr[1, h, here, :] = (1.0 - DAMPING) * e + wg[top, h, here, :] * (snk[h, here, :] + flow)
            gr[0, h, here, :] = wg[top - 1, h, here, :] * (fv[top - 1, h, here, :] * e)

    over_rows(sink_second, margins=False)
    first_gy = sum_along_gy(0, sums_gx)

    for _, c in cm_in.values():
        c.wait_recv()
    def coupling(q):
        def of(tile):
            return jnp.where((lane8 >> 3) & 3 == (q + 1) % 4, tile, 0.0)

        rows = []
        for dx in (-1, 0, 1):
            tiles = [cm[...] if (dx, dy) == (0, 0) else cmr[cm_in[(-dx, -dy)][0]] for dy in (-1, 0, 1)]
            rows.append(sum(shift(of(tile), 8 * (dy - q), 1) for dy, tile in zip((-1, 0, 1), tiles, strict=True)))
        return jnp.concatenate(rows, axis=0)

    w_east, w_north, w_up, w_diag = (coupling(q) for q in range(4))
    w_sink = jnp.where(lane24 >= 96, w_up, 0.0)
    w_up = jnp.where(lane24 < 96, w_up, 0.0)
    gain = jnp.where((lane24 & 31) < 24, DAMPING / jnp.maximum(w_diag, 1e-30), 0.0)
    coef[0] = gain
    coef[1] = gain * w_east
    coef[2] = gain * shift(w_east, 1, 0)
    coef[3] = gain * w_north
    coef[4] = gain * shift(w_north, 1, 1)
    coef[5] = gain * w_up
    coef[6] = gain * shift(w_up, 32, 1)
    adjoint = coarse_sweeps(w_sink)
    own_adjoint = jnp.where(own_block, adjoint[8:16, :], 0.0)
    sums_gx = sum_along_gx(1, own_adjoint * own_c)

    @pl.loop(0, N // 32)
    def _(a):
        for k in range(4):
            for h in range(2):
                dyn_out[pl.ds(pl.multiple_of(a * 32 + k * 8, 8), 8), halves[h]] = jnp.broadcast_to(
                    dynr[h, pl.ds(8 + 4 * a + k, 1), :], (8, LN)
                )
    for _, c in th_in.values():
        c.wait_recv()

    def rim(d, k):
        return th[th_in[(-d[0], -d[1])][0], k : k + 1, :]

    wide_rims = pick_dot(stack(rim((-1, 0), 3) * edge_n, rim((1, 0), 2) * edge_s), spread_cols)
    for h in range(2):
        dynr[h, 0:8, :] = jnp.broadcast_to(wide_rims[0:1, halves[h]], (8, LN))
        dynr[h, 40:48, :] = jnp.broadcast_to(wide_rims[1:2, halves[h]], (8, LN))
    body = stack(rim((0, -1), 1), ts[0:1, :], ts[1:2, :], rim((0, 1), 0))
    top = stack(rim((-1, -1), 1), rim((-1, 0), 0), rim((-1, 0), 1), rim((-1, 1), 0))
    low = stack(rim((1, -1), 1), rim((1, 0), 0), rim((1, 0), 1), rim((1, 1), 0))
    tall = jnp.where(
        lane8 == 0,
        shift(top, -31, 1),
        jnp.where(lane8 == 33, shift(low, 33, 1), jnp.where(lane8 < 33, shift(body, 1, 1), 0.0)),
    )
    spread_rows = jnp.where(iota((LN, SL), 0) == ((iota((LN, SL), 1) - (SO - 8)) >> 3), 1.0, 0.0).astype(BF16)
    tall = pick_dot(tall, spread_rows)
    for g in sides:
        dyn_s = jnp.where(sl_row < 8, tall[2 * g : 2 * g + 1, :], tall[2 * g + 1 : 2 * g + 2, :]) * keep[g]
        dys[g] = dyn_s
        srs[g] = dyn_s + drn_s[g]
    first_residual(RO - 8, None, -1, 3)
    first_residual(RO + N, None, 8, 0)

    rs = [[srs[g] for g in sides]]
    e1s = [[wgs[0, g] * srs[g] for g in sides]]
    live = 1
    zeros_s = jnp.zeros((16, SL), F32)
    edge_terms(e1s + [[zeros_s, zeros_s]] * (NL - 1), cf_e)
    second_sweep(RO - 8, 1, columns(cf_e, RO - 8), True)
    second_sweep(RO + N, 1, columns(cf_e, RO + N), True)

    def over_edges(base, sums, a, k):
        here = pl.ds(base, 8)
        edge = columns(cf_e, base)[0]
        for h, lane in ((0, first_lane), (1, last_lane)):
            t_[0, h, here, :] = t_[0, h, here, :] + jnp.where(lane, wg[0, h, here, :] * edge, 0.0)

    over_rows(over_edges, margins=False)
    for h in range(2):
        for row, beyond, face in ((RO, RO - 1, RO - 1), (RO + N - 1, RO + N, RO + N - 1)):
            t_[0, h, row : row + 1, :] = t_[0, h, row : row + 1, :] + wg[0, h, row : row + 1, :] * (
                fr[0, h, face : face + 1, :] * e1_[0, h, beyond : beyond + 1, :]
            )

    ts_old = None
    former = diag_total = sink_total = source_total = None
    sweeps = OUTER * INNER
    for it in range(sweeps):
        first, last = it == 0, it == sweeps - 1
        fresh = (it + 1) % INNER == 0

        if not first:
            over_rows(
                lambda base, sums, a, k: second_sweep(base, NL, columns(cf_e, base), False), margins=not last
            )

        if not last:
            us = [[None, None] for _ in range(NL)]
            for g in sides:
                res = strip_couple([e1s[l][g] for l in range(live)], g, live)
                for l in range(NL):
                    if l < live:
                        u = (1.0 - DAMPING) * e1s[l][g] + wgs[l, g] * (rs[l][g] + res[l])
                    elif res[l] is not None:
                        u = wgs[l, g] * res[l]
                    else:
                        u = zeros_s
                    us[l][g] = u if first else ts_old[l][g] + u
            edge_terms(us, cf_t)

            held = 2 if first else NL
            def half_residual(base, sums, a, k):
                here = pl.ds(base, 8)
                mid, res = couple(t_, base, columns(cf_t, base), held)
                for l in range(NL):
                    for h in range(2):
                        r = zero8 if res[l][h] is None else res[l][h]
                        if l < held:
                            r = r - dg[l, h, here, :] * mid[l][h]
                        if l == 0 and not fresh:
                            r = r + src[h, here, :]
                        r_[l, h, here, :] = r
                        if sums is not None:
                            sums[2 * l + h] += r

            over_rows(half_residual)
            if it == 2:
                sums_gy = sum_along_gy(2, sums_gx)
            next_c = block_rows(pick_dot(acc[...], cb[...]))

        if last:
            for c in started[: -len(DIRS)]:
                c.wait_send()
        for _, c in side.values():
            c.wait_recv()
        x = coarse_sweeps(assemble(own_c, lambda d: nb[it, side[(-d[0], -d[1])][0]]))
        if it == 1:
            source_total = source_total - sum_end(1, sums_gy, 1)[0] - former * sink_total
            x = x + former * (1.0 - adjoint)
        elif last:
            source_total, less = sum_end(2, sums_gy, 2)
            former = BALANCE_WEIGHT * source_total / diag_total
            source_total = source_total - less - former * sink_total
            x = x + former * (1.0 - adjoint)
        if it % INNER == 1:
            x = x + BALANCE_WEIGHT * source_total / diag_total

        def send_next(total_c):
            moved = (x - sum(sweep_neighbours(x)) * (1.0 / DAMPING))[8:16, :] * c_diag
            own = total_c - jnp.where(own_block, moved, 0.0)
            return own, send_coarse(it + 1, own)

        if not last and not fresh:
            own_c, side = send_next(next_c)

        for l in range(NL):
            for h in range(2):
                at_col = l * 32 + 8 + h * 4
                cv[l, h] = jnp.take_along_axis(x, at_col + (lane24 >> 5), axis=1)
                if not last:
                    cvr[l, h] = jnp.take_along_axis(x, at_col + ((lane24 + 1) >> 5), axis=1)
                    cvl[l, h] = jnp.take_along_axis(x, at_col + ((lane24 - 1) >> 5), axis=1)

        if last:

            @pl.loop(0, N // 32)
            def _(a):
                for l in range(NL):
                    for h in range(2):
                        add = cv[l, h, pl.ds(8 + a, 1), :]
                        for k in range(4):
                            rows = pl.ds(pl.multiple_of(32 * a + 8 * k, 8), 8)
                            here = pl.ds(pl.multiple_of(RO + 32 * a + 8 * k, 8), 8)
                            u = t_[l, h, here, :] + add
                            if l >= NL - 2:
                                u = u - former * gr[l - (NL - 2), h, here, :]
                            out[l, rows, halves[h]] = u

            break

        if fresh:

            def new_source(base, sums, a, k):
                here = pl.ds(base, 8)
                for h in range(2):
                    u = t_[0, h, here, :] + cv[0, h, pl.ds(8 + a, 1), :]
                    s = dyn_rows(base, h) + drn[h, here, :] * jnp.exp(DRAIN_SLOPE * u)
                    src[h, here, :] = s
                    if sums is not None:
                        sums[h] += s

            over_rows(new_source)
            next_c = next_c + block_rows(pick_dot(acc[:, 0 : 2 * LN], cb[0 : 2 * LN, :]))
            own_c, side = send_next(next_c)
        if first:
            sums_gy = sum_along_gy(1, sums_gx)

        def whole_residual(base, sums, a, k):
            here, above = pl.ds(base, 8), pl.ds(base - 1, 8)
            block = pl.ds(8 + a, 1)
            xs = [[cv[l, h, block, :] for h in range(2)] for l in range(NL)]
            for h in range(2):
                flow = None
                for l in range(NL):
                    v = xs[l][h]
                    t_[l, h, here, :] = t_[l, h, here, :] + v
                    r = r_[l, h, here, :]
                    if l == 0 and fresh:
                        r = r + src[h, here, :]
                    r = r - fc[l, h, here, :] * (v - cvr[l, h, block, :])
                    r = r - fl[l, h, here, :] * (v - cvl[l, h, block, :])
                    if k == 0:
                        step = v - cv[l, h, pl.ds(7 + a, 1), :]
                        r = r - jnp.where(sub8 == 0, fr[l, h, above, :] * step, 0.0)
                    if k == 3:
                        step = v - cv[l, h, pl.ds(9 + a, 1), :]
                        r = r - jnp.where(sub8 == 7, fr[l, h, here, :] * step, 0.0)
                    if l > 0:
                        r = r + flow
                    if l < NL - 1:
                        flow = fv[l, h, here, :] * (v - xs[l + 1][h])
                        r = r - flow
                    else:
                        r = r - snk[h, here, :] * v
                    r_[l, h, here, :] = r
                    e1_[l, h, here, :] = wg[l, h, here, :] * r
                    if it == 1 and l >= NL - 2 and sums is not None:
                        sums[0] += gr[l - (NL - 2), h, here, :] * r

        over_rows(whole_residual)
        if it == 1:
            response = acc[0:8, 0:LN]
            for a in range(1, 8):
                response = response + acc[8 * a : 8 * a + 8, 0:LN]
            sums_gx = sum_along_gx(2, own_c, response + own_adjoint * own_c)

        xt[...] = jnp.concatenate([x, jnp.zeros((LN - 24, LN), F32)], axis=0).T
        picked = jnp.concatenate(
            [xt[l * 32 + c : l * 32 + c + 1, :] for l in range(NL) for c in (7, 8, 15, 16)], axis=0
        )
        picked = jnp.concatenate(
            [jnp.take_along_axis(picked, 6 + 4 * k + (lane16 >> 5), axis=1) for k in range(SL // LN)], axis=1
        )
        live = NL
        ts_old = [[None, None] for _ in range(NL)]
        rs = [[None, None] for _ in range(NL)]
        e1s = [[None, None] for _ in range(NL)]
        for g in sides:
            for l in range(NL):
                k = 4 * l + 2 * g
                ts_old[l][g] = us[l][g] + jnp.where(sl_row < 8, picked[k : k + 1, :], picked[k + 1 : k + 2, :])
            if fresh:
                srs[g] = dys[g] + drn_s[g] * jnp.exp(DRAIN_SLOPE * ts_old[0][g])
            res = strip_couple([ts_old[l][g] for l in range(NL)], g, NL)
            for l in range(NL):
                r = res[l] - dgs[l, g] * ts_old[l][g]
                if l == 0:
                    r = r + srs[g]
                rs[l][g] = r
                e1s[l][g] = wgs[l, g] * r
        if first:
            source_total, diag_total, sink_total = sum_end(0, first_gy, 3)
            former = BALANCE_WEIGHT * source_total / diag_total

            def sink_part(base, sums, a, k):
                here = pl.ds(base, 8)
                for h in range(2):
                    r = r_[NL - 1, h, here, :] - former * snk[h, here, :]
                    r_[NL - 1, h, here, :] = r
                    e1_[NL - 1, h, here, :] = wg[NL - 1, h, here, :] * r

            over_rows(sink_part)
            for g in sides:
                rs[NL - 1][g] = rs[NL - 1][g] - former * sks[g]
                e1s[NL - 1][g] = wgs[NL - 1, g] * rs[NL - 1][g]
        edge_terms(e1s, cf_e)

    for c in started[-len(DIRS) :]:
        c.wait_send()


def hand_over(a, b, to_a, to_b, sem):
    copies = [
        pltpu.make_async_copy(a.at[l], to_a.at[l], sem.at[l]) for l in range(NL)
    ] + [pltpu.make_async_copy(b, to_b, sem.at[NL])]
    for c in copies:
        c.start()
    for c in copies:
        c.wait()


def n_copies(nx, ny):
    setup = (ny - 1) + 2 + 6 + 2 + (nx - 1) + 8 + 8
    return setup + OUTER * INNER * 8 + 3 * (nx - 1 + ny - 1)


def solution(mesh):
    nx, ny = mesh.shape["gx"], mesh.shape["gy"]
    its = OUTER * INNER
    devices = nx * ny

    def step(material, material_table, sink_cond, drain_current, instance_tile, instance_power):
        n_inst = instance_tile.shape[0]
        field = pltpu.VMEM((NL, 2, NR, LN), F32)
        single = pltpu.VMEM((2, NR, LN), F32)
        vm = lambda *shape: pltpu.VMEM(shape, F32)
        half = lambda *shape: pltpu.VMEM(shape, BF16)
        copies = n_copies(nx, ny)
        scratch = [
            pltpu.VMEM((NL, N, N), jnp.int32), vm(N, N), vm(N, N),
            pltpu.SMEM((2, 16), F32), pltpu.VMEM((n_inst // LN, LN), jnp.int32), vm(n_inst // LN, LN),
            field, field, field, field, field, pltpu.VMEM((NL - 1, 2, NR, LN), F32), field, field,
            single, single, single, field, field, field,
            vm(SL, LN), vm(SL, LN), vm(SL, LN), vm(64, 8 * LN), vm(64, 8 * LN), vm(SL, LN),
            half(8 * LN, LN), half(8 * LN, LN),
            half(devices, n_inst), half(3, 64, n_inst), vm(devices, LN), vm(devices, LN),
            vm(nx, ny, LN), vm(devices, LN), half(32, 32 * devices), half(3, 32, 32 * devices),
            vm(8, LN), vm(8, 8, LN), vm(2, 48, LN),
            vm(2, NQ, 2, 8, LN), vm(2, NQ, 2, 8, LN), vm(2, 8, LN), vm(6, 8, LN),
            vm(2, 8 * NQ, SL), vm(2, 8 * NQ, SL),
            vm(NL, 2, 16, SL), vm(NL, 2, 16, SL), vm(NL - 1, 2, 16, SL), vm(NL, 2, 16, SL), vm(NL, 2, 16, SL),
            vm(2, 16, SL), vm(2, 16, SL), vm(2, 16, SL), vm(2, 16, SL), single, pltpu.VMEM((2, 2, NR, LN), F32),
            vm(8, LN), vm(8, 8, LN), vm(7, 24, LN), vm(its, 8, LN), vm(its, 8, 8, LN),
            vm(3, 8, LN), vm(3, nx - 1, 8, LN), vm(3, 8, LN), vm(3, ny - 1, 8, LN),
            vm(NL, 2, 24, LN), vm(NL, 2, 24, LN), vm(NL, 2, 24, LN), vm(LN, LN),
            pltpu.SemaphoreType.DMA((copies,)), pltpu.SemaphoreType.DMA((copies,)), pltpu.SemaphoreType.DMA((6,)),
        ]
        vmem = pl.BlockSpec(memory_space=pltpu.VMEM)
        hbm = pl.BlockSpec(memory_space=pltpu.HBM)
        shapes = (jax.ShapeDtypeStruct((NL, N, N), F32), jax.ShapeDtypeStruct((N, N), F32))
        inside = (vm(NL, N, N), vm(N, N))
        results = pl.pallas_call(
            functools.partial(kernel, nx, ny),
            out_shape=inside,
            in_specs=[hbm] * 6,
            out_specs=(vmem, vmem),
            scratch_shapes=scratch,
            compiler_params=pltpu.CompilerParams(
                collective_id=0, has_side_effects=True, vmem_limit_bytes=56 * 1024 * 1024
            ),
        )(
            material,
            material_table,
            sink_cond,
            drain_current,
            instance_tile.reshape(n_inst // LN, LN),
            instance_power.reshape(n_inst // LN, LN),
        )
        return pl.pallas_call(
            hand_over,
            out_shape=shapes,
            in_specs=[pl.BlockSpec(memory_space=pl.ANY)] * 2,
            out_specs=(hbm, hbm),
            compiler_params=pltpu.CompilerParams(vmem_limit_bytes=1024 * 1024),
            scratch_shapes=[pltpu.SemaphoreType.DMA((NL + 1,))],
        )(*results)

    return jax.shard_map(
        step,
        mesh=mesh,
        in_specs=(
            P(None, "gx", "gy"),
            P(),
            P("gx", "gy"),
            P("gx", "gy"),
            P(("gx", "gy")),
            P(("gx", "gy")),
        ),
        out_specs=(P(None, "gx", "gy"), P("gx", "gy")),
        check_vma=False,
    )
```

```python
import functools

import jax
import jax.numpy as jnp
from jax import lax
from jax.experimental import pallas as pl
from jax.experimental.pallas import tpu as pltpu
from jax.sharding import PartitionSpec as P

MESH = pl.DeviceIdType.MESH
F32 = jnp.float32
BF16 = jnp.bfloat16

NL = 4
N = 256
LN = 128
RO = 16
NR = N + 2 * RO
NQ = 6
SL = 384
SO = 64
OUTER = 2
INNER = 2
CJ = 8
DAMPING = 0.8
DRAIN_SLOPE = 0.5
FACE_FLOOR = 0.5
BALANCE_WEIGHT = 0.5
DIRS = ((-1, -1), (-1, 0), (-1, 1), (0, -1), (0, 1), (1, -1), (1, 0), (1, 1))
DIAG = tuple(d for d in DIRS if d[0] and d[1])
OFF_LINE = tuple(d for d in DIRS if d[1])


def iota(shape, dim):
    return lax.broadcasted_iota(jnp.int32, shape, dim)


def harmonic(a, b):
    return 2.0 * a * b / jnp.maximum(a + b, FACE_FLOOR)


def shift(x, amount, axis):
    return pltpu.roll(x, amount % x.shape[axis], axis)


def lookup(ids, table):
    level = list(table)
    for bit in range(4):
        odd = ((ids >> bit) & 1) == 1
        level = [jnp.where(odd, level[2 * k + 1], level[2 * k]) for k in range(len(level) // 2)]
    return level[0]


def exact_dot(a, b):
    return lax.dot_general(
        a, b, (((1,), (0,)), ((), ())), precision=lax.Precision.HIGHEST, preferred_element_type=F32
    )


def pieces(x, count):
    out = []
    for _ in range(count - 1):
        part = x.astype(BF16)
        out.append(part)
        x = x - part.astype(F32)
    return out + [x.astype(BF16)]


def pick_dot(x, ones, parts=3):
    return sum(jnp.dot(part, ones, preferred_element_type=F32) for part in pieces(x, parts))


class Layout:
    def __init__(self):
        self.count = 0

    def take(self):
        self.count += 1
        return self.count - 1


def kernel(nx, ny, *refs):
    (mat_hbm, tab_hbm, sink_hbm, drain_hbm, tile_hbm, power_hbm, out, dyn_out) = refs[:8]
    (
        mat, sink, drain, tab, inst_tile, inst_power,
        lat, ver, fr, fc, fl, fv, dg, wg, src, drn, snk, t_, r_, e1_,
        cf_t, cf_e, cf_f, acc, acc_n, pk, cb, cbn,
        dest, slots, sout, tin1, tred, tin2, dense_a, dense_b, ts, th, dynr,
        sq_row, rq_row, sq_c, rq_c, sq_s, rq_s,
        fcs, frs, fvs, dgs, wgs, drn_s, dys, srs, sks, gs, gr,
        cm, cmr, coef, ct, nb, s1, ls1, s2, ls2, cv, cvr, cvl, xt,
        ssem, rsem, lsem,
    ) = refs[8:]
    mx, my = lax.axis_index("gx"), lax.axis_index("gy")

    def at(dx, dy):
        return {"gx": lax.rem(mx + (dx + nx), nx), "gy": lax.rem(my + (dy + ny), ny)}

    fetch_small = [
        pltpu.make_async_copy(a, b, lsem.at[3 + k])
        for k, (a, b) in enumerate(((tile_hbm, inst_tile), (power_hbm, inst_power), (tab_hbm, tab)))
    ]
    for c in fetch_small:
        c.start()

    partners = [(d, 0) for d in range(1, nx)] + [(0, d) for d in range(1, ny)] + list(DIAG)
    barrier = pltpu.get_barrier_semaphore()
    for d in partners:
        pl.semaphore_signal(barrier, inc=1, device_id=at(*d), device_id_type=MESH)

    fetch = [
        pltpu.make_async_copy(a, b, lsem.at[k])
        for k, (a, b) in enumerate(((mat_hbm, mat), (sink_hbm, sink), (drain_hbm, drain)))
    ]
    for c in fetch:
        c.start()

    numbers = Layout()
    started = []

    def send(a, b, to):
        k = numbers.take()
        copy = pltpu.make_async_remote_copy(
            src_ref=a, dst_ref=b, send_sem=ssem.at[k], recv_sem=rsem.at[k],
            device_id=at(*to), device_id_type=MESH,
        )
        copy.start()
        started.append(copy)
        return copy

    lane8 = iota((8, LN), 1)
    first_lane = lane8 == 0
    last_lane = lane8 == LN - 1
    low_half = lane8 < LN // 2

    devices = nx * ny
    chunks = inst_tile.shape[0]
    col_n = iota((LN, LN), 1)
    row_n = iota((LN, LN), 0)
    for l in range(NL):
        for h in range(2):
            span = pl.ds((2 * l + h) * LN, LN)
            goal = l * 32 + 8 + h * 4 + (row_n >> 5)
            cb[span, :] = jnp.where(col_n == goal, 1.0, 0.0).astype(BF16)
            hit = ((row_n & 31) == 31) & (col_n == goal)
            if h == 0:
                hit = hit | ((row_n == 0) & (col_n == l * 32 + 7))
            cbn[span, :] = jnp.where(hit, 1.0, 0.0).astype(BF16)
    zero8 = jnp.zeros((8, LN), F32)
    for ref, places in ((t_, (0, NR - 8)), (e1_, (0, 8, NR - 16, NR - 8)), (fr, (0,)), (lat, (NR - 16, NR - 8))):
        for l in range(NL):
            for h in range(2):
                for place in places:
                    ref[l, h, place : place + 8, :] = zero8
    for c in fetch_small:
        c.wait()
    sub_d = iota((devices, LN), 0)
    lane_d = iota((devices, LN), 1)
    up_to = jnp.where(iota((LN, LN), 0) <= iota((LN, LN), 1), 1.0, 0.0).astype(BF16)
    for k in range(chunks):
        s = inst_tile[k : k + 1, :] >> 10
        owner = (s % ny) * nx + s // ny
        dest[:, k * LN : (k + 1) * LN] = jnp.where(sub_d == owner, 1.0, 0.0).astype(BF16)
    before = jnp.zeros((devices, LN), F32)
    all_ones = jnp.ones((LN, LN), BF16)
    slot_row = iota((64, LN), 0)
    for k in range(chunks):
        span = slice(k * LN, (k + 1) * LN)
        d = dest[:, span]
        within = jnp.dot(d, up_to, preferred_element_type=F32)
        rank = jnp.sum(d.astype(F32) * (within + before), axis=0, keepdims=True)
        before = before + jnp.dot(d, all_ones, preferred_element_type=F32)
        at_slot = (slot_row & 31) == rank.astype(jnp.int32) - 1
        t = inst_tile[k : k + 1, :]
        ids = ((t & 992).astype(F32), (t & 31).astype(F32), jnp.zeros((1, LN), F32))
        for q, part in enumerate(pieces(inst_power[k : k + 1, :], 3)):
            value = jnp.where(slot_row < 32, part.astype(F32), ids[q])
            slots[q, :, span] = jnp.where(at_slot, value, 0.0).astype(BF16)
    total = None
    for q in range(3):
        term = lax.dot_general(
            dest[...], slots[q], (((1,), (1,)), ((), ())), preferred_element_type=F32
        )
        total = term if total is None else total + term
    sout[...] = jnp.concatenate([total, jnp.zeros((devices, LN - 64), F32)], axis=1)
    power_sum = jnp.zeros((8, LN), F32)
    for k in range(chunks // 8):
        power_sum = power_sum + inst_power[8 * k : 8 * k + 8, :]

    def bundle(j):
        return sout.at[pl.ds(pl.multiple_of(j * nx, nx), nx), :]

    pl.semaphore_wait(barrier, len(partners))
    tile_in = []
    for d in range(1, ny):
        tile_in.append(send(bundle(lax.rem(my + d, ny)), tin1.at[pl.ds(d * nx, nx)], (0, d)))
    tin1[0:nx, :] = bundle(my)[...]

    def pack(values):
        packed = jnp.zeros((8, LN), F32)
        for q, (a, b) in enumerate(values):
            both = shift(jnp.where(low_half, a, b), 16 * q + 8, 1)
            packed = jnp.where((lane8 >> 4) == q, both, packed)
        return packed

    halves = (slice(0, LN), slice(LN, N))

    def raw(rows):
        mats = [tuple(mat[l, rows, h].astype(F32) for h in halves) for l in range(NL)]
        return mats + [tuple(a[rows, h] for h in halves) for a in (sink, drain)]

    for c in fetch:
        c.wait()
    for side, rows in enumerate((slice(0, 8), slice(N - 8, N))):
        values = raw(rows)
        for q, (a, b) in enumerate(values):
            sq_row[side, q, 0] = a
            sq_row[side, q, 1] = b
        sq_c[side] = pack(values)
    margin_row = [send(sq_row.at[s], rq_row.at[s], (2 * s - 1, 0)) for s in range(2)]
    corner_dirs = ((-1, 0), (1, 0)) + DIAG
    margin_c = {
        d: (k, send(sq_c.at[0 if d[0] < 0 else 1], rq_c.at[k], d)) for k, d in enumerate(corner_dirs)
    }

    @pl.loop(0, N // 32)
    def _(a):
        for k in range(4):
            rows = pl.ds(pl.multiple_of(a * 32 + k * 8, 8), 8)
            pk[pl.ds(pl.multiple_of(a * 32 + k * 8 + SO, 8), 8), :] = pack(raw(rows))

    pk[0:SO, :] = jnp.zeros((SO, LN), F32)
    pk[SO + N :, :] = jnp.zeros((SL - N - SO, LN), F32)
    for k in range(SL // LN):
        span = slice(k * LN, (k + 1) * LN)
        block = pk[span, :].T
        for q in range(NQ):
            sq_s[0, 8 * q : 8 * q + 8, span] = block[16 * q + 8 : 16 * q + 16, :]
            sq_s[1, 8 * q : 8 * q + 8, span] = block[16 * q : 16 * q + 8, :]
    margin_we = [send(sq_s.at[s], rq_s.at[s], (0, 2 * s - 1)) for s in range(2)]

    table = [[tab[q, k] for k in range(16)] for q in range(2)]

    @pl.loop(0, N // 32, init_carry=power_sum)
    def source_sum(a, source_sum):
        for k in range(4):
            rows = pl.ds(pl.multiple_of(a * 32 + k * 8, 8), 8)
            into = pl.ds(pl.multiple_of(a * 32 + k * 8 + RO, 8), 8)
            for h in range(2):
                for l in range(NL):
                    ids = mat[l, rows, halves[h]]
                    lat[l, h, into, :] = lookup(ids, table[0])
                    ver[l, h, into, :] = lookup(ids, table[1])
                snk[h, into, :] = sink[rows, halves[h]]
                d = drain[rows, halves[h]]
                drn[h, into, :] = d
                source_sum = source_sum + d
        return source_sum

    def row_faces(base):
        here, below = pl.ds(base, 8), pl.ds(base + 1, 8)
        for l in range(NL):
            for h in range(2):
                fr[l, h, here, :] = harmonic(lat[l, h, here, :], lat[l, h, below, :])

    def layer_faces(base, sums):
        here = pl.ds(base, 8)
        for h in range(2):
            vs = [ver[l, h, here, :] for l in range(NL)]
            for l in range(NL):
                if l < NL - 1:
                    v = harmonic(vs[l], vs[l + 1])
                    fv[l, h, here, :] = v
                else:
                    v = snk[h, here, :]
                if sums is not None:
                    sums[2 * l + h] += v

    def column_faces(base, sums):
        here = pl.ds(base, 8)
        for l in range(NL):
            a0, a1 = lat[l, 0, here, :], lat[l, 1, here, :]
            ra0, ra1 = shift(a0, -1, 1), shift(a1, -1, 1)
            c0 = harmonic(a0, jnp.where(last_lane, ra1, ra0))
            c1 = harmonic(a1, ra1)
            rc0, rc1 = shift(c0, 1, 1), shift(c1, 1, 1)
            fc[l, 0, here, :] = c0
            fc[l, 1, here, :] = c1
            fl[l, 0, here, :] = rc0
            fl[l, 1, here, :] = jnp.where(first_lane, rc0, rc1)
            if sums is not None:
                sums[2 * l] += c0
                sums[2 * l + 1] += c1

    @pl.loop(0, N // 64)
    def _(pair):
        for a in (2 * pair, 2 * pair + 1):
            sums, sums_n = [zero8] * 8, [zero8] * 8
            for k in range(4):
                base = pl.multiple_of(RO + 32 * a + 8 * k, 8)
                row_faces(base)
                layer_faces(base, sums)
                column_faces(base, sums_n)
            rows = pl.ds(pl.multiple_of(a * 8, 8), 8)
            for q in range(8):
                acc[rows, q * LN : (q + 1) * LN] = sums[q]
                acc_n[rows, q * LN : (q + 1) * LN] = sums_n[q]

    for c in tile_in:
        c.wait_recv()
    for x in range(nx):
        tred[x] = tin1[pl.ds(x, ny, stride=nx), :]
    tile_in2 = []
    for d in range(1, nx):
        x = lax.rem(mx + d, nx)
        tile_in2.append(send(tred.at[x], tin2.at[pl.ds(d * ny, ny)], (d, 0)))
    tin2[0:ny, :] = tred[mx]

    edge_n = jnp.where(mx == 0, 0.0, 1.0)
    edge_s = jnp.where(mx == nx - 1, 0.0, 1.0)
    edge_w = jnp.where(my == 0, 0.0, 1.0)
    edge_e = jnp.where(my == ny - 1, 0.0, 1.0)
    for c in margin_row:
        c.wait_recv()
    for slot, base, keep in ((1, RO - 8, edge_n), (0, RO + N, edge_s)):
        rows = slice(base, base + 8)
        for h in range(2):
            for l in range(NL):
                ids = rq_row[slot, l, h].astype(jnp.int32)
                lat[l, h, rows, :] = lookup(ids, table[0]) * keep
                ver[l, h, rows, :] = lookup(ids, table[1]) * keep
            snk[h, rows, :] = rq_row[slot, 4, h] * keep
            drn[h, rows, :] = rq_row[slot, 5, h] * keep
    for c in margin_we:
        c.wait_recv()
    for _, c in margin_c.values():
        c.wait_recv()

    def corner_block(dy):
        top, low = (rq_c[margin_c[(-dx, -dy)][0]] for dx in (-1, 1))
        pad = jnp.zeros((SO - 8, LN), F32)
        return jnp.concatenate([pad, top, low, pad], axis=0).T

    blocks = {dy: corner_block(dy) for dy in (-1, 0, 1)}

    def merge(body, corners):
        return jnp.concatenate(
            [
                jnp.where((lane8 >> 3) == SO // 8 - 1, corners, body[:, :LN]),
                body[:, LN : 2 * LN],
                jnp.where((lane8 >> 3) == SO // 8, corners, body[:, 2 * LN :]),
            ],
            axis=1,
        )

    def raw_strip(q, side):
        own, got = slice(8 * q, 8 * q + 8), slice(16 * q, 16 * q + 16)
        if side == 0:
            outside = merge(rq_s[1, own, :], blocks[-1][got, :][0:8, :])
            inside = merge(sq_s[0, own, :], blocks[0][got, :][8:16, :])
            return jnp.concatenate([outside, inside], axis=0)
        outside = merge(rq_s[0, own, :], blocks[1][got, :][8:16, :])
        inside = merge(sq_s[1, own, :], blocks[0][got, :][0:8, :])
        return jnp.concatenate([inside, outside], axis=0)

    sl_lane = iota((16, SL), 1)
    sl_row = iota((16, SL), 0)
    one = jnp.ones((16, SL), F32)
    keep_rows = jnp.where(sl_lane < SO, one * edge_n, jnp.where(sl_lane >= SO + N, one * edge_s, one))
    keep = (
        keep_rows * jnp.where(sl_row < 8, one * edge_w, one),
        keep_rows * jnp.where(sl_row >= 8, one * edge_e, one),
    )
    sides = range(2)
    for g in sides:
        lats, vers = [], []
        for l in range(NL):
            ids = raw_strip(l, g).astype(jnp.int32)
            lats.append(lookup(ids, table[0]) * keep[g])
            vers.append(lookup(ids, table[1]) * keep[g])
        sink_s = raw_strip(4, g) * keep[g]
        sks[g] = sink_s
        drn_s[g] = raw_strip(5, g) * keep[g]
        up = None
        for l in range(NL):
            c = harmonic(lats[l], shift(lats[l], -1, 0))
            r = harmonic(lats[l], shift(lats[l], -1, 1))
            fcs[l, g] = c
            frs[l, g] = r
            d = c + shift(c, 1, 0) + r + shift(r, 1, 1)
            if l > 0:
                d = d + up
            if l < NL - 1:
                up = harmonic(vers[l], vers[l + 1])
                fvs[l, g] = up
                d = d + up
            else:
                d = d + sink_s
            d = jnp.maximum(d, FACE_FLOOR)
            dgs[l, g] = d
            wgs[l, g] = DAMPING / d

    row_z = iota((8, SL), 0)

    def column_form(west, east, ref):
        z = jnp.zeros((8, SL), F32)
        for l in range(NL):
            if west[l] is not None:
                z = jnp.where(row_z == 2 * l + 1, west[l], jnp.where(row_z == 2 * l, east[l], z))
        for k in range(SL // LN):
            block = jnp.concatenate([z[:, k * LN : (k + 1) * LN], jnp.zeros((LN - 8, LN), F32)], axis=0)
            ref[k * LN : (k + 1) * LN, :] = block.T

    def columns(ref, base):
        tile = ref[pl.ds(base + (SO - RO), 8), :]
        return [shift(tile, -(2 * l + 1), 1) for l in range(NL)]

    def edge_terms(v, ref):
        column_form(
            [(fcs[l, 0] * v[l][0])[7:8, :] for l in range(NL)],
            [fcs[l, 1][7:8, :] * v[l][1][8:9, :] for l in range(NL)],
            ref,
        )

    column_form([fcs[l, 0, 7:8, :] for l in range(NL)], [fcs[l, 1, 7:8, :] for l in range(NL)], cf_f)

    def edge_faces(base, sums):
        bf = columns(cf_f, base)
        here = pl.ds(base, 8)
        for l in range(NL):
            fc[l, 1, here, :] = jnp.where(last_lane, bf[l], fc[l, 1, here, :])
            fl[l, 0, here, :] = jnp.where(first_lane, bf[l], fl[l, 0, here, :])
            if sums is not None:
                sums[l] += bf[l]

    for base in (RO - 8, RO + N):
        column_faces(base, None)
        row_faces(base)
        layer_faces(base, None)
        edge_faces(base, None)
    row_faces(RO + N - 8)

    @pl.loop(0, N // 64)
    def _(pair):
        for a in (2 * pair, 2 * pair + 1):
            sums = [zero8] * NL
            for k in range(4):
                edge_faces(pl.multiple_of(RO + 32 * a + 8 * k, 8), sums)
            rows = pl.ds(pl.multiple_of(a * 8, 8), 8)
            for l in range(NL):
                for h, lane in ((0, first_lane), (1, last_lane)):
                    span = slice((2 * l + h) * LN, (2 * l + h + 1) * LN)
                    acc_n[rows, span] = jnp.where(lane, sums[l], acc_n[rows, span])

    block_lane = lane8 & 31
    own_block = (block_lane >= 8) & (block_lane < 16)

    def block_rows(x):
        return x.reshape(8, 8, LN).sum(axis=1)

    def edge_sums(start):
        rows = [fr[l, h, pl.ds(start, 8, stride=32), :] for l in range(NL) for h in range(2)]
        return pick_dot(jnp.concatenate(rows, axis=1), cb[...])

    c_east = edge_sums(RO + 31)
    c_east_prev = edge_sums(RO - 1)
    c_north_wide = block_rows(pick_dot(acc_n[...], cbn[...]))
    c_north = jnp.where(own_block, c_north_wide, 0.0)
    c_north_prev = jnp.where(own_block, shift(c_north_wide, 1, 1), 0.0)
    up_sink = block_rows(pick_dot(acc[...], cb[...]))
    c_up = jnp.where(lane8 < 96, up_sink, 0.0)
    c_sink = jnp.where(lane8 >= 96, up_sink, 0.0)
    c_diag = c_east + c_east_prev + c_north + c_north_prev + c_up + shift(c_up, 32, 1) + c_sink
    tile = zero8
    for q, x in enumerate((c_east, c_north, c_up + c_sink, c_diag)):
        tile = tile + shift(jnp.where(own_block, x, 0.0), 8 * q, 1)
    cm[...] = tile
    cm_in = {d: (k, send(cm, cmr.at[k], d)) for k, d in enumerate(DIRS)}

    sub8 = iota((8, LN), 0)

    def stack(*rows):
        out8 = zero8
        for k, x in enumerate(rows):
            out8 = jnp.where(sub8 == k, x, out8)
        return out8

    def sum_along_gx(it, *tiles):
        s1[it] = stack(*(x.sum(axis=0, keepdims=True) for x in tiles))
        return [send(s1.at[it], ls1.at[it, d - 1], (d, 0)) for d in range(1, nx)]

    def sum_along_gy(it, arriving):
        total = s1[it]
        for d in range(1, nx):
            arriving[d - 1].wait_recv()
            total = total + ls1[it, d - 1]
        s2[it] = total
        return [send(s2.at[it], ls2.at[it, d - 1], (0, d)) for d in range(1, ny)]

    def sum_end(it, arriving, parts):
        total = s2[it]
        for d in range(1, ny):
            arriving[d - 1].wait_recv()
            total = total + ls2[it, d - 1]
        total = total.sum(axis=1, keepdims=True)
        return [total[q : q + 1, :] for q in range(parts)]

    sums_gx = sum_along_gx(0, source_sum, c_diag, c_sink)

    for c in tile_in2:
        c.wait_recv()
    quarter = devices // 4
    lane_q = iota((quarter, LN), 1)
    power = jnp.zeros((quarter, LN), F32)
    ids = power
    for k in range(4):
        part = tin2[k * quarter : (k + 1) * quarter, :]
        mine = (lane_q >> 5) == k
        power = jnp.where(mine, shift(part, 32 * k, 1), power)
        ids = jnp.where(mine, shift(part, 32 * k - 32, 1), ids)
    ids = ids.astype(jnp.int32)
    powers = [part.astype(F32) for part in pieces(power, 3)]
    sub32 = iota((32, LN), 0)
    for k in range(quarter):
        span = slice(k * LN, (k + 1) * LN)
        one_id = ids[k : k + 1, :]
        dense_a[:, span] = jnp.where(sub32 == (one_id >> 5), 1.0, 0.0).astype(BF16)
        hit = sub32 == (one_id & 31)
        for q in range(3):
            dense_b[q, :, span] = jnp.where(hit, powers[q][k : k + 1, :], 0.0).astype(BF16)
    total = None
    for q in range(3):
        term = lax.dot_general(
            dense_a[...], dense_b[q], (((1,), (1,)), ((), ())), preferred_element_type=F32
        )
        total = term if total is None else total + term
    total = jnp.concatenate([total * (1.0 / 64.0), jnp.zeros((32, LN - 32), F32)], axis=1)
    total_t = jnp.concatenate([total, jnp.zeros((LN - 32, LN), F32)], axis=0).T
    ts[...] = stack(total_t[0:1, :], total_t[31:32, :], total[0:1, :], total[31:32, :])
    th_in = {d: (k, send(ts, th.at[k], d)) for k, d in enumerate(DIRS)}
    spread_cols = jnp.where(iota((LN, N), 0) == (iota((LN, N), 1) >> 3), 1.0, 0.0).astype(BF16)
    wide = pick_dot(total, spread_cols)
    for h in range(2):
        dynr[h, 8:40, :] = wide[:, halves[h]]

    def diagonal(base):
        here, above = pl.ds(base, 8), pl.ds(base - 1, 8)
        for l in range(NL):
            for h in range(2):
                d = fr[l, h, above, :] + fr[l, h, here, :] + fl[l, h, here, :] + fc[l, h, here, :]
                if l > 0:
                    d = d + fv[l - 1, h, here, :]
                if l < NL - 1:
                    d = d + fv[l, h, here, :]
                else:
                    d = d + snk[h, here, :]
                d = jnp.maximum(d, FACE_FLOOR)
                dg[l, h, here, :] = d
                wg[l, h, here, :] = DAMPING / d

    diagonal(RO - 8)
    diagonal(RO + N)

    @pl.loop(0, N // 32)
    def _(a):
        for k in range(4):
            diagonal(pl.multiple_of(RO + 32 * a + 8 * k, 8))

    def couple(ref, base, edge, live):
        here, above, below = pl.ds(base, 8), pl.ds(base - 1, 8), pl.ds(base + 1, 8)
        res = [[None, None] for _ in range(NL)]
        mid = [[ref[l, h, here, :] for h in range(2)] for l in range(live)]
        for l in range(live):
            a0, a1 = mid[l]
            f0, f1 = fc[l, 0, here, :], fc[l, 1, here, :]
            ra0, ra1 = shift(a0, -1, 1), shift(a1, -1, 1)
            p0, p1 = shift(f0 * a0, 1, 1), shift(f1 * a1, 1, 1)
            lateral = (
                f0 * jnp.where(last_lane, ra1, ra0) + jnp.where(first_lane, edge[l], p0),
                jnp.where(last_lane, edge[l], f1 * ra1) + jnp.where(first_lane, p0, p1),
            )
            for h in range(2):
                res[l][h] = (
                    lateral[h]
                    + fr[l, h, above, :] * ref[l, h, above, :]
                    + fr[l, h, here, :] * ref[l, h, below, :]
                )
        for l in range(live):
            for h in range(2):
                for face, to in ((l - 1, l - 1), (l, l + 1)):
                    if 0 <= to < NL:
                        term = fv[face, h, here, :] * mid[l][h]
                        res[to][h] = term if res[to][h] is None else res[to][h] + term
        return mid, res

    def strip_couple(v, g, live):
        res = []
        for l in range(live):
            p, r = fcs[l, g] * v[l], frs[l, g]
            res.append(
                fcs[l, g] * shift(v[l], -1, 0) + shift(p, 1, 0) + r * shift(v[l], -1, 1) + shift(r * v[l], 1, 1)
            )
        res += [None] * (NL - live)
        for l in range(live):
            for face, to in ((l - 1, l - 1), (l, l + 1)):
                if 0 <= to < NL:
                    term = fvs[face, g] * v[l]
                    res[to] = term if res[to] is None else res[to] + term
        return res

    def dyn_rows(base, h):
        return dynr[h, pl.ds(base // 8 + 6, 1), :]

    def over_rows(body, margins=True, carry=None):
        if margins:
            body(RO - 8, None, -1, 3)
            body(RO + N, None, 8, 0)

        @pl.loop(0, N // 128)
        def _(pair):
            for a in (4 * pair, 4 * pair + 1, 4 * pair + 2, 4 * pair + 3):
                sums = [zero8] * 8
                for k in range(4):
                    body(pl.multiple_of(RO + 32 * a + 8 * k, 8), sums, a, k)
                rows = pl.ds(pl.multiple_of(a * 8, 8), 8)
                for q in range(8):
                    if sums[q] is not zero8:
                        acc[rows, q * LN : (q + 1) * LN] = sums[q]

    lane16 = iota((16, LN), 1)
    lane24 = iota((24, LN), 1)

    def sweep_neighbours(x):
        lanes = [shift(x, by, 1) for by in (-1, 1, -32, 32)]
        rows = coef[1] * shift(x, -1, 0) + coef[2] * shift(x, 1, 0)
        return rows, (coef[3] * lanes[0] + coef[4] * lanes[1]) + (coef[5] * lanes[2] + coef[6] * lanes[3])

    def coarse_sweeps(right):
        rw = coef[0] * right
        x = rw
        for _ in range(CJ - 1):
            rows, lanes = sweep_neighbours(x)
            x = ((1.0 - DAMPING) * x + rw + rows) + lanes
        return x

    def assemble(own, other):
        rows = []
        for dx in (-1, 0, 1):
            centre = own if dx == 0 else other((dx, 0))
            rows.append(centre + shift(other((dx, -1)), -8, 1) + shift(other((dx, 1)), 8, 1))
        return jnp.concatenate(rows, axis=0)

    def send_coarse(it, own):
        ct[it] = own
        return {d: (k, send(ct.at[it], nb.at[it, k], d)) for k, d in enumerate(DIRS)}

    def first_residual(base, sums, a, k):
        here = pl.ds(base, 8)
        for h in range(2):
            r = dyn_rows(base, h) + drn[h, here, :]
            src[h, here, :] = r
            r_[0, h, here, :] = r
            e1_[0, h, here, :] = wg[0, h, here, :] * r
            if sums is not None:
                sums[h] += r

    over_rows(first_residual, margins=False)
    own_c = block_rows(pick_dot(acc[:, 0 : 2 * LN], cb[0 : 2 * LN, :]))
    side = send_coarse(0, own_c)

    def second_sweep(base, live, edge, first):
        here = pl.ds(base, 8)
        mid, res = couple(e1_, base, edge, live)
        for l in range(NL):
            for h in range(2):
                if l < live:
                    u = (1.0 - DAMPING) * mid[l][h] + wg[l, h, here, :] * (r_[l, h, here, :] + res[l][h])
                elif res[l][h] is not None:
                    u = wg[l, h, here, :] * res[l][h]
                else:
                    u = zero8
                if not first:
                    u = u + t_[l, h, here, :]
                t_[l, h, here, :] = u

    over_rows(lambda base, sums, a, k: second_sweep(base, 1, [zero8], True), margins=False)

    snk_e1 = [wgs[NL - 1, g] * sks[g] for g in sides]
    column_form(
        [None] * (NL - 1) + [(fcs[NL - 1, 0] * snk_e1[0])[7:8, :]],
        [None] * (NL - 1) + [fcs[NL - 1, 1][7:8, :] * snk_e1[1][8:9, :]],
        cf_t,
    )

    def sink_first(base, sums, a, k):
        here = pl.ds(base, 8)
        for h in range(2):
            gs[h, here, :] = wg[NL - 1, h, here, :] * snk[h, here, :]

    over_rows(sink_first)

    def sink_second(base, sums, a, k):
        here, above, below = pl.ds(base, 8), pl.ds(base - 1, 8), pl.ds(base + 1, 8)
        top = NL - 1
        edge = columns(cf_t, base)[top]
        a0, a1 = gs[0, here, :], gs[1, here, :]
        f0, f1 = fc[top, 0, here, :], fc[top, 1, here, :]
        ra0, ra1 = shift(a0, -1, 1), shift(a1, -1, 1)
        p0, p1 = shift(f0 * a0, 1, 1), shift(f1 * a1, 1, 1)
        lateral = (
            f0 * jnp.where(last_lane, ra1, ra0) + jnp.where(first_lane, edge, p0),
            jnp.where(last_lane, edge, f1 * ra1) + jnp.where(first_lane, p0, p1),
        )
        for h, e in ((0, a0), (1, a1)):
            flow = (
                lateral[h]
                + fr[top, h, above, :] * gs[h, above, :]
                + fr[top, h, here, :] * gs[h, below, :]
            )
            gr[1, h, here, :] = (1.0 - DAMPING) * e + wg[top, h, here, :] * (snk[h, here, :] + flow)
            gr[0, h, here, :] = wg[top - 1, h, here, :] * (fv[top - 1, h, here, :] * e)

    over_rows(sink_second, margins=False)
    first_gy = sum_along_gy(0, sums_gx)

    for _, c in cm_in.values():
        c.wait_recv()
    def coupling(q):
        def of(tile):
            return jnp.where((lane8 >> 3) & 3 == (q + 1) % 4, tile, 0.0)

        rows = []
        for dx in (-1, 0, 1):
            tiles = [cm[...] if (dx, dy) == (0, 0) else cmr[cm_in[(-dx, -dy)][0]] for dy in (-1, 0, 1)]
            rows.append(sum(shift(of(tile), 8 * (dy - q), 1) for dy, tile in zip((-1, 0, 1), tiles, strict=True)))
        return jnp.concatenate(rows, axis=0)

    w_east, w_north, w_up, w_diag = (coupling(q) for q in range(4))
    w_sink = jnp.where(lane24 >= 96, w_up, 0.0)
    w_up = jnp.where(lane24 < 96, w_up, 0.0)
    gain = jnp.where((lane24 & 31) < 24, DAMPING / jnp.maximum(w_diag, 1e-30), 0.0)
    coef[0] = gain
    coef[1] = gain * w_east
    coef[2] = gain * shift(w_east, 1, 0)
    coef[3] = gain * w_north
    coef[4] = gain * shift(w_north, 1, 1)
    coef[5] = gain * w_up
    coef[6] = gain * shift(w_up, 32, 1)
    adjoint = coarse_sweeps(w_sink)
    own_adjoint = jnp.where(own_block, adjoint[8:16, :], 0.0)
    sums_gx = sum_along_gx(1, own_adjoint * own_c)

    @pl.loop(0, N // 32)
    def _(a):
        for k in range(4):
            for h in range(2):
                dyn_out[pl.ds(pl.multiple_of(a * 32 + k * 8, 8), 8), halves[h]] = jnp.broadcast_to(
                    dynr[h, pl.ds(8 + 4 * a + k, 1), :], (8, LN)
                )
    for _, c in th_in.values():
        c.wait_recv()

    def rim(d, k):
        return th[th_in[(-d[0], -d[1])][0], k : k + 1, :]

    wide_rims = pick_dot(stack(rim((-1, 0), 3) * edge_n, rim((1, 0), 2) * edge_s), spread_cols)
    for h in range(2):
        dynr[h, 0:8, :] = jnp.broadcast_to(wide_rims[0:1, halves[h]], (8, LN))
        dynr[h, 40:48, :] = jnp.broadcast_to(wide_rims[1:2, halves[h]], (8, LN))
    body = stack(rim((0, -1), 1), ts[0:1, :], ts[1:2, :], rim((0, 1), 0))
    top = stack(rim((-1, -1), 1), rim((-1, 0), 0), rim((-1, 0), 1), rim((-1, 1), 0))
    low = stack(rim((1, -1), 1), rim((1, 0), 0), rim((1, 0), 1), rim((1, 1), 0))
    tall = jnp.where(
        lane8 == 0,
        shift(top, -31, 1),
        jnp.where(lane8 == 33, shift(low, 33, 1), jnp.where(lane8 < 33, shift(body, 1, 1), 0.0)),
    )
    spread_rows = jnp.where(iota((LN, SL), 0) == ((iota((LN, SL), 1) - (SO - 8)) >> 3), 1.0, 0.0).astype(BF16)
    tall = pick_dot(tall, spread_rows)
    for g in sides:
        dyn_s = jnp.where(sl_row < 8, tall[2 * g : 2 * g + 1, :], tall[2 * g + 1 : 2 * g + 2, :]) * keep[g]
        dys[g] = dyn_s
        srs[g] = dyn_s + drn_s[g]
    first_residual(RO - 8, None, -1, 3)
    first_residual(RO + N, None, 8, 0)

    rs = [[srs[g] for g in sides]]
    e1s = [[wgs[0, g] * srs[g] for g in sides]]
    live = 1
    zeros_s = jnp.zeros((16, SL), F32)
    edge_terms(e1s + [[zeros_s, zeros_s]] * (NL - 1), cf_e)
    second_sweep(RO - 8, 1, columns(cf_e, RO - 8), True)
    second_sweep(RO + N, 1, columns(cf_e, RO + N), True)

    def over_edges(base, sums, a, k):
        here = pl.ds(base, 8)
        edge = columns(cf_e, base)[0]
        for h, lane in ((0, first_lane), (1, last_lane)):
            t_[0, h, here, :] = t_[0, h, here, :] + jnp.where(lane, wg[0, h, here, :] * edge, 0.0)

    over_rows(over_edges, margins=False)
    for h in range(2):
        for row, beyond, face in ((RO, RO - 1, RO - 1), (RO + N - 1, RO + N, RO + N - 1)):
            t_[0, h, row : row + 1, :] = t_[0, h, row : row + 1, :] + wg[0, h, row : row + 1, :] * (
                fr[0, h, face : face + 1, :] * e1_[0, h, beyond : beyond + 1, :]
            )

    ts_old = None
    former = diag_total = sink_total = source_total = None
    sweeps = OUTER * INNER
    for it in range(sweeps):
        first, last = it == 0, it == sweeps - 1
        fresh = (it + 1) % INNER == 0

        if not first:
            over_rows(
                lambda base, sums, a, k: second_sweep(base, NL, columns(cf_e, base), False), margins=not last
            )

        if not last:
            us = [[None, None] for _ in range(NL)]
            for g in sides:
                res = strip_couple([e1s[l][g] for l in range(live)], g, live)
                for l in range(NL):
                    if l < live:
                        u = (1.0 - DAMPING) * e1s[l][g] + wgs[l, g] * (rs[l][g] + res[l])
                    elif res[l] is not None:
                        u = wgs[l, g] * res[l]
                    else:
                        u = zeros_s
                    us[l][g] = u if first else ts_old[l][g] + u
            edge_terms(us, cf_t)

            held = 2 if first else NL
            def half_residual(base, sums, a, k):
                here = pl.ds(base, 8)
                mid, res = couple(t_, base, columns(cf_t, base), held)
                for l in range(NL):
                    for h in range(2):
                        r = zero8 if res[l][h] is None else res[l][h]
                        if l < held:
                            r = r - dg[l, h, here, :] * mid[l][h]
                        if l == 0 and not fresh:
                            r = r + src[h, here, :]
                        r_[l, h, here, :] = r
                        if sums is not None:
                            sums[2 * l + h] += r

            over_rows(half_residual)
            if it == 2:
                sums_gy = sum_along_gy(2, sums_gx)
            next_c = block_rows(pick_dot(acc[...], cb[...], 2))

        if last:
            for c in started[: -len(DIRS)]:
                c.wait_send()
        for _, c in side.values():
            c.wait_recv()
        x = coarse_sweeps(assemble(own_c, lambda d: nb[it, side[(-d[0], -d[1])][0]]))
        if it == 1:
            source_total = source_total - sum_end(1, sums_gy, 1)[0] - former * sink_total
            x = x + former * (1.0 - adjoint)
        elif last:
            source_total, less = sum_end(2, sums_gy, 2)
            former = BALANCE_WEIGHT * source_total / diag_total
            source_total = source_total - less - former * sink_total
            x = x + former * (1.0 - adjoint)
        if it % INNER == 1:
            x = x + BALANCE_WEIGHT * source_total / diag_total

        def send_next(total_c):
            moved = (x - sum(sweep_neighbours(x)) * (1.0 / DAMPING))[8:16, :] * c_diag
            own = total_c - jnp.where(own_block, moved, 0.0)
            return own, send_coarse(it + 1, own)

        if not last and not fresh:
            own_c, side = send_next(next_c)

        for l in range(NL):
            for h in range(2):
                at_col = l * 32 + 8 + h * 4
                cv[l, h] = jnp.take_along_axis(x, at_col + (lane24 >> 5), axis=1)
                if not last:
                    cvr[l, h] = jnp.take_along_axis(x, at_col + ((lane24 + 1) >> 5), axis=1)
                    cvl[l, h] = jnp.take_along_axis(x, at_col + ((lane24 - 1) >> 5), axis=1)

        if last:

            @pl.loop(0, N // 32)
            def _(a):
                for l in range(NL):
                    for h in range(2):
                        add = cv[l, h, pl.ds(8 + a, 1), :]
                        for k in range(4):
                            rows = pl.ds(pl.multiple_of(32 * a + 8 * k, 8), 8)
                            here = pl.ds(pl.multiple_of(RO + 32 * a + 8 * k, 8), 8)
                            u = t_[l, h, here, :] + add
                            if l >= NL - 2:
                                u = u - former * gr[l - (NL - 2), h, here, :]
                            out[l, rows, halves[h]] = u

            break

        if fresh:

            def new_source(base, sums, a, k):
                here = pl.ds(base, 8)
                for h in range(2):
                    u = t_[0, h, here, :] + cv[0, h, pl.ds(8 + a, 1), :]
                    s = dyn_rows(base, h) + drn[h, here, :] * jnp.exp(DRAIN_SLOPE * u)
                    src[h, here, :] = s
                    if sums is not None:
                        sums[h] += s

            over_rows(new_source)
            next_c = next_c + block_rows(pick_dot(acc[:, 0 : 2 * LN], cb[0 : 2 * LN, :]))
            own_c, side = send_next(next_c)
        if first:
            sums_gy = sum_along_gy(1, sums_gx)

        def whole_residual(base, sums, a, k):
            here, above = pl.ds(base, 8), pl.ds(base - 1, 8)
            block = pl.ds(8 + a, 1)
            xs = [[cv[l, h, block, :] for h in range(2)] for l in range(NL)]
            for h in range(2):
                flow = None
                for l in range(NL):
                    v = xs[l][h]
                    t_[l, h, here, :] = t_[l, h, here, :] + v
                    r = r_[l, h, here, :]
                    if l == 0 and fresh:
                        r = r + src[h, here, :]
                    r = r - fc[l, h, here, :] * (v - cvr[l, h, block, :])
                    r = r - fl[l, h, here, :] * (v - cvl[l, h, block, :])
                    if k == 0:
                        step = v - cv[l, h, pl.ds(7 + a, 1), :]
                        r = r - jnp.where(sub8 == 0, fr[l, h, above, :] * step, 0.0)
                    if k == 3:
                        step = v - cv[l, h, pl.ds(9 + a, 1), :]
                        r = r - jnp.where(sub8 == 7, fr[l, h, here, :] * step, 0.0)
                    if l > 0:
                        r = r + flow
                    if l < NL - 1:
                        flow = fv[l, h, here, :] * (v - xs[l + 1][h])
                        r = r - flow
                    else:
                        r = r - snk[h, here, :] * v
                    r_[l, h, here, :] = r
                    e1_[l, h, here, :] = wg[l, h, here, :] * r
                    if it == 1 and l >= NL - 2 and sums is not None:
                        sums[0] += gr[l - (NL - 2), h, here, :] * r

        over_rows(whole_residual)
        if it == 1:
            response = acc[0:8, 0:LN]
            for a in range(1, 8):
                response = response + acc[8 * a : 8 * a + 8, 0:LN]
            sums_gx = sum_along_gx(2, own_c, response + own_adjoint * own_c)

        xt[...] = jnp.concatenate([x, jnp.zeros((LN - 24, LN), F32)], axis=0).T
        picked = jnp.concatenate(
            [xt[l * 32 + c : l * 32 + c + 1, :] for l in range(NL) for c in (7, 8, 15, 16)], axis=0
        )
        picked = jnp.concatenate(
            [jnp.take_along_axis(picked, 6 + 4 * k + (lane16 >> 5), axis=1) for k in range(SL // LN)], axis=1
        )
        live = NL
        ts_old = [[None, None] for _ in range(NL)]
        rs = [[None, None] for _ in range(NL)]
        e1s = [[None, None] for _ in range(NL)]
        for g in sides:
            for l in range(NL):
                k = 4 * l + 2 * g
                ts_old[l][g] = us[l][g] + jnp.where(sl_row < 8, picked[k : k + 1, :], picked[k + 1 : k + 2, :])
            if fresh:
                srs[g] = dys[g] + drn_s[g] * jnp.exp(DRAIN_SLOPE * ts_old[0][g])
            res = strip_couple([ts_old[l][g] for l in range(NL)], g, NL)
            for l in range(NL):
                r = res[l] - dgs[l, g] * ts_old[l][g]
                if l == 0:
                    r = r + srs[g]
                rs[l][g] = r
                e1s[l][g] = wgs[l, g] * r
        if first:
            source_total, diag_total, sink_total = sum_end(0, first_gy, 3)
            former = BALANCE_WEIGHT * source_total / diag_total

            def sink_part(base, sums, a, k):
                here = pl.ds(base, 8)
                for h in range(2):
                    r = r_[NL - 1, h, here, :] - former * snk[h, here, :]
                    r_[NL - 1, h, here, :] = r
                    e1_[NL - 1, h, here, :] = wg[NL - 1, h, here, :] * r

            over_rows(sink_part)
            for g in sides:
                rs[NL - 1][g] = rs[NL - 1][g] - former * sks[g]
                e1s[NL - 1][g] = wgs[NL - 1, g] * rs[NL - 1][g]
        edge_terms(e1s, cf_e)

    for c in started[-len(DIRS) :]:
        c.wait_send()


def hand_over(a, b, to_a, to_b, sem):
    copies = [
        pltpu.make_async_copy(a.at[l], to_a.at[l], sem.at[l]) for l in range(NL)
    ] + [pltpu.make_async_copy(b, to_b, sem.at[NL])]
    for c in copies:
        c.start()
    for c in copies:
        c.wait()


def n_copies(nx, ny):
    setup = (ny - 1) + 2 + 6 + 2 + (nx - 1) + 8 + 8
    return setup + OUTER * INNER * 8 + 3 * (nx - 1 + ny - 1)


def solution(mesh):
    nx, ny = mesh.shape["gx"], mesh.shape["gy"]
    its = OUTER * INNER
    devices = nx * ny

    def step(material, material_table, sink_cond, drain_current, instance_tile, instance_power):
        n_inst = instance_tile.shape[0]
        field = pltpu.VMEM((NL, 2, NR, LN), F32)
        single = pltpu.VMEM((2, NR, LN), F32)
        vm = lambda *shape: pltpu.VMEM(shape, F32)
        half = lambda *shape: pltpu.VMEM(shape, BF16)
        copies = n_copies(nx, ny)
        scratch = [
            pltpu.VMEM((NL, N, N), jnp.int32), vm(N, N), vm(N, N),
            pltpu.SMEM((2, 16), F32), pltpu.VMEM((n_inst // LN, LN), jnp.int32), vm(n_inst // LN, LN),
            field, field, field, field, field, pltpu.VMEM((NL - 1, 2, NR, LN), F32), field, field,
            single, single, single, field, field, field,
            vm(SL, LN), vm(SL, LN), vm(SL, LN), vm(64, 8 * LN), vm(64, 8 * LN), vm(SL, LN),
            half(8 * LN, LN), half(8 * LN, LN),
            half(devices, n_inst), half(3, 64, n_inst), vm(devices, LN), vm(devices, LN),
            vm(nx, ny, LN), vm(devices, LN), half(32, 32 * devices), half(3, 32, 32 * devices),
            vm(8, LN), vm(8, 8, LN), vm(2, 48, LN),
            vm(2, NQ, 2, 8, LN), vm(2, NQ, 2, 8, LN), vm(2, 8, LN), vm(6, 8, LN),
            vm(2, 8 * NQ, SL), vm(2, 8 * NQ, SL),
            vm(NL, 2, 16, SL), vm(NL, 2, 16, SL), vm(NL - 1, 2, 16, SL), vm(NL, 2, 16, SL), vm(NL, 2, 16, SL),
            vm(2, 16, SL), vm(2, 16, SL), vm(2, 16, SL), vm(2, 16, SL), single, pltpu.VMEM((2, 2, NR, LN), F32),
            vm(8, LN), vm(8, 8, LN), vm(7, 24, LN), vm(its, 8, LN), vm(its, 8, 8, LN),
            vm(3, 8, LN), vm(3, nx - 1, 8, LN), vm(3, 8, LN), vm(3, ny - 1, 8, LN),
            vm(NL, 2, 24, LN), vm(NL, 2, 24, LN), vm(NL, 2, 24, LN), vm(LN, LN),
            pltpu.SemaphoreType.DMA((copies,)), pltpu.SemaphoreType.DMA((copies,)), pltpu.SemaphoreType.DMA((6,)),
        ]
        vmem = pl.BlockSpec(memory_space=pltpu.VMEM)
        hbm = pl.BlockSpec(memory_space=pltpu.HBM)
        shapes = (jax.ShapeDtypeStruct((NL, N, N), F32), jax.ShapeDtypeStruct((N, N), F32))
        inside = (vm(NL, N, N), vm(N, N))
        results = pl.pallas_call(
            functools.partial(kernel, nx, ny),
            out_shape=inside,
            in_specs=[hbm] * 6,
            out_specs=(vmem, vmem),
            scratch_shapes=scratch,
            compiler_params=pltpu.CompilerParams(
                collective_id=0, has_side_effects=True, vmem_limit_bytes=56 * 1024 * 1024
            ),
        )(
            material,
            material_table,
            sink_cond,
            drain_current,
            instance_tile.reshape(n_inst // LN, LN),
            instance_power.reshape(n_inst // LN, LN),
        )
        return pl.pallas_call(
            hand_over,
            out_shape=shapes,
            in_specs=[pl.BlockSpec(memory_space=pl.ANY)] * 2,
            out_specs=(hbm, hbm),
            compiler_params=pltpu.CompilerParams(vmem_limit_bytes=1024 * 1024),
            scratch_shapes=[pltpu.SemaphoreType.DMA((NL + 1,))],
        )(*results)

    return jax.shard_map(
        step,
        mesh=mesh,
        in_specs=(
            P(None, "gx", "gy"),
            P(),
            P("gx", "gy"),
            P("gx", "gy"),
            P(("gx", "gy")),
            P(("gx", "gy")),
        ),
        out_specs=(P(None, "gx", "gy"), P("gx", "gy")),
        check_vma=False,
    )
```
